32 devices in a mesh: wide: 16 (over z, y, core), narrow: 2 (over x).
Axes of the slice: x: 2, y: 2, z: 4, core: 2. Of those that a mesh axis runs over, the one named last changes fastest.
Arguments:
- tokens: bfloat16 [2, 8192, 768], P(None, 'wide'), may hold values from -6 to 6
- segments: int32 [2, 8192], P(None, 'wide'), may hold values from -1 to 7, as said below
- query_weight: bfloat16 [768, 768], P(None, 'narrow'), may hold values from -0.21875 to 0.21875
- key_weight: bfloat16 [768, 768], P(None, 'narrow'), may hold values from -0.21875 to 0.21875
- value_weight: bfloat16 [768, 768], P(None, 'narrow'), may hold values from -0.21875 to 0.21875
- output_weight: bfloat16 [768, 768], P('narrow'), may hold values from -0.875 to 0.875
- expand_weight: bfloat16 [768, 3072], P(None, 'narrow'), may hold values from -0.21875 to 0.21875
- reduce_weight: bfloat16 [3072, 768], P('narrow'), may hold values from -0.109375 to 0.109375
- heads_bias: float32 [3, 768], P(None, 'narrow'), may hold values from -1.8 to 1.8
- model_bias: float32 [6, 768], replicated, may hold values from -1.8 to 1.8
- hidden_bias: float32 [3072], P('narrow'), may hold values from -1.8 to 1.8
- mentor_query: bfloat16 [768, 768], P(None, 'narrow'), may hold values from -0.21875 to 0.21875
- mentor_key: bfloat16 [768, 768], P(None, 'narrow'), may hold values from -0.21875 to 0.21875
- mentor_value: bfloat16 [768, 768], P(None, 'narrow'), may hold values from -0.21875 to 0.21875
- mentor_output: bfloat16 [768, 768], P('narrow'), may hold values from -0.875 to 0.875
- mentor_expand: bfloat16 [768, 3072], P(None, 'narrow'), may hold values from -0.21875 to 0.21875
- mentor_reduce: bfloat16 [3072, 768], P('narrow'), may hold values from -0.109375 to 0.109375
- mentor_heads: float32 [3, 768], P(None, 'narrow'), may hold values from -1.8 to 1.8
- mentor_model: float32 [6, 768], replicated, may hold values from -1.8 to 1.8
- mentor_hidden: float32 [3072], P('narrow'), may hold values from -1.8 to 1.8
Outputs:
- student_out: bfloat16 [2, 8192, 768], P(None, 'wide')
- grad_tokens: float32 [2, 8192, 768], P(None, 'wide')
- grad_query: float32 [768, 768], P(None, 'narrow')
- grad_key: float32 [768, 768], P(None, 'narrow')
- grad_value: float32 [768, 768], P(None, 'narrow')
- grad_output: float32 [768, 768], P('narrow')
- grad_expand: float32 [768, 3072], P(None, 'narrow')
- grad_reduce: float32 [3072, 768], P('narrow')
- grad_heads: float32 [3, 768], P(None, 'narrow')
- grad_model: float32 [6, 768], replicated
- grad_hidden: float32 [3072], P('narrow')
The draws below stay inside these ranges and needn't reach their ends.
Inputs may be any that keep to these rules, and one draw needn't show every extreme that they name: `segments`: within each device's 512 slots of a micro-batch, slots come in regions of 256; a live region holds examples of one length (64, 128 or 256) numbered 4 * region + place in order; padding regions (-1) follow the live ones and each device's first region is live; in every draw some device's slots hold no padding.
All inputs are finite; a program needn't handle non-finite values.
Results may differ from the reference program's by a relative error of at most 0.0078.
Values sent between devices are 32-bit elements; how exact they have to be, the bound alone decides.
No kernel may reach another device: no remote copies, remote signals or barrier semaphores. Data moves between devices by JAX's collectives and lax.ppermute only.
A program may use at most 192 MiB of HBM per device.

```python
import jax
import jax.numpy as jnp
from jax import lax

D = 768
HEADS = 12
HEAD = 64
FF = 3072
UNIT = 64
MB = 2
SLOTS = 512
TOK = 8192
N_WIDE = 16


def draw_segments(key, part):
    regions = SLOTS // (4 * UNIT)
    packs = MB * N_WIDE
    bucket_key = jax.random.fold_in(key, 101)
    count_key = jax.random.fold_in(key, 202)
    buckets = jax.random.randint(bucket_key, (packs, regions), 0, 3)
    buckets = buckets.at[0, 0].set(2)
    buckets = buckets.at[0, regions - 1].set(0)
    counts = jax.random.randint(count_key, (packs,), 1, regions + 1)
    counts = counts.at[0].set(regions)
    counts = counts.at[1].set(1)
    lengths = jnp.where(buckets == 0, UNIT, jnp.where(buckets == 1, 2 * UNIT, 4 * UNIT))
    places = jnp.arange(4 * UNIT, dtype=jnp.int32)
    region_ids = jnp.arange(regions, dtype=jnp.int32)
    labels = region_ids[None, :, None] * 4 + places[None, None, :] // lengths[:, :, None]
    live = region_ids[None, :, None] < counts[:, None, None]
    labels = jnp.where(live, labels, -1)
    return labels.reshape(MB, N_WIDE * SLOTS).astype(jnp.int32)


def block_scale(rng, extent, split, low, largest):
    def one(position, parts):
        steps = jax.random.uniform(jax.random.fold_in(jax.random.fold_in(rng, 6), position), (parts,), jnp.float32, low / len(split), largest / len(split))
        return jnp.repeat(jnp.exp(steps), extent[position] // parts).reshape((-1,) + (1,) * (len(extent) - position - 1))

    level = one(*split[0])
    for cut in split[1:]:
        level = level * one(*cut)
    return level


def gaussian(key, dims, scale, reach, pieces=(), held_as=jnp.bfloat16):
    loudness = block_scale(key, dims, pieces, -0.22, 0.18) if pieces else 1.0
    result = jax.random.normal(key, dims, jnp.float32) * scale * loudness
    return jnp.minimum(jnp.maximum(result, -reach), reach).astype(held_as)


def setup_inputs(seed: int = 0) -> dict:
    arg_keys = jax.random.split(jax.random.key(seed), 21)
    return {
        "tokens": gaussian(arg_keys[0], (MB, TOK, D), 1.0, 6.0, ((1, 16),)),
        "segments": draw_segments(jax.random.fold_in(arg_keys[20], 71), 0),
        "query_weight": gaussian(arg_keys[2], (D, D), D ** -0.5, 0.21875, ((1, 2),)),
        "key_weight": gaussian(arg_keys[3], (D, D), D ** -0.5, 0.21875, ((1, 2),)),
        "value_weight": gaussian(arg_keys[4], (D, D), D ** -0.5, 0.21875, ((1, 2),)),
        "output_weight": gaussian(arg_keys[5], (D, D), (D // 16) ** -0.5, 0.875, ((0, 2),)),
        "expand_weight": gaussian(arg_keys[6], (D, FF), D ** -0.5, 0.21875, ((1, 2),)),
        "reduce_weight": gaussian(arg_keys[7], (FF, D), FF ** -0.5, 0.109375, ((0, 2),)),
        "heads_bias": gaussian(arg_keys[8], (3, D), 0.3, 1.8, ((1, 2),), jnp.float32),
        "model_bias": gaussian(arg_keys[9], (6, D), 0.3, 1.8, (), jnp.float32),
        "hidden_bias": gaussian(arg_keys[10], (FF,), 0.3, 1.8, ((0, 2),), jnp.float32),
        "mentor_query": gaussian(arg_keys[11], (D, D), D ** -0.5, 0.21875, ((1, 2),)),
        "mentor_key": gaussian(arg_keys[12], (D, D), D ** -0.5, 0.21875, ((1, 2),)),
        "mentor_value": gaussian(arg_keys[13], (D, D), D ** -0.5, 0.21875, ((1, 2),)),
        "mentor_output": gaussian(arg_keys[14], (D, D), (D // 16) ** -0.5, 0.875, ((0, 2),)),
        "mentor_expand": gaussian(arg_keys[15], (D, FF), D ** -0.5, 0.21875, ((1, 2),)),
        "mentor_reduce": gaussian(arg_keys[16], (FF, D), FF ** -0.5, 0.109375, ((0, 2),)),
        "mentor_heads": gaussian(arg_keys[17], (3, D), 0.3, 1.8, ((1, 2),), jnp.float32),
        "mentor_model": gaussian(arg_keys[18], (6, D), 0.3, 1.8, (), jnp.float32),
        "mentor_hidden": gaussian(arg_keys[19], (FF,), 0.3, 1.8, ((0, 2),), jnp.float32),
    }


@jax.custom_vjp
def low(v):
    return lax.optimization_barrier(v.astype(jnp.bfloat16)).astype(jnp.float32)

@jax.custom_vjp
def low_back(v):
    return v

def low_keep(v):
    return (low(v), None)

def low_pass(kept, grad):
    return (grad,)

def back_keep(v):
    return (v, None)

def back_low(kept, grad):
    return (low(grad),)
low.defvjp(low_keep, low_pass)
low_back.defvjp(back_keep, back_low)
norm_eps = 1e-06
score_weight = 0.05
big_negative = -1e+30

def project(left, right):
    return jnp.dot(left, right, precision=lax.Precision.HIGHEST)

def split_heads(values):
    return values.reshape(values.shape[0], HEADS, HEAD)

def layer_norm(values, gain, shift):
    centred = values - lax.optimization_barrier(jnp.mean(values, axis=-1, keepdims=True))
    spread = lax.optimization_barrier(jnp.mean(centred * centred, axis=-1, keepdims=True))
    return centred * lax.rsqrt(spread + norm_eps) * (1.0 + gain) + shift

def binarize(weight, axis):
    alpha = lax.optimization_barrier(jnp.mean(jnp.abs(weight), axis=axis, keepdims=True))
    return (alpha * jnp.sign(weight)).astype(jnp.bfloat16).astype(jnp.float32)

def layer(inputs, segment, params):
    query_w, key_w, value_w, output_w, expand_w, reduce_w, heads_b, model_b, hidden_b = params
    rows = inputs.shape[0]
    same_doc = segment[:, None] == segment[None, :]
    live_row = segment >= 0
    diagonal = jnp.arange(rows)[:, None] == jnp.arange(rows)[None, :]
    allowed = same_doc & (live_row[:, None] | diagonal)
    query = low(low_back(project(inputs, query_w) + heads_b[0]))
    keys = low(low_back(project(inputs, key_w) + heads_b[1]))
    values = low(low_back(project(inputs, value_w) + heads_b[2]))
    scores = low_back(jnp.einsum('qhd,khd->hqk', split_heads(query), split_heads(keys), precision=lax.Precision.HIGHEST) * HEAD ** (-0.5))
    probs = low(jax.nn.softmax(jnp.where(allowed, scores, big_negative), axis=-1))
    mixed = low(low_back(jnp.einsum('hqk,khd->qhd', probs, split_heads(values), precision=lax.Precision.HIGHEST).reshape(rows, D)))
    attended = low_back(project(mixed, output_w) + model_b[0])
    first = layer_norm(inputs + attended, model_b[2], model_b[3])
    upward = low_back(project(low(first), expand_w) + hidden_b)
    active = low(jax.nn.gelu(upward, approximate=False))
    downward = low_back(project(active, reduce_w) + model_b[1])
    return (layer_norm(first + downward, model_b[4], model_b[5]), scores)

def reference(tokens, segments, query_weight, key_weight, value_weight, output_weight, expand_weight, reduce_weight, heads_bias, model_bias, hidden_bias, mentor_query, mentor_key, mentor_value, mentor_output, mentor_expand, mentor_reduce, mentor_heads, mentor_model, mentor_hidden):
    wide_f = jnp.float32
    student = (binarize(query_weight.astype(wide_f), 0), binarize(key_weight.astype(wide_f), 0), binarize(value_weight.astype(wide_f), 0), binarize(output_weight.astype(wide_f), 1), binarize(expand_weight.astype(wide_f), 0), binarize(reduce_weight.astype(wide_f), 1), heads_bias.astype(wide_f), model_bias.astype(wide_f), hidden_bias.astype(wide_f))
    teacher = (mentor_query.astype(wide_f), mentor_key.astype(wide_f), mentor_value.astype(wide_f), mentor_output.astype(wide_f), mentor_expand.astype(wide_f), mentor_reduce.astype(wide_f), mentor_heads.astype(wide_f), mentor_model.astype(wide_f), mentor_hidden.astype(wide_f))
    packs = MB * N_WIDE
    inputs = tokens.astype(wide_f).reshape(packs, SLOTS, D)
    fixed_inputs = tokens.astype(wide_f).reshape(packs, SLOTS, D)
    labels = segments.reshape(packs, SLOTS)

    def total(moving, params):

        def one(item):
            pack_in, pack_fixed, pack_seg = item
            out_s, scores_s = layer(pack_in, pack_seg, params)
            out_t, scores_t = layer(pack_fixed, pack_seg, teacher)
            live_row = pack_seg >= 0
            pairs = ((pack_seg[:, None] == pack_seg[None, :]) & live_row[:, None]).astype(jnp.float32)
            gap = out_s - out_t
            hidden_term = jnp.sum(jnp.where(live_row[:, None], gap * gap, 0.0))
            score_gap = scores_s - scores_t
            score_term = jnp.sum(pairs[None, :, :] * score_gap * score_gap)
            return (0.5 * hidden_term + 0.5 * score_weight * score_term, out_s)
        losses, outs = lax.map(jax.checkpoint(one), (moving, fixed_inputs, labels))
        return (jnp.sum(losses), outs)
    loss, back_fn, outs = jax.vjp(total, inputs, student, has_aux=True)
    d_inputs, d_student = back_fn(jnp.ones((), jnp.float32))
    student_out = outs.reshape(MB, N_WIDE * SLOTS, D).astype(jnp.bfloat16)
    grad_tokens = d_inputs.reshape(MB, N_WIDE * SLOTS, D)
    return (student_out, grad_tokens, d_student[0], d_student[1], d_student[2], d_student[3], d_student[4], d_student[5], d_student[6], d_student[7], d_student[8])
```

```python
import functools

import jax
import jax.numpy as jnp
from jax import lax
from jax.experimental import pallas as pl
from jax.experimental.pallas import tpu as pltpu
from jax.sharding import PartitionSpec as P

HEAD = 64
REGION = 256

norm_eps = 1e-06
score_weight = 0.05
big_negative = -1e30
f32 = jnp.float32
bf16 = jnp.bfloat16


def dot_nn(left, right):
    return jnp.dot(left, right, preferred_element_type=f32)


def dot_tn(left, right):
    return lax.dot_general(left, right, (((0,), (0,)), ((), ())), preferred_element_type=f32)


def dot_nt(left, right):
    return lax.dot_general(left, right, (((1,), (1,)), ((), ())), preferred_element_type=f32)


def layer_norm(values, gain, shift):
    centred = values - jnp.mean(values, axis=-1, keepdims=True)
    spread = jnp.mean(centred * centred, axis=-1, keepdims=True)
    return centred * lax.rsqrt(spread + norm_eps) * (1.0 + gain) + shift


def binarize(weight, axis):
    widened = weight.astype(f32)
    alpha = jnp.mean(jnp.abs(widened), axis=axis, keepdims=True)
    return (alpha * jnp.sign(widened)).astype(bf16)


def half_masks():
    lane = lax.broadcasted_iota(jnp.int32, (1, 2 * HEAD), 1)
    low = jnp.where(lane < HEAD, 1.0, 0.0).astype(bf16)
    return (low, (1.0 - low.astype(f32)).astype(bf16))


def region_masks(row_ref, col_ref):
    across = row_ref[0]
    down = col_ref[...]
    same = down == across
    live = down >= 0
    size = down.shape[0]
    diagonal = lax.broadcasted_iota(jnp.int32, (size, size), 0) == lax.broadcasted_iota(
        jnp.int32, (size, size), 1
    )
    pairs = same & live
    return pairs, pairs | diagonal


def probabilities(scores, allowed):
    masked = jnp.where(allowed, scores, big_negative)
    top = jnp.max(masked, axis=-1, keepdims=True)
    expo = jnp.exp(masked - top)
    total = jnp.sum(expo, axis=-1, keepdims=True)
    return expo * (1.0 / total)


def attend_kernel(width, qkv_ref, row_ref, col_ref, out_ref):
    pairs, allowed = region_masks(row_ref, col_ref)
    masks = half_masks()
    scale = HEAD ** (-0.5)
    for net in range(2):
        base = net * 3 * width
        for at in range(0, width, 2 * HEAD):
            query = qkv_ref[:, base + at : base + at + 2 * HEAD]
            keys = qkv_ref[:, base + width + at : base + width + at + 2 * HEAD]
            values = qkv_ref[:, base + 2 * width + at : base + 2 * width + at + 2 * HEAD]
            probs = [
                probabilities(dot_nt(query * mask, keys) * scale, allowed).astype(bf16)
                for mask in masks
            ]
            stacked = jnp.concatenate([values * mask for mask in masks], axis=0)
            mixed = dot_nn(jnp.concatenate(probs, axis=1), stacked)
            out_ref[:, net * width + at : net * width + at + 2 * HEAD] = mixed.astype(bf16)


def attend(qkv, seg_row, seg_col):
    rows, columns = qkv.shape
    width = columns // 6
    regions = rows // REGION
    return pl.pallas_call(
        functools.partial(attend_kernel, width),
        grid=(regions,),
        in_specs=[
            pl.BlockSpec((REGION, columns), lambda i: (i, 0)),
            pl.BlockSpec((1, 1, REGION), lambda i: (i, 0, 0)),
            pl.BlockSpec((REGION, 1), lambda i: (i, 0)),
        ],
        out_specs=pl.BlockSpec((REGION, 2 * width), lambda i: (i, 0)),
        out_shape=jax.ShapeDtypeStruct((rows, 2 * width), bf16),
        compiler_params=pltpu.CompilerParams(vmem_limit_bytes=32 * 2**20),
        cost_estimate=pl.CostEstimate(
            flops=8 * rows * REGION * width, bytes_accessed=8 * rows * columns, transcendentals=0
        ),
        name="attend",
    )(qkv, seg_row, seg_col)


def attend_back_kernel(width, own_ref, oth_ref, grad_ref, row_ref, col_ref, out_ref):
    pairs, allowed = region_masks(row_ref, col_ref)
    weight = jnp.where(pairs, score_weight, 0.0)
    masks = half_masks()
    scale = HEAD ** (-0.5)
    step = 2 * HEAD
    for part, qkv_ref in enumerate((own_ref, oth_ref)):
        for at in range(0, width, step):
            query, keys, values, query_t, keys_t = (
                qkv_ref[:, k * width + at : k * width + at + step] for k in range(5)
            )
            grad = grad_ref[:, part * width + at : part * width + at + step]
            probs = []
            slopes = []
            for mask in masks:
                scores = dot_nt(query * mask, keys) * scale
                prob = probabilities(scores, allowed)
                gap = scores - dot_nt(query_t * mask, keys_t) * scale
                d_prob = dot_nt(grad * mask, values)
                mean = jnp.sum(prob * d_prob, axis=-1, keepdims=True)
                slope = prob * (d_prob - mean) + weight * gap
                probs.append(prob.astype(bf16))
                slopes.append(slope.astype(bf16))

            def both(array):
                return jnp.concatenate([array * mask for mask in masks], axis=0)

            d_query = dot_nn(jnp.concatenate(slopes, axis=1), both(keys)) * scale
            d_keys = dot_tn(jnp.concatenate(slopes, axis=0), both(query)) * scale
            d_values = dot_tn(jnp.concatenate(probs, axis=0), both(grad))
            for k, result in enumerate((d_query, d_keys, d_values)):
                start = part * 3 * width + k * width + at
                out_ref[:, start : start + step] = result.astype(bf16)


def attend_back(qkv_own, qkv_oth, grad, seg_row, seg_col):
    rows, columns = qkv_own.shape
    width = columns // 6
    regions = rows // REGION
    return pl.pallas_call(
        functools.partial(attend_back_kernel, width),
        grid=(regions,),
        in_specs=[
            pl.BlockSpec((REGION, columns), lambda i: (i, 0)),
            pl.BlockSpec((REGION, columns), lambda i: (i, 0)),
            pl.BlockSpec((REGION, 2 * width), lambda i: (i, 0)),
            pl.BlockSpec((1, 1, REGION), lambda i: (i, 0, 0)),
            pl.BlockSpec((REGION, 1), lambda i: (i, 0)),
        ],
        out_specs=pl.BlockSpec((REGION, 6 * width), lambda i: (i, 0)),
        out_shape=jax.ShapeDtypeStruct((rows, 6 * width), bf16),
        compiler_params=pltpu.CompilerParams(vmem_limit_bytes=48 * 2**20),
        cost_estimate=pl.CostEstimate(
            flops=28 * rows * REGION * width, bytes_accessed=16 * rows * columns, transcendentals=0
        ),
        name="attend_back",
    )(qkv_own, qkv_oth, grad, seg_row, seg_col)


def assemble_kernel(count, where_ref, *refs):
    out_ref = refs[-1]
    step = pl.program_id(0)
    for k, ref in enumerate(refs[:-1]):

        @pl.when(step // count == k)
        def _(ref=ref):
            out_ref[...] = ref[...].astype(out_ref.dtype)


def assemble(pieces, where, count, dtype=bf16):
    rows = pieces[0].shape[0] // count
    columns = pieces[0].shape[1]
    total = count * len(pieces)
    specs = [
        pl.BlockSpec((rows, columns), lambda i, w, k=k: (jnp.clip(i - count * k, 0, count - 1), 0))
        for k in range(len(pieces))
    ]
    return pl.pallas_call(
        functools.partial(assemble_kernel, count),
        grid_spec=pltpu.PrefetchScalarGridSpec(
            num_scalar_prefetch=1,
            grid=(total,),
            in_specs=specs,
            out_specs=pl.BlockSpec((rows, columns), lambda i, w: (jnp.bitwise_xor(i, w[0]), 0)),
        ),
        out_shape=jax.ShapeDtypeStruct((total * rows, columns), dtype),
        compiler_params=pltpu.CompilerParams(vmem_limit_bytes=40 * 2**20),
        cost_estimate=pl.CostEstimate(
            flops=0, bytes_accessed=6 * total * rows * columns, transcendentals=0
        ),
        name="assemble",
    )(where.reshape(1).astype(jnp.int32), *pieces)


def on_device(
    n_wide,
    tokens,
    segments,
    query_weight,
    key_weight,
    value_weight,
    output_weight,
    expand_weight,
    reduce_weight,
    heads_bias,
    model_s,
    hidden_bias,
    mentor_query,
    mentor_key,
    mentor_value,
    mentor_output,
    mentor_expand,
    mentor_reduce,
    mentor_heads,
    model_t,
    mentor_hidden,
):
    n_bits = n_wide.bit_length() - 1
    side = lax.axis_index("narrow")
    place = lax.axis_index("wide")
    bits = [(place >> b) & 1 for b in range(n_bits)]

    def swap(array, bit):
        if bit == "x":
            return lax.ppermute(array, "narrow", [(0, 1), (1, 0)])
        return lax.ppermute(array, "wide", [(i, i ^ (1 << bit)) for i in range(n_wide)])

    w_qkv = jnp.concatenate(
        [
            binarize(query_weight, 0),
            binarize(key_weight, 0),
            binarize(value_weight, 0),
            mentor_query,
            mentor_key,
            mentor_value,
        ],
        axis=1,
    )
    w_out = jnp.concatenate([binarize(output_weight, 1), mentor_output], axis=1)
    w_up = jnp.concatenate([binarize(expand_weight, 0), mentor_expand], axis=1)
    w_down = jnp.concatenate([binarize(reduce_weight, 1), mentor_reduce], axis=1)
    width = query_weight.shape[1]
    hidden = expand_weight.shape[1]
    dim = query_weight.shape[0]

    biases = jnp.concatenate(
        [heads_bias.reshape(-1), mentor_heads.reshape(-1), hidden_bias, mentor_hidden]
    )
    biases_oth = swap(biases.reshape(-1, 128), "x").reshape(-1)

    def fetch(weight, first, second):
        rows = weight.shape[0] // 8
        index = bits[0] * 4 + bits[second] * 2 + bits[first]
        piece = lax.dynamic_slice_in_dim(weight, index * rows, rows, 0).astype(f32)
        piece = lax.optimization_barrier(piece)
        zero = swap(piece, "x")
        pair = jnp.concatenate([zero, swap(zero, first)], axis=0)
        pair_b = swap(pair, second)
        return assemble([pair, pair_b, swap(pair, 0), swap(pair_b, 0)], index, 2)

    def fetch_direct(weight):
        rows = weight.shape[0] // 2
        piece = lax.dynamic_slice_in_dim(weight, bits[0] * rows, rows, 0).astype(f32)
        piece = lax.optimization_barrier(piece)
        mine = swap(piece, "x")
        return assemble([mine, swap(mine, 0)], bits[0] * 2 , 2)

    v_qkv = fetch(w_qkv, 1, 2)
    v_out = fetch(w_out, 2, 1)
    v_up = fetch(w_up, 1, 2)
    cut = w_down.shape[0] * 2 // 3
    v_down_a = fetch(w_down[:cut], 2, 1)
    v_down_b = fetch_direct(w_down[cut:])

    x = lax.dynamic_index_in_dim(tokens, side, 0, keepdims=False)
    segment = lax.dynamic_index_in_dim(segments, side, 0, keepdims=False)
    rows = x.shape[0]
    live = (segment >= 0)[:, None]
    seg_row = segment.reshape(rows // REGION, 1, REGION)
    seg_col = segment.reshape(rows, 1)
    resident = x.astype(f32)

    heads_end = 6 * width
    qkv_own = (dot_nn(x, w_qkv) + biases[:heads_end]).astype(bf16)
    qkv_oth = (dot_nn(x, v_qkv) + biases_oth[:heads_end]).astype(bf16)
    mixed_own = attend(qkv_own, seg_row, seg_col)
    mixed_oth = attend(qkv_oth, seg_row, seg_col)

    def net_parts(own, oth, net, size):
        return own[:, net * size : (net + 1) * size], oth[:, net * size : (net + 1) * size]

    def first_norm_in(net, model):
        m_own, m_oth = net_parts(mixed_own, mixed_oth, net, width)
        o_own, o_oth = net_parts(w_out, v_out, net, dim)
        return resident + (dot_nn(m_own, o_own) + dot_nn(m_oth, o_oth)) + model[0]

    pre_s = first_norm_in(0, model_s)
    pre_t = first_norm_in(1, model_t)
    first_s, first_back = jax.vjp(layer_norm, pre_s, model_s[2], model_s[3])
    first_t = layer_norm(pre_t, model_t[2], model_t[3])
    low_s = first_s.astype(bf16)
    low_t = first_t.astype(bf16)

    def cdf_of(up):
        return 0.5 * lax.erfc(-up * 0.5**0.5)

    def forward_up(weight, bias):
        up_s = dot_nn(low_s, weight[:, :hidden]) + bias[heads_end : heads_end + hidden]
        up_t = dot_nn(low_t, weight[:, hidden:]) + bias[heads_end + hidden :]
        cdf = cdf_of(up_s)
        slope = cdf + up_s * jnp.exp(-0.5 * up_s * up_s) * (2.0 * jnp.pi) ** -0.5
        return (up_s * cdf).astype(bf16), slope, (up_t * cdf_of(up_t)).astype(bf16)

    act_s_own, slope_own, act_t_own = forward_up(w_up, biases)
    act_s_oth, slope_oth, act_t_oth = forward_up(v_up, biases_oth)

    def down(own, oth, net):
        lo, hi = net * dim, (net + 1) * dim
        return (
            dot_nn(own, w_down[:, lo:hi])
            + dot_nn(oth[:, :cut], v_down_a[:, lo:hi])
            + dot_nn(oth[:, cut:], v_down_b[:, lo:hi])
        )

    down_s = down(act_s_own, act_s_oth, 0)
    down_t = down(act_t_own, act_t_oth, 1)
    out_s, second_back = jax.vjp(layer_norm, first_s + down_s + model_s[1], model_s[4], model_s[5])
    out_t = layer_norm(first_t + down_t + model_t[1], model_t[4], model_t[5])

    d_out = jnp.where(live, out_s - out_t, 0.0)
    d_pre2, d_gain2, d_shift2 = second_back(d_out)
    d_down = d_pre2.astype(bf16)

    act_s = jnp.concatenate([act_s_own, act_s_oth], axis=1)
    grad_reduce = dot_tn(act_s, d_down).reshape(2, hidden, dim)
    d_up_own = (dot_nt(d_down, w_down[:, :dim]) * slope_own).astype(bf16)
    d_act_oth = jnp.concatenate(
        [dot_nt(d_down, v_down_a[:, :dim]), dot_nt(d_down, v_down_b[:, :dim])], axis=1
    )
    d_up_oth = (d_act_oth * slope_oth).astype(bf16)
    d_up = jnp.concatenate([d_up_own, d_up_oth], axis=1)
    grad_expand = dot_tn(low_s, d_up)
    d_first = dot_nt(d_up_own, w_up[:, :hidden]) + dot_nt(d_up_oth, v_up[:, :hidden]) + d_pre2
    d_pre1, d_gain1, d_shift1 = first_back(d_first)
    d_attn = d_pre1.astype(bf16)
    mixed_s = jnp.concatenate([mixed_own[:, :width], mixed_oth[:, :width]], axis=1)
    grad_output = dot_tn(mixed_s, d_attn).reshape(2, width, dim)
    d_mixed = jnp.concatenate(
        [dot_nt(d_attn, w_out[:, :dim]), dot_nt(d_attn, v_out[:, :dim])], axis=1
    ).astype(bf16)
    d_qkv = attend_back(qkv_own, qkv_oth, d_mixed, seg_row, seg_col)
    grad_qkv = dot_tn(x, d_qkv)
    d_tokens = (
        dot_nt(d_qkv[:, : 3 * width], w_qkv[:, : 3 * width])
        + dot_nt(d_qkv[:, 3 * width :], v_qkv[:, : 3 * width])
        + d_pre1
    )

    def cut_rows(array, bit, mine):
        size = array.shape[-2] // 2
        start = (bits[bit] if mine else 1 - bits[bit]) * size
        return lax.dynamic_slice_in_dim(array, start, size, array.ndim - 2)

    def total(grad, order):
        def cut_one(array, name, mine):
            if name != "x":
                return cut_rows(array, name, mine)
            if array.ndim == 3:
                return array[0 if mine else 1]
            size = array.shape[-1] // 2
            return array[:, :size] if mine else array[:, size:]

        terms = [grad]
        for name in order:
            send = functools.reduce(jnp.add, [cut_one(t, name, False) for t in terms])
            got = swap(send, name)
            terms = [cut_one(t, name, True) for t in terms] + [got]
        block = functools.reduce(jnp.add, terms)
        for extra in range(4, n_bits):
            block = block + swap(block, extra)
        for name in [n for n in reversed(order) if n != "x"]:
            got = swap(block, name)
            first = bits[name] == 0
            block = jnp.where(
                first,
                jnp.concatenate([block, got], axis=0),
                jnp.concatenate([got, block], axis=0),
            )
        return block

    out_reduce = total(grad_reduce, (0, "x", 1, 2, 3))
    out_expand = total(grad_expand, (0, 1, 2, "x", 3))
    out_output = total(grad_output, (0, "x", 2, 1, 3))
    out_qkv = total(grad_qkv, (0, "x", 2, 1, 3))

    sum_qkv = jnp.sum(d_qkv.astype(f32), axis=0)
    sum_up = jnp.sum(d_up.astype(f32), axis=0)
    sums_model = jnp.concatenate(
        [
            jnp.sum(d_attn.astype(f32), axis=0),
            jnp.sum(d_down.astype(f32), axis=0),
            d_gain1,
            d_shift1,
            d_gain2,
            d_shift2,
        ]
    )
    mine = jnp.concatenate([sum_qkv[: 3 * width], sum_up[:hidden], sums_model])
    theirs = jnp.concatenate([sum_qkv[3 * width :], sum_up[hidden:], sums_model])
    small = mine.reshape(-1, 128) + swap(theirs.reshape(-1, 128), "x")
    for b in range(n_bits):
        small = small + swap(small, b)
    small = small.reshape(-1)
    out_heads = small[: 3 * width].reshape(3, width)
    out_hidden = small[3 * width : 3 * width + hidden]
    out_model = small[3 * width + hidden :].reshape(6, dim)

    def both_batches(array, dtype):
        return assemble([array, swap(array, "x")], side * 4, 4, dtype).reshape(2, rows, dim)

    student_out = both_batches(out_s, bf16)
    grad_tokens = both_batches(d_tokens, f32)
    return (
        student_out,
        grad_tokens,
        out_qkv[:, :width],
        out_qkv[:, width : 2 * width],
        out_qkv[:, 2 * width :],
        out_output,
        out_expand,
        out_reduce,
        out_heads,
        out_model,
        out_hidden,
    )


def solution(mesh):
    cols = P(None, "narrow")
    rows = P("narrow", None)
    net = (cols, cols, cols, rows, cols, rows, cols, P(), P("narrow"))
    data = P(None, "wide", None)
    return jax.shard_map(
        functools.partial(on_device, mesh.shape["wide"]),
        mesh=mesh,
        in_specs=(data, P(None, "wide")) + net + net,
        out_specs=(data, data) + net,
        check_vma=False,
    )
```

```python
import functools
import types

import jax
import jax.numpy as jnp
from jax import lax
from jax.experimental import pallas as pl
from jax.experimental.pallas import tpu as pltpu
from jax.sharding import PartitionSpec as P

HEAD = 64
REGION = 256

norm_eps = 1e-06
score_weight = 0.05
big_negative = -1e30
f32 = jnp.float32
bf16 = jnp.bfloat16


def dot_nn(left, right):
    return jnp.dot(left, right, preferred_element_type=f32)


def dot_tn(left, right):
    return lax.dot_general(left, right, (((0,), (0,)), ((), ())), preferred_element_type=f32)


def dot_nt(left, right):
    return lax.dot_general(left, right, (((1,), (1,)), ((), ())), preferred_element_type=f32)


MIB = 2**20
STRIP = 384
C, Y, ZL, ZH, SIDE = range(5)


def shape(dims, dtype=f32):
    return jax.ShapeDtypeStruct(dims, dtype)


def vmem(dims, dtype=f32):
    return pltpu.VMEM(dims, dtype)


TOKEN = (8, 128)


def invoke(kernel, name, bits, arrays, specs, outs, out_specs, dep, limit, grid, scratch=(), into=None):
    single = not isinstance(outs, (list, tuple))
    outs = [outs] if single else list(outs)
    out_specs = [out_specs] if single else list(out_specs)
    count = len(arrays)
    after = [in_hbm(token) for token in dep] + ([] if into is None else [in_hbm(into)])
    first = count + len(after)
    end = first + len(outs)

    def body(bits_ref, *refs):
        kernel(bits_ref, refs[:count], refs[first:end] + refs[end + 1 :])

    anywhere = pl.BlockSpec(memory_space=pl.ANY)
    in_specs = list(specs) + [anywhere] * len(after)
    form = dict(
        in_specs=in_specs, out_specs=out_specs + [anywhere], scratch_shapes=scratch
    )
    if grid is None:
        form["in_specs"] = [pl.BlockSpec(memory_space=pltpu.SMEM)] + in_specs
    else:
        form = dict(
            grid_spec=pltpu.PrefetchScalarGridSpec(num_scalar_prefetch=1, grid=grid, **form)
        )
    *results, token = pl.pallas_call(
        body,
        out_shape=outs + [pltpu.HBM(TOKEN, f32)],
        input_output_aliases={} if into is None else {first: 0},
        compiler_params=pltpu.CompilerParams(vmem_limit_bytes=limit * MIB),
        cost_estimate=pl.CostEstimate(flops=0, bytes_accessed=0, transcendentals=0),
        name=name,
        **form,
    )(bits, *arrays, *after)
    dep[:] = [token]
    return results[0] if single else results


def call(kernel, name, bits, arrays, specs, outs, out_specs, grid, dep, limit=20, scratch=(), into=None):
    return invoke(
        kernel, name, bits, arrays, specs, outs, out_specs, dep, limit, grid, scratch, into
    )


def whole_call(kernel, name, bits, arrays, outs, dep, limit=16, hold=True):
    if hold:
        arrays = [pin(a) for a in arrays]
    count = len(arrays)
    return invoke(
        kernel, name, bits, arrays, [IN_VMEM] * count, outs, [IN_VMEM] * len(outs), dep, limit, None
    )


def pin(array):
    return pltpu.with_memory_space_constraint(array, pltpu.VMEM)


def in_hbm(array):
    return pltpu.with_memory_space_constraint(array, pltpu.HBM)


IN_VMEM = pl.BlockSpec(memory_space=pltpu.VMEM)


def place_of(bits_ref, names):
    index = 0
    for name in names:
        index = index * 2 + bits_ref[name]
    return index


def fixed(dims):
    return pl.BlockSpec(dims, lambda *a: (0,) * len(dims))


def normalize(values):
    centred = values - jnp.mean(values, axis=-1, keepdims=True)
    spread = jnp.mean(centred * centred, axis=-1, keepdims=True)
    scale = lax.rsqrt(spread + norm_eps)
    return centred * scale, scale


def norm_back(grad, unit, scale, gain):
    inner = grad * (1.0 + gain)
    return scale * (
        inner
        - jnp.mean(inner, axis=-1, keepdims=True)
        - unit * jnp.mean(inner * unit, axis=-1, keepdims=True)
    )


def cdf_of(up):
    return 0.5 + 0.5 * lax.erf(up * 0.5**0.5)


def sign_of(wide, axis):
    alpha = jnp.mean(jnp.abs(wide), axis=axis, keepdims=True)
    return (jnp.where(wide > 0, alpha, jnp.where(wide < 0, -alpha, 0.0))).astype(bf16)


def binarize(weight, axis, bits, dep):
    def kernel(bits_ref, ins, outs):
        outs[0][...] = sign_of(ins[0][...].astype(f32), axis)

    rows, columns = weight.shape
    if axis == 0:
        spec = pl.BlockSpec((rows, STRIP), lambda i, b: (0, i))
        steps = columns // STRIP
    else:
        spec = pl.BlockSpec((STRIP, columns), lambda i, b: (i, 0))
        steps = rows // STRIP
    return call(
        kernel,
        "binarize",
        bits,
        [weight],
        [spec],
        shape(weight.shape, bf16),
        spec,
        (steps,),
        dep,
    )


def binarize_pack(weights, axes, names, bits, dep):
    parts = 2 ** len(names)

    def kernel(bits_ref, ins, outs):
        part = place_of(bits_ref, names)
        at = 0
        for ref, axis, out in zip(ins, axes, outs):
            result = sign_of(ref[...].astype(f32), axis)
            out[...] = result
            rows, columns = ref.shape[0] // parts, ref.shape[1]
            mine = out[pl.ds(part * rows, rows), :].astype(f32)
            for left in range(0, columns, STRIP):
                outs[-1][at : at + rows, :] = mine[:, left : left + STRIP]
                at += rows

    total = sum(w.size for w in weights) // parts // STRIP
    return whole_call(
        kernel,
        "binarize_pack",
        bits,
        weights,
        [shape(w.shape, bf16) for w in weights] + [vmem((total, STRIP))],
        dep,
        hold=False,
    )


def pack(weights, names, bits, dep):
    parts = 2 ** len(names)

    def kernel(bits_ref, ins, outs):
        at = 0
        for ref in ins:
            rows, columns = ref.shape
            for left in range(0, columns, STRIP):
                outs[0][at : at + rows, :] = ref[:, left : left + STRIP].astype(f32)
                at += rows

    specs = [
        pl.BlockSpec((w.shape[0] // parts, w.shape[1]), lambda i, b: (place_of(b, names), 0))
        for w in weights
    ]
    total = sum(w.size for w in weights) // parts // STRIP
    return call(
        kernel,
        "pack",
        bits,
        [in_hbm(w) for w in weights],
        specs,
        [vmem((total, STRIP))],
        [IN_VMEM],
        (1,),
        dep,
    )[0]


def pack_tile(weight, row_names, column_names, bits, dep):
    def kernel(bits_ref, ins, outs):
        at = pl.multiple_of(pl.program_id(0) * tall, 8)
        outs[0][pl.ds(at, tall), :] = ins[0][...].astype(f32)

    dims = (weight.shape[0] >> len(row_names), weight.shape[1] >> len(column_names))
    steps = max(1, dims[0] // 384)
    tall = dims[0] // steps
    return call(
        kernel,
        "pack_tile",
        bits,
        [weight],
        [
            pl.BlockSpec(
                (tall, dims[1]),
                lambda i, b: (place_of(b, row_names) * steps + i, place_of(b, column_names)),
            )
        ],
        [vmem(dims)],
        [IN_VMEM],
        (steps,),
        dep,
    )[0]


def touch(array, bits, dep):
    count = len(dep)

    def body(bits_ref, *refs):
        pass

    anywhere = pl.BlockSpec(memory_space=pl.ANY)
    result, token = pl.pallas_call(
        body,
        in_specs=[pl.BlockSpec(memory_space=pltpu.SMEM)] + [anywhere] * (1 + count),
        out_specs=[anywhere] * 2,
        out_shape=[shape(array.shape, array.dtype), pltpu.HBM(TOKEN, f32)],
        input_output_aliases={1: 0},
        compiler_params=pltpu.CompilerParams(vmem_limit_bytes=MIB),
        cost_estimate=pl.CostEstimate(flops=0, bytes_accessed=0, transcendentals=0),
        name="touch",
    )(bits, array, *map(in_hbm, dep))
    dep[:] = [token]
    return result


def join(first, second, bits, dep):
    rows, columns = first.shape

    def kernel(bits_ref, ins, outs):
        for k in range(2):
            outs[0][k * rows : (k + 1) * rows, :] = ins[k][...]

    return whole_call(kernel, "join", bits, [first, second], [vmem((2 * rows, columns))], dep)[0]


def half_masks():
    lane = lax.broadcasted_iota(jnp.int32, (1, 2 * HEAD), 1)
    low = jnp.where(lane < HEAD, 1.0, 0.0).astype(bf16)
    return (low, (1.0 - low.astype(f32)).astype(bf16))


def region_masks(row_ref, col_ref):
    across = row_ref[0]
    down = col_ref[...]
    same = down == across
    live = down >= 0
    size = down.shape[0]
    diagonal = lax.broadcasted_iota(jnp.int32, (size, size), 0) == lax.broadcasted_iota(
        jnp.int32, (size, size), 1
    )
    pairs = same & live
    return pairs, pairs | diagonal


def probabilities(scores, allowed):
    masked = jnp.where(allowed, scores, big_negative)
    top = jnp.max(masked, axis=-1, keepdims=True)
    expo = jnp.exp(masked - top)
    total = jnp.sum(expo, axis=-1, keepdims=True)
    return expo * (1.0 / total)


def attention(parts, allowed, masks, scale, write):
    width = parts[0].shape[1]
    for at in range(0, width, 2 * HEAD):
        query, keys, values = (part[:, at : at + 2 * HEAD] for part in parts)
        probs = [
            probabilities(dot_nt(query * mask, keys) * scale, allowed).astype(bf16) for mask in masks
        ]
        stacked = jnp.concatenate([values * mask for mask in masks], axis=0)
        write(at, dot_nn(jnp.concatenate(probs, axis=1), stacked).astype(bf16))


def attend_own(x, weights, biases, seg_row, seg_col, bits, dep):
    rows, dim = x.shape
    width = weights[0].shape[1]

    def kernel(bits_ref, ins, outs):
        x_ref, bias_ref, row_ref, col_ref = ins[:4]
        tokens = x_ref[...]
        pairs, allowed = region_masks(row_ref, col_ref)
        masks = half_masks()
        for net in range(2):
            parts = []
            for k in range(3):
                row = 3 * net + k
                part = dot_nn(tokens, ins[4 + row][...]) + bias_ref[row : row + 1, :]
                parts.append(part.astype(bf16))
                if row < 5:
                    outs[0][:, row * width : (row + 1) * width] = parts[k]

            def write(at, mixed, net=net):
                outs[1 + net][:, at : at + 2 * HEAD] = mixed

            attention(parts, allowed, masks, HEAD ** (-0.5), write)

    def block(columns):
        return pl.BlockSpec((REGION, columns), lambda i, b: (i, 0))

    return call(
        kernel,
        "attend_own",
        bits,
        [x, biases, seg_row, seg_col, *weights],
        [
            block(dim),
            fixed(biases.shape),
            pl.BlockSpec((1, 1, REGION), lambda i, b: (i, 0, 0)),
            block(1),
        ]
        + [fixed(w.shape) for w in weights],
        [shape((rows, 5 * width), bf16), shape((rows, width), bf16), shape((rows, width), bf16)],
        [block(5 * width), block(width), block(width)],
        (rows // REGION,),
        dep,
    )


def attend_other(
    x, pieces, names, biases, seg_row, seg_col, mixed, output, model, student, bits, dep
):
    rows, dim = x.shape
    width = mixed.shape[1]
    parts = 2 ** len(names)
    half_parts = parts // 2
    tall = dim // parts
    short = width // parts
    per_part = 3 * tall + 2 * short
    first_row = 0 if student else 3
    kept = 3 if student else 2

    def kernel(bits_ref, ins, outs):
        x_ref, bias_ref, row_ref, col_ref, mine_ref, theirs_ref, mixed_ref, out_ref, model_ref = ins
        qkv_ref, low_ref, first_ref = outs[:3]
        weight_refs = outs[5:9] if student else outs[3:7]
        part = place_of(bits_ref, names)

        @pl.when(pl.program_id(0) == 0)
        def _():
            for k in range(parts):
                ref = (mine_ref, theirs_ref)[k // half_parts]
                base = (k % half_parts) * per_part
                where = jnp.bitwise_xor(part, k)
                for m in range(3):
                    weight_refs[m][pl.ds(pl.multiple_of(where * tall, 16), tall), :] = ref[
                        base + m * tall : base + (m + 1) * tall, :
                    ].astype(bf16)
                for m in range(2):
                    at = base + 3 * tall + m * short
                    weight_refs[3][
                        pl.ds(pl.multiple_of(where * short, 16), short), m * STRIP : (m + 1) * STRIP
                    ] = ref[at : at + short, :].astype(bf16)

        tokens = x_ref[...]
        pairs, allowed = region_masks(row_ref, col_ref)
        masks = half_masks()
        parts_qkv = []
        for k in range(3):
            row = first_row + k
            part_k = dot_nn(tokens, weight_refs[k][...]) + bias_ref[row : row + 1, :]
            parts_qkv.append(part_k.astype(bf16))
            if k < kept:
                qkv_ref[:, k * width : (k + 1) * width] = parts_qkv[k]
        tiles = []
        attention(parts_qkv, allowed, masks, HEAD ** (-0.5), lambda at, tile: tiles.append(tile))
        mine = jnp.concatenate(tiles, axis=1)
        pre = (
            tokens.astype(f32)
            + (dot_nn(mixed_ref[...], out_ref[...]) + dot_nn(mine, weight_refs[3][...]))
            + model_ref[0:1, :]
        )
        unit, scale = normalize(pre)
        first = unit * (1.0 + model_ref[2:3, :]) + model_ref[3:4, :]
        low_ref[...] = first.astype(bf16)
        first_ref[...] = first
        if student:
            outs[3][...] = mine
            outs[4][...] = pre

    def block(columns):
        return pl.BlockSpec((REGION, columns), lambda i, b: (i, 0))

    weights = [shape((dim, width), bf16)] * 3 + [shape((width, dim), bf16)]
    outs = [shape((rows, kept * width), bf16), shape((rows, dim), bf16), shape((rows, dim))]
    out_specs = [block(kept * width), block(dim), block(dim)]
    if student:
        outs += [shape((rows, width), bf16), shape((rows, dim)), *weights]
        out_specs += [block(width), block(dim)] + [fixed(w.shape) for w in weights]
    return call(
        kernel,
        "attend_other",
        bits,
        [x, biases, seg_row, seg_col, *map(pin, pieces), mixed, output, model],
        [
            block(dim),
            fixed(biases.shape),
            pl.BlockSpec((1, 1, REGION), lambda i, b: (i, 0, 0)),
            block(1),
            IN_VMEM,
            IN_VMEM,
            block(width),
            fixed(output.shape),
            fixed(model.shape),
        ],
        outs,
        out_specs,
        (rows // REGION,),
        dep,
        limit=24,
        scratch=[] if student else [pltpu.VMEM(w.shape, bf16) for w in weights],
    )


def activate(up, outs, student):
    cdf = cdf_of(up)
    outs[0][...] = (up * cdf).astype(bf16)
    if student:
        bell = jnp.exp(-0.5 * up * up) * (2.0 * jnp.pi) ** -0.5
        outs[1][...] = (cdf + up * bell).astype(bf16)


def up_own(low, weight, biases, first_row, student, bits, dep):
    tokens, dim = low.shape
    hidden = weight.shape[1]

    def kernel(bits_ref, ins, outs):
        j = pl.program_id(0)
        up = dot_nn(ins[0][...], ins[1][...]) + ins[2][pl.ds(first_row + j, 1), :]
        activate(up, outs, student)

    count = 2 if student else 1
    return call(
        kernel,
        "up_own",
        bits,
        [low, weight, biases],
        [fixed(low.shape), pl.BlockSpec((dim, STRIP), lambda j, b: (0, j)), fixed(biases.shape)],
        [shape((tokens, hidden), bf16)] * count,
        [pl.BlockSpec((tokens, STRIP), lambda j, b: (0, j))] * count,
        (hidden // STRIP,),
        dep,
    )


def up_other(low, mine, theirs, names, biases, first_row, student, bits, dep):
    tokens, dim = low.shape
    steps = mine.shape[0] // STRIP
    half = dim // 2

    def kernel(bits_ref, ins, outs):
        low_ref, tile_m, tile_o, bias_ref = ins
        j = jnp.bitwise_xor(pl.program_id(0), place_of(bits_ref, names))
        at = pl.ds(pl.multiple_of(pl.program_id(0) * half, 8), half)
        weight_ref = outs[2] if student else outs[1]
        core = bits_ref[C]
        weight_ref[pl.ds(pl.multiple_of(core * half, 16), half), :] = tile_m[at, :].astype(bf16)
        weight_ref[pl.ds(pl.multiple_of((1 - core) * half, 16), half), :] = tile_o[at, :].astype(bf16)
        up = dot_nn(low_ref[...], weight_ref[...]) + bias_ref[pl.ds(first_row + j, 1), :]
        activate(up, outs, student)

    def column(j, b):
        return (0, jnp.bitwise_xor(j, place_of(b, names)))

    outs = [shape((tokens, steps * STRIP), bf16)]
    out_specs = [pl.BlockSpec((tokens, STRIP), column)]
    if student:
        outs += [outs[0], shape((dim, steps * STRIP), bf16)]
        out_specs += [out_specs[0], pl.BlockSpec((dim, STRIP), column)]
    return call(
        kernel,
        "up_other",
        bits,
        [low, pin(mine), pin(theirs), biases],
        [fixed(low.shape), IN_VMEM, IN_VMEM, fixed(biases.shape)],
        outs,
        out_specs,
        (steps,),
        dep,
        limit=16,
        scratch=[] if student else [pltpu.VMEM((dim, STRIP), bf16)],
    )


def down_own(acts, weights, firsts, models, bits, dep):
    tokens, hidden = acts[0].shape
    dim = weights[0].shape[1]

    def kernel(bits_ref, ins, outs):
        for net in range(2):
            act, weight, first, model = ins[4 * net : 4 * net + 4]
            outs[net][...] = first[...] + model[1:2, :] + dot_nn(act[...], weight[...])

    def block(columns):
        return pl.BlockSpec((REGION, columns), lambda i, b: (i, 0))

    arrays = []
    specs = []
    for net in range(2):
        arrays += [acts[net], weights[net], firsts[net], models[net]]
        specs += [block(hidden), fixed((hidden, dim)), block(dim), fixed(models[net].shape)]
    return call(
        kernel,
        "down_own",
        bits,
        arrays,
        specs,
        [shape((tokens, dim))] * 2,
        [block(dim)] * 2,
        (tokens // REGION,),
        dep,
        limit=24,
    )


def down_other(acts, student_tiles, teacher_tiles, names, partials, models, seg_col, bits, dep):
    tokens, hidden = acts[0].shape
    dim = partials[0].shape[1]
    half = dim // 2
    steps = hidden // STRIP

    def kernel(bits_ref, ins, outs):
        act_s, act_t, s_mine, s_other, t_mine, t_other, part_s, part_t, model_s, model_t, seg = ins
        out_ref, pre_ref, down_ref, sums_ref, weight_ref, low_ref, teacher_ref = outs
        step = pl.program_id(0)
        first_core = bits_ref[C] == 0

        @pl.when(step == 0)
        def _():
            place = place_of(bits_ref, names)
            for k in range(steps):
                rows = slice(k * STRIP, (k + 1) * STRIP)
                where = pl.ds(pl.multiple_of(jnp.bitwise_xor(place, k) * STRIP, 16), STRIP)
                tile, other = s_mine[rows, :].astype(bf16), s_other[rows, :].astype(bf16)
                weight_ref[where, :half] = jnp.where(first_core, tile, other)
                weight_ref[where, half:] = jnp.where(first_core, other, tile)
                tile, other = t_mine[rows, :].astype(bf16), t_other[rows, :].astype(bf16)
                teacher_ref[rows, :half] = jnp.where(first_core, tile, other)
                teacher_ref[rows, half:] = jnp.where(first_core, other, tile)

        unit_s, scale_s = normalize(part_s[...] + dot_nn(act_s[...], weight_ref[...]))
        unit_t, _ = normalize(part_t[...] + dot_nn(act_t[...], teacher_ref[...]))
        gain = model_s[4:5, :]
        out_s = unit_s * (1.0 + gain) + model_s[5:6, :]
        out_t = unit_t * (1.0 + model_t[4:5, :]) + model_t[5:6, :]
        out_ref[...] = out_s
        low_ref[0] = out_s.astype(bf16)
        grad = jnp.where(seg[...] >= 0, out_s - out_t, 0.0)
        d_pre = norm_back(grad, unit_s, scale_s, gain)
        pre_ref[...] = d_pre
        low = d_pre.astype(bf16)
        down_ref[...] = low
        add_sums(sums_ref, (grad * unit_s, grad, low.astype(f32)), step)

    def block(columns):
        return pl.BlockSpec((REGION, columns), lambda i, b: (i, 0))

    return call(
        kernel,
        "down_other",
        bits,
        [*acts, *map(pin, student_tiles), *map(pin, teacher_tiles), *partials, *models, seg_col],
        [block(hidden)] * 2
        + [IN_VMEM] * 4
        + [block(dim)] * 2
        + [fixed(m.shape) for m in models]
        + [block(1)],
        [
            shape((tokens, dim)),
            shape((tokens, dim)),
            shape((tokens, dim), bf16),
            shape((8, dim)),
            shape((hidden, dim), bf16),
            pltpu.HBM((2, tokens, dim), bf16),
        ],
        [
            block(dim),
            block(dim),
            block(dim),
            fixed((8, dim)),
            fixed((hidden, dim)),
            pl.BlockSpec((1, REGION, dim), lambda i, b: (b[SIDE], i, 0)),
        ],
        (tokens // REGION,),
        dep,
        limit=28,
        scratch=[pltpu.VMEM((hidden, dim), bf16)],
    )


def up_back(d_down, weights, slopes, bits, dep):
    tokens, dim = d_down.shape
    hidden = weights[0].shape[0]

    def kernel(bits_ref, ins, outs):
        rows = []
        for half in range(2):
            grad = dot_nt(ins[0][...], ins[1 + half][...])
            low = (grad * ins[3 + half][...].astype(f32)).astype(bf16)
            outs[half][...] = low
            rows.append(jnp.sum(low.astype(f32), axis=0, keepdims=True))
        outs[2][...] = jnp.concatenate(rows + [jnp.zeros((6, STRIP), f32)], axis=0)

    block = pl.BlockSpec((tokens, STRIP), lambda j, b: (0, j))
    return call(
        kernel,
        "up_back",
        bits,
        [d_down, *weights, *slopes],
        [fixed(d_down.shape)] + [pl.BlockSpec((STRIP, dim), lambda j, b: (j, 0))] * 2 + [block] * 2,
        [shape((tokens, hidden), bf16)] * 2 + [shape((8, hidden))],
        [block, block, pl.BlockSpec((8, STRIP), lambda j, b: (0, j))],
        (hidden // STRIP,),
        dep,
    )


def add_sums(ref, arrays, step):
    rows = [jnp.sum(v, axis=0, keepdims=True) for v in arrays]
    rows.append(jnp.zeros((8 - len(rows), rows[0].shape[1]), f32))
    new = jnp.concatenate(rows, axis=0)
    ref[...] = jnp.where(step == 0, new, ref[...] + new)


def first_back(d_ups, weights, d_pre2, pre, model, outputs, bits, dep):
    tokens, hidden = d_ups[0].shape
    dim = d_pre2.shape[1]
    width = outputs[0].shape[0]

    def kernel(bits_ref, ins, outs):
        d_own, d_oth, w_own, w_oth, d_pre2_ref, pre_ref, model_ref, o_own, o_oth = ins
        grad = d_pre2_ref[...] + (dot_nt(d_own[...], w_own[...]) + dot_nt(d_oth[...], w_oth[...]))
        unit, scale = normalize(pre_ref[...])
        d_pre = norm_back(grad, unit, scale, model_ref[2:3, :])
        outs[0][...] = d_pre
        low = d_pre.astype(bf16)
        outs[1][...] = low
        outs[2][...] = dot_nt(low, o_own[...]).astype(bf16)
        outs[3][...] = dot_nt(low, o_oth[...]).astype(bf16)
        add_sums(outs[4], (grad * unit, grad, low.astype(f32)), pl.program_id(0))

    def block(columns):
        return pl.BlockSpec((REGION, columns), lambda i, b: (i, 0))

    return call(
        kernel,
        "first_back",
        bits,
        [*d_ups, *weights, d_pre2, pre, model, *outputs],
        [block(hidden)] * 2
        + [fixed(w.shape) for w in weights]
        + [block(dim)] * 2
        + [fixed(model.shape)]
        + [fixed(o.shape) for o in outputs],
        [
            shape((tokens, dim)),
            shape((tokens, dim), bf16),
            shape((tokens, width), bf16),
            shape((tokens, width), bf16),
            shape((8, dim)),
        ],
        [block(dim), block(dim), block(width), block(width), fixed((8, dim))],
        (tokens // REGION,),
        dep,
        limit=28,
    )


def token_grad(d_pre, terms, bits, dep):
    tokens, dim = d_pre.shape

    def kernel(bits_ref, ins, outs):
        total = ins[0][...]
        for k in range(len(terms)):
            total = total + dot_nt(ins[1 + 2 * k][...], ins[2 + 2 * k][...])
        outs[0][...] = total
        outs[1][0] = total

    arrays = [d_pre]
    specs = [pl.BlockSpec((REGION, dim), lambda i, b: (i, 0))]
    for grad, at, weight in terms:
        arrays += [grad, weight]
        specs += [
            pl.BlockSpec((REGION, weight.shape[1]), lambda i, b, at=at: (i, at)),
            fixed(weight.shape),
        ]
    return call(
        kernel,
        "token_grad",
        bits,
        arrays,
        specs,
        [shape((tokens, dim)), pltpu.HBM((2, tokens, dim), f32)],
        [specs[0], pl.BlockSpec((1, REGION, dim), lambda i, b: (b[SIDE], i, 0))],
        (tokens // REGION,),
        dep,
    )


def attend_back(qkv, grads, seg_row, seg_col, bits, dep):
    rows, columns = qkv[0].shape
    width = columns // 5
    step = 2 * HEAD

    def kernel(bits_ref, ins, outs):
        pairs, allowed = region_masks(ins[5], ins[6])
        weight = jnp.where(pairs, score_weight, 0.0)
        masks = half_masks()
        scale = HEAD ** (-0.5)

        @pl.when(pl.program_id(0) == 0)
        def _():
            outs[4][...] = jnp.zeros_like(outs[4])

        for part in range(2):
            for at in range(0, width, step):
                places = [(0, k) for k in range(5)] if part == 0 else [(1, 0), (1, 1), (1, 2), (2, 0), (2, 1)]
                query, keys, values, query_t, keys_t = (
                    ins[r][:, k * width + at : k * width + at + step] for r, k in places
                )
                grad = ins[3 + part][:, at : at + step]
                probs = []
                slopes = []
                for mask in masks:
                    scores = dot_nt(query * mask, keys) * scale
                    prob = probabilities(scores, allowed)
                    gap = scores - dot_nt(query_t * mask, keys_t) * scale
                    d_prob = dot_nt(grad * mask, values)
                    mean = jnp.sum(prob * d_prob, axis=-1, keepdims=True)
                    slope = prob * (d_prob - mean) + weight * gap
                    probs.append(prob.astype(bf16))
                    slopes.append(slope.astype(bf16))

                def both(array):
                    return jnp.concatenate([array * mask for mask in masks], axis=0)

                d_query = dot_nn(jnp.concatenate(slopes, axis=1), both(keys)) * scale
                d_keys = dot_tn(jnp.concatenate(slopes, axis=0), both(query)) * scale
                d_values = dot_tn(jnp.concatenate(probs, axis=0), both(grad))
                for k, result in enumerate((d_query, d_keys, d_values)):
                    low = result.astype(bf16)
                    if k < 2:
                        outs[part][:, k * width + at : k * width + at + step] = low
                    else:
                        outs[2 + part][:, at : at + step] = low
                    outs[4][part : part + 1, k * width + at : k * width + at + step] += jnp.sum(
                        low.astype(f32), axis=0, keepdims=True
                    )

    def block(columns):
        return pl.BlockSpec((REGION, columns), lambda i, b: (i, 0))

    return call(
        kernel,
        "attend_back",
        bits,
        [*qkv, *grads, seg_row, seg_col],
        [
            block(columns),
            block(3 * width),
            block(2 * width),
            block(width),
            block(width),
            pl.BlockSpec((1, 1, REGION), lambda i, b: (i, 0, 0)),
            block(1),
        ],
        [shape((rows, 2 * width), bf16)] * 2
        + [shape((rows, width), bf16)] * 2
        + [shape((8, 3 * width))],
        [block(2 * width)] * 2 + [block(width)] * 2 + [fixed((8, 3 * width))],
        (rows // REGION,),
        dep,
    )


def outer(groups, bits, dep, start=0, size=None, block=384):
    size = size or groups[0][0][0].shape[1]
    tall = size // 2
    steps = tall // block
    tokens = groups[0][0][0].shape[0]
    arrays = []
    specs = []
    for lhs, rhs, at, columns in groups:
        for half in range(2):

            def left(p, h, i, b, half=half, lhs=lhs):
                core = jnp.where(p == 0, 1 - b[C], b[C])
                where = start // block + core * steps + i
                return (0, where if lhs[0] is lhs[1] else jnp.where(h == half, where, start // block))

            arrays += [lhs[half], rhs[half]]
            specs += [
                pl.BlockSpec((tokens, block), left),
                pl.BlockSpec((tokens, columns), lambda p, h, i, b, at=at: (0, at)),
            ]
    wide = sum(g[3] for g in groups)

    def kernel(bits_ref, ins, outs):
        for phase in range(2):
            for half in range(2):

                @pl.when((pl.program_id(0) == phase) & (pl.program_id(1) == half))
                def _(phase=phase, half=half):
                    at = 0
                    row = pl.multiple_of(pl.program_id(2) * block, 8)
                    for k, group in enumerate(groups):
                        lhs, rhs = ins[4 * k + 2 * half], ins[4 * k + 2 * half + 1]
                        outs[phase][half, pl.ds(row, block), at : at + group[3]] = dot_tn(
                            lhs[...], rhs[...]
                        )
                        at += group[3]

    out = vmem((2, tall, wide))
    return call(
        kernel, "outer", bits, arrays, specs, [out, out], [IN_VMEM, IN_VMEM], (2, 2, steps), dep, limit=16
    )


def split(first, second, name, bits, dep, limit=16):
    halves, rows, columns = first.shape
    out = vmem((1, rows, columns)) if name == "x" else vmem((halves, rows // 2, columns))

    def kernel(bits_ref, ins, outs):
        for k in range(2):
            if name == "x":
                where = (pl.ds(1 - k, 1), slice(None))
            else:
                bit = bits_ref[name]
                start = (1 - bit if k == 0 else bit) * (rows // 2)
                where = (slice(None), pl.ds(pl.multiple_of(start, 8), rows // 2))
            outs[k][...] = ins[0][where] + ins[1][where]

    return whole_call(kernel, "split", bits, [first, second], [out, out], dep, limit)


def add(first, second, bits, dep):
    def kernel(bits_ref, ins, outs):
        outs[0][...] = ins[0][...] + ins[1][...]

    return whole_call(kernel, "add", bits, [first, second], [vmem(first.shape)], dep)[0]


def merge(mine, theirs, name, bits, dep):
    one, rows, columns = mine.shape

    def kernel(bits_ref, ins, outs):
        bit = bits_ref[name]
        for k in range(2):
            start = (bit if k == 0 else 1 - bit) * rows
            outs[0][:, pl.ds(pl.multiple_of(start, 8), rows)] = ins[k][...]

    return whole_call(kernel, "merge", bits, [mine, theirs], [vmem((1, 2 * rows, columns))], dep)[0]


def finish(pieces, cuts, outs, bits, dep, into=None):
    def kernel(bits_ref, ins, refs):
        results, sems = refs[:-1], refs[-1]
        copies = []
        for k, (piece, source, out, target) in enumerate(cuts):
            copy = pltpu.make_async_copy(
                ins[piece].at[source], results[out].at[target(bits_ref)], sems.at[k]
            )
            copy.start()
            copies.append(copy)
        for copy in copies:
            copy.wait()

    return invoke(
        kernel,
        "finish",
        bits,
        [*map(pin, pieces)],
        [IN_VMEM] * len(pieces),
        [pltpu.HBM(o.shape, o.dtype) for o in outs],
        [pl.BlockSpec(memory_space=pl.ANY)] * len(outs),
        dep,
        8,
        None,
        [pltpu.SemaphoreType.DMA((len(cuts),))],
        into,
    )


def flip(array, bits, dep):
    def kernel(bits_ref, ins, outs):
        outs[0][...] = ins[0][0].T

    one, rows, columns = array.shape
    return whole_call(kernel, "flip", bits, [array], [vmem((columns, rows))], dep)[0]


def put_rows(array, bits, dep, into):
    two, rows, dim = into.shape
    tall = rows // 4

    def kernel(bits_ref, ins, outs):
        at = pl.ds(pl.multiple_of(pl.program_id(0) * tall, 8), tall)
        outs[-1][0] = ins[0][at, :].astype(into.dtype)

    return call(
        kernel,
        "place",
        bits,
        [pin(array)],
        [IN_VMEM],
        [pltpu.HBM(into.shape, into.dtype)],
        [pl.BlockSpec((1, tall, dim), lambda i, b: (1 - b[SIDE], i, 0))],
        (4,),
        dep,
        into=into,
    )[0]


def collect(sums, other, bits, dep):
    wide = sum(s.shape[1] for s in sums)

    def kernel(bits_ref, ins, outs):
        at = 0
        for k, ref in enumerate(ins):
            columns = ref.shape[1]
            if other and k < 2:
                both = jnp.concatenate([ref[1:2, :], ref[0:1, :], ref[2:, :]], axis=0)
            else:
                both = ref[...]
            outs[0][:, at : at + columns] = both
            at += columns

    return whole_call(kernel, "collect", bits, sums, [vmem((8, wide))], dep)[0]


R0, R1, E0, E1, QK, VO, SUMS = range(7)
(
    DO_B0,
    DO_B1,
    DO_BIN_A,
    DO_BIN_E,
    DO_BIN_R,
    DO_ATT_O,
    DO_KBT,
    DO_KBS,
    DO_UP_OT,
    DO_UP_OS,
    DO_UP_XT,
    DO_UP_XS,
    DO_DN_O,
    DO_KD,
    DO_S,
    DO_TT,
    DO_SF,
    DO_TF,
    DO_DU,
    DO_DH1,
    DO_ATT,
    DO_TOK,
    DO_O_R0,
    DO_O_R1,
    DO_O_E0,
    DO_O_E1,
    DO_O_QK,
    DO_O_VO,
) = range(28)
OUTERS = (DO_O_R0, DO_O_R1, DO_O_E0, DO_O_E1, DO_O_QK, DO_O_VO)
CHUNK_STEP, FETCH_STEP = 50, 60
PATHS = {
    R0: ("x", Y, ZL, ZH),
    R1: ("x", Y, ZL, ZH),
    E0: (Y, ZL, "x", ZH),
    E1: (ZL, "x", ZH, Y),
    QK: ("x", Y, ZL, ZH),
    VO: (ZL, Y, "x", ZH),
}
FETCH = ((Y,), (Y, ZL), (Y, ZL), (Y, ZL), (ZL, Y))
ORDER = (
    FETCH_STEP + 3, DO_B0, DO_BIN_A, DO_B1, DO_BIN_E, DO_BIN_R, FETCH_STEP + 2, FETCH_STEP + 3,
    FETCH_STEP + 5, FETCH_STEP + 6, FETCH_STEP + 1, FETCH_STEP + 2, FETCH_STEP + 3, DO_ATT_O,
    FETCH_STEP + 2, FETCH_STEP + 1, FETCH_STEP + 3, FETCH_STEP + 4, FETCH_STEP + 5,
    FETCH_STEP + 4, FETCH_STEP + 1, FETCH_STEP + 2, FETCH_STEP + 3, FETCH_STEP + 1, DO_KBT,
    FETCH_STEP + 4, FETCH_STEP + 2, FETCH_STEP + 5, DO_KBS, DO_UP_OT, DO_UP_XT, DO_UP_OS,
    DO_DN_O, FETCH_STEP + 4, FETCH_STEP + 5, FETCH_STEP + 6, FETCH_STEP + 4, DO_UP_XS,
    FETCH_STEP + 5, FETCH_STEP + 6, DO_KD, DO_DU, DO_O_R0, DO_O_E1, CHUNK_STEP + R0,
    CHUNK_STEP + E1, DO_O_E0, CHUNK_STEP + E0, DO_O_R1, CHUNK_STEP + R1, CHUNK_STEP + E1,
    CHUNK_STEP + R0, DO_DH1, DO_ATT, DO_O_VO, CHUNK_STEP + VO, DO_O_QK, CHUNK_STEP + R0,
    CHUNK_STEP + E1, CHUNK_STEP + QK, CHUNK_STEP + VO, CHUNK_STEP + R1, DO_TOK,
    CHUNK_STEP + QK, CHUNK_STEP + E0, CHUNK_STEP + R0, CHUNK_STEP + E1, CHUNK_STEP + E1,
    CHUNK_STEP + R0, CHUNK_STEP + VO, CHUNK_STEP + E0, CHUNK_STEP + R0, CHUNK_STEP + E1,
    CHUNK_STEP + R1, DO_S, CHUNK_STEP + E0, CHUNK_STEP + QK, DO_TT, CHUNK_STEP + E1,
    CHUNK_STEP + VO, CHUNK_STEP + E0, CHUNK_STEP + SUMS, CHUNK_STEP + VO, CHUNK_STEP + R0,
    CHUNK_STEP + SUMS, CHUNK_STEP + E0, CHUNK_STEP + R1, CHUNK_STEP + SUMS, CHUNK_STEP + E1,
    CHUNK_STEP + QK, CHUNK_STEP + R1, CHUNK_STEP + SUMS, CHUNK_STEP + VO, CHUNK_STEP + R0,
    CHUNK_STEP + QK, CHUNK_STEP + R1, CHUNK_STEP + E0, CHUNK_STEP + VO, CHUNK_STEP + R1,
    CHUNK_STEP + QK, CHUNK_STEP + SUMS, DO_TF, CHUNK_STEP + QK, CHUNK_STEP + E0,
    CHUNK_STEP + R1, DO_SF, CHUNK_STEP + E1, CHUNK_STEP + E0, CHUNK_STEP + R0,
    CHUNK_STEP + SUMS, CHUNK_STEP + R1, CHUNK_STEP + QK, CHUNK_STEP + VO, CHUNK_STEP + QK,
    CHUNK_STEP + VO,
)


def on_device(n_wide, tokens, segments, *params):
    (w_q, w_k, w_v, w_o, w_e, w_r, heads_s, model_s, hidden_s) = params[:9]
    (t_q, t_k, t_v, t_o, t_e, t_r, heads_t, model_t, hidden_t) = params[9:]
    n_bits = n_wide.bit_length() - 1
    side = lax.axis_index("narrow")
    place = lax.axis_index("wide")
    bits = jnp.stack([(place >> b) & 1 for b in range(4)] + [side]).astype(jnp.int32)
    dim, width = w_q.shape
    hidden = w_e.shape[1]

    def swap(array, bit):
        if bit == "x":
            return lax.ppermute(array, "narrow", [(0, 1), (1, 0)])
        return lax.ppermute(array, "wide", [(i, i ^ (1 << bit)) for i in range(n_wide)])

    x = lax.dynamic_index_in_dim(tokens, side, 0, keepdims=False)
    segment = lax.dynamic_index_in_dim(segments, side, 0, keepdims=False)
    rows = x.shape[0]
    seg_row = segment.reshape(rows // REGION, 1, REGION)
    seg_col = segment.reshape(rows, 1)
    biases = jnp.concatenate(
        [heads_s, heads_t, hidden_s.reshape(-1, width), hidden_t.reshape(-1, width)]
    )
    blocks = hidden // width
    models = (model_s, model_t)
    half = hidden // 2

    v = types.SimpleNamespace()
    fetched = {}
    last = []

    def fetch(key, made, path):
        held = swap(made(), "x")
        yield
        held = touch(held, bits, last)
        for name in path:
            got = swap(held, name)
            yield
            held = join(held, got, bits, last)
        got = swap(held, C)
        yield
        fetched[key] = (held, touch(got, bits, last))
        yield

    def fetch_direct(key, made):
        zero = swap(made(), "x")
        yield
        zero = touch(zero, bits, last)
        got = swap(zero, C)
        yield
        fetched[key] = (zero, touch(got, bits, last))
        yield

    def reduce_chunk(made, path):
        send, keep = made
        got = swap(touch(send, bits, last), C)
        yield
        for name in path[:-1]:
            send, keep = split(keep, got, name, bits, last)
            got = swap(send, name)
            yield
        block = add(keep, got, bits, last)
        got = swap(block, path[-1])
        yield
        for extra in range(4, n_bits):
            block = block + got
            got = swap(block, extra)
        block = add(block, got, bits, last)
        back = [name for name in reversed(path[:-1]) if name != "x"] + [C]
        for name in back[:-1]:
            got = swap(block, name)
            yield
            block = merge(block, got, name, bits, last)
        got = swap(block, C)
        yield
        yield (block, got)

    def small_sums():
        sums = [v.sums_qkv, v.sums_up, v.sums1, v.sums2]
        total = collect(sums, False, bits, last)
        got = swap(collect(sums, True, bits, last), "x")
        yield
        for b in range(4):
            total = add(total, got, bits, last)
            got = swap(total, b)
            yield
        total = add(total, got, bits, last)
        for b in range(4, n_bits):
            total = total + swap(total, b)
        yield total

    tall = dim // 2
    steps = {}
    fetching = {}
    outs = types.SimpleNamespace(reduce=None, expand=None)

    def names_of(k):
        return (C, *reversed(FETCH[k - 1]))

    def start_fetch(k):
        names = names_of(k)
        makers = {
            1: lambda: pack([t_q, t_k, t_v, t_o], names, bits, last),
            2: lambda: touch(v.b_pack, bits, last),
            3: lambda: pack_tile(t_e, (C,), names[1:], bits, last),
            4: lambda: pack_tile(v.b_e, (C,), names[1:], bits, last),
            5: lambda: pack_tile(v.b_r, names[1:], (C,), bits, last),
        }
        return fetch(k, makers[k], FETCH[k - 1])

    def do(name):
        if name == DO_B0:
            v.biases_oth = swap(touch(biases, bits, last), "x")
        elif name == DO_B1:
            v.biases_oth = touch(v.biases_oth, bits, last)
        elif name == DO_BIN_A:
            *v.b, v.b_pack = binarize_pack(
                [w_q, w_k, w_v, w_o], (0, 0, 0, 1), names_of(2), bits, last
            )
        elif name == DO_BIN_E:
            v.b_e = binarize(w_e, 0, bits, last)
        elif name == DO_BIN_R:
            v.b_r = binarize(w_r, 1, bits, last)
        elif name == DO_ATT_O:
            b = v.b
            v.qkv_own, *v.mixed_own = attend_own(
                x,
                (b[0], b[1], b[2], in_hbm(t_q), in_hbm(t_k), in_hbm(t_v)),
                biases,
                seg_row,
                seg_col,
                bits,
                last,
            )
        elif name == DO_KBT:
            v.qk_t, v.low_t, v.first_t = attend_other(
                x,
                fetched[1],
                names_of(1),
                v.biases_oth,
                seg_row,
                seg_col,
                v.mixed_own[1],
                t_o,
                model_t,
                False,
                bits,
                last,
            )
        elif name == DO_KBS:
            v.qkv_oth, v.low_s, v.first_s, v.mixed_oth, v.pre_s, *v.o = attend_other(
                x,
                fetched[2],
                names_of(2),
                v.biases_oth,
                seg_row,
                seg_col,
                v.mixed_own[0],
                v.b[3],
                model_s,
                True,
                bits,
                last,
            )
        elif name == DO_UP_OT:
            (v.act_t_own,) = up_own(v.low_t, t_e, biases, 6 + blocks, False, bits, last)
        elif name == DO_UP_OS:
            v.act_s_own, v.slope_own = up_own(
                v.low_s, v.b_e, biases, 6, True, bits, last
            )
        elif name == DO_UP_XT:
            (v.act_t_oth,) = up_other(
                v.low_t, *fetched[3], names_of(3)[1:], v.biases_oth, 6 + blocks, False, bits, last
            )
        elif name == DO_UP_XS:
            v.act_s_oth, v.slope_oth, v.o_e = up_other(
                v.low_s, *fetched[4], names_of(4)[1:], v.biases_oth, 6, True, bits, last
            )
        elif name == DO_DN_O:
            v.partials = down_own(
                (v.act_s_own, v.act_t_own),
                (v.b_r, t_r),
                (v.first_s, v.first_t),
                models,
                bits,
                last,
            )
        elif name == DO_KD:
            v.out_s, v.d_pre2, v.d_down, v.sums2, v.o_r, v.out_low = down_other(
                (v.act_s_oth, v.act_t_oth),
                fetched[5],
                fetched[6],
                names_of(5)[1:],
                v.partials,
                models,
                seg_col,
                bits,
                last,
            )
        elif name == DO_S:
            v.out_other = swap(touch(v.out_s, bits, last), "x")
        elif name == DO_TT:
            v.tok_other = swap(touch(v.d_tokens, bits, last), "x")
        elif name in (DO_SF, DO_TF):
            if name == DO_SF:
                outs.low = put_rows(v.out_other, bits, last, v.out_low)
            else:
                outs.tok = put_rows(v.tok_other, bits, last, v.out_tok)
        elif name == DO_DU:
            v.d_up_own, v.d_up_oth, v.sums_up = up_back(
                v.d_down,
                (v.b_r, v.o_r),
                (v.slope_own, v.slope_oth),
                bits,
                last,
            )
        elif name == DO_DH1:
            v.d_pre1, v.d_attn, *v.d_mixed, v.sums1 = first_back(
                (v.d_up_own, v.d_up_oth),
                (v.b_e, v.o_e),
                v.d_pre2,
                v.pre_s,
                model_s,
                (v.b[3], v.o[3]),
                bits,
                last,
            )
        elif name == DO_ATT:
            *v.dqk, v.dv_own, v.dv_oth, v.sums_qkv = attend_back(
                (v.qkv_own, v.qkv_oth, v.qk_t), v.d_mixed, seg_row, seg_col, bits, last
            )
        elif name == DO_TOK:
            terms = []
            for d_qk, d_v, weights in (
                (v.dqk[0], v.dv_own, v.b),
                (v.dqk[1], v.dv_oth, v.o),
            ):
                terms += [(d_qk, 0, weights[0]), (d_qk, 1, weights[1]), (d_v, 0, weights[2])]
            v.d_tokens, v.out_tok = token_grad(v.d_pre1, terms, bits, last)
        elif name in OUTERS:
            chunk = OUTERS.index(name)
            part = chunk % 2
            if chunk in (R0, R1):
                acts = (v.act_s_own, v.act_s_oth)
                made = outer([(acts, (v.d_down,) * 2, 0, dim)], bits, last, half * part, half)
            elif chunk in (E0, E1):
                d_ups = (v.d_up_own, v.d_up_oth)
                made = outer([((v.low_s,) * 2, d_ups, part, half)], bits, last)
            elif chunk == QK:
                made = outer([((x, x), v.dqk, 0, 2 * width)], bits, last)
            else:
                mixed = (v.mixed_own[0], v.mixed_oth)
                made = outer(
                    [
                        ((x, x), (v.dv_own, v.dv_oth), 0, width),
                        ((v.d_attn,) * 2, mixed, 0, width),
                    ],
                    bits,
                    last,
                )
            steps[chunk] = reduce_chunk(made, PATHS[chunk])
        elif name >= FETCH_STEP:
            k = name - FETCH_STEP
            if k not in fetching:
                fetching[k] = (
                    fetch_direct(6, lambda: pack_tile(t_r, (), (C,), bits, last))
                    if k == 6
                    else start_fetch(k)
                )
            next(fetching[k])
        else:
            chunk = name - CHUNK_STEP
            if chunk == SUMS and chunk not in steps:
                steps[chunk] = small_sums()
            pieces = next(steps[chunk])
            if pieces is None:
                return
            if chunk == SUMS:
                outs.sums = pieces
                return

            def rows_of(k, b):
                place = b[C] if k == 0 else 1 - b[C]
                return pl.ds(pl.multiple_of(place * tall, 8), tall)

            everything = (0, slice(None), slice(None))
            if chunk in (R0, R1):
                base = (chunk % 2) * dim

                def target(k):
                    def at(b):
                        place = b[C] if k == 0 else 1 - b[C]
                        return (pl.ds(pl.multiple_of(base + place * tall, 8), tall), slice(None))

                    return at

                cuts = [(k, everything, 0, target(k)) for k in range(2)]
                (outs.reduce,) = finish(
                    pieces, cuts, [shape((hidden, dim))], bits, last, outs.reduce
                )
            elif chunk in (E0, E1):
                left = (chunk % 2) * half
                cuts = [
                    (k, everything, 0, lambda b, k=k: (rows_of(k, b), pl.ds(left, half)))
                    for k in range(2)
                ]
                (outs.expand,) = finish(
                    pieces, cuts, [shape((dim, hidden))], bits, last, outs.expand
                )
            else:
                cuts = []
                if chunk == VO:
                    pieces = [*pieces]
                    for k in range(2):
                        pieces.append(flip(pieces[k][:, :, width:], bits, last))
                        cuts.append(
                            (2 + k, (slice(None), slice(None)), 1, lambda b, k=k: (slice(None), rows_of(k, b)))
                        )
                for j in range(1 if chunk == VO else 2):
                    source = (0, slice(None), pl.ds(j * width, width))
                    cuts += [
                        (k, source, j, lambda b, k=k: (rows_of(k, b), slice(None))) for k in range(2)
                    ]
                dims = [(dim, width), (width, dim) if chunk == VO else (dim, width)]
                pair = finish(pieces, cuts, [shape(d) for d in dims], bits, last)
                if chunk == VO:
                    outs.value, outs.output = pair
                else:
                    outs.query, outs.key = pair

    for name in ORDER:
        do(name)
    small = outs.sums
    n_qkv, n_up = 3 * width, hidden
    out_heads = small[0, :n_qkv].reshape(3, width)
    out_hidden = small[0, n_qkv : n_qkv + n_up]
    first, second = (small[:3, n_qkv + n_up + k * dim :][:, :dim] for k in range(2))
    out_model = jnp.stack([first[2], second[2], first[0], first[1], second[0], second[1]])
    return (
        outs.low,
        outs.tok,
        outs.query,
        outs.key,
        outs.value,
        outs.output,
        outs.expand,
        outs.reduce,
        out_heads,
        out_model,
        out_hidden,
    )


def solution(mesh):
    cols = P(None, "narrow")
    rows = P("narrow", None)
    net = (cols, cols, cols, rows, cols, rows, cols, P(), P("narrow"))
    data = P(None, "wide", None)
    return jax.shard_map(
        functools.partial(on_device, mesh.shape["wide"]),
        mesh=mesh,
        in_specs=(data, P(None, "wide")) + net + net,
        out_specs=(data, data) + net,
        check_vma=False,
    )
```

```python
import functools
import types

import jax
import jax.numpy as jnp
from jax import lax
from jax.experimental import pallas as pl
from jax.experimental.pallas import tpu as pltpu
from jax.sharding import PartitionSpec as P

HEAD = 64
REGION = 256

norm_eps = 1e-06
score_weight = 0.05
big_negative = -1e30
f32 = jnp.float32
bf16 = jnp.bfloat16


def dot_nn(left, right):
    return jnp.dot(left, right, preferred_element_type=f32)


def dot_tn(left, right):
    return lax.dot_general(left, right, (((0,), (0,)), ((), ())), preferred_element_type=f32)


def dot_nt(left, right):
    return lax.dot_general(left, right, (((1,), (1,)), ((), ())), preferred_element_type=f32)


MIB = 2**20
STRIP = 384
C, Y, ZL, ZH, SIDE = range(5)


def shape(dims, dtype=f32):
    return jax.ShapeDtypeStruct(dims, dtype)


def vmem(dims, dtype=f32):
    return pltpu.VMEM(dims, dtype)


def hbm(dims, dtype=f32):
    return pltpu.HBM(dims, dtype)


TOKEN = (8, 128)


def invoke(kernel, name, bits, arrays, specs, outs, out_specs, dep, limit, grid, scratch=(), into=None):
    single = not isinstance(outs, (list, tuple))
    outs = [outs] if single else list(outs)
    out_specs = [out_specs] if single else list(out_specs)
    count = len(arrays)
    after = [in_hbm(token) for token in dep] + ([] if into is None else [in_hbm(into)])
    first = count + len(after)
    end = first + len(outs)

    def body(bits_ref, *refs):
        kernel(bits_ref, refs[:count], refs[first:end] + refs[end + 1 :])

    anywhere = pl.BlockSpec(memory_space=pl.ANY)
    in_specs = list(specs) + [anywhere] * len(after)
    form = dict(
        in_specs=in_specs, out_specs=out_specs + [anywhere], scratch_shapes=scratch
    )
    if grid is None:
        form["in_specs"] = [pl.BlockSpec(memory_space=pltpu.SMEM)] + in_specs
    else:
        form = dict(
            grid_spec=pltpu.PrefetchScalarGridSpec(num_scalar_prefetch=1, grid=grid, **form)
        )
    *results, token = pl.pallas_call(
        body,
        out_shape=outs + [pltpu.HBM(TOKEN, f32)],
        input_output_aliases={} if into is None else {first: 0},
        compiler_params=pltpu.CompilerParams(vmem_limit_bytes=limit * MIB),
        cost_estimate=pl.CostEstimate(flops=0, bytes_accessed=0, transcendentals=0),
        name=name,
        **form,
    )(bits, *arrays, *after)
    dep[:] = [token]
    return results[0] if single else results


def call(kernel, name, bits, arrays, specs, outs, out_specs, grid, dep, limit=20, scratch=(), into=None):
    return invoke(
        kernel, name, bits, arrays, specs, outs, out_specs, dep, limit, grid, scratch, into
    )


def whole_call(kernel, name, bits, arrays, outs, dep, limit=16, hold=True):
    if hold:
        arrays = [pin(a) for a in arrays]
    count = len(arrays)
    return invoke(
        kernel, name, bits, arrays, [IN_VMEM] * count, outs, [IN_VMEM] * len(outs), dep, limit, None
    )


def pin(array):
    return pltpu.with_memory_space_constraint(array, pltpu.VMEM)


def in_hbm(array):
    return pltpu.with_memory_space_constraint(array, pltpu.HBM)


IN_VMEM = pl.BlockSpec(memory_space=pltpu.VMEM)


def place_of(bits_ref, names):
    index = 0
    for name in names:
        index = index * 2 + bits_ref[name]
    return index


def fixed(dims):
    return pl.BlockSpec(dims, lambda *a: (0,) * len(dims))


def normalize(values):
    centred = values - jnp.mean(values, axis=-1, keepdims=True)
    spread = jnp.mean(centred * centred, axis=-1, keepdims=True)
    scale = lax.rsqrt(spread + norm_eps)
    return centred * scale, scale


def norm_back(grad, unit, scale, gain):
    inner = grad * (1.0 + gain)
    return scale * (
        inner
        - jnp.mean(inner, axis=-1, keepdims=True)
        - unit * jnp.mean(inner * unit, axis=-1, keepdims=True)
    )


def cdf_of(up):
    return 0.5 + 0.5 * lax.erf(up * 0.5**0.5)


def sign_of(wide, axis):
    alpha = jnp.mean(jnp.abs(wide), axis=axis, keepdims=True)
    return (jnp.where(wide > 0, alpha, jnp.where(wide < 0, -alpha, 0.0))).astype(bf16)


def binarize(weight, axis, bits, dep):
    def kernel(bits_ref, ins, outs):
        outs[0][...] = sign_of(ins[0][...].astype(f32), axis)

    rows, columns = weight.shape
    if axis == 0:
        spec = pl.BlockSpec((rows, STRIP), lambda i, b: (0, i))
        steps = columns // STRIP
    else:
        spec = pl.BlockSpec((STRIP, columns), lambda i, b: (i, 0))
        steps = rows // STRIP
    return call(
        kernel,
        "binarize",
        bits,
        [weight],
        [spec],
        hbm(weight.shape, bf16),
        spec,
        (steps,),
        dep,
    )


def binarize_pack(weights, axes, names, bits, dep):
    parts = 2 ** len(names)

    def kernel(bits_ref, ins, outs):
        part = place_of(bits_ref, names)
        at = 0
        for ref, axis, out in zip(ins, axes, outs):
            result = sign_of(ref[...].astype(f32), axis)
            out[...] = result
            rows, columns = ref.shape[0] // parts, ref.shape[1]
            mine = out[pl.ds(part * rows, rows), :].astype(f32)
            for left in range(0, columns, STRIP):
                outs[-1][at : at + rows, :] = mine[:, left : left + STRIP]
                at += rows

    total = sum(w.size for w in weights) // parts // STRIP
    specs = [fixed(w.shape) for w in weights]
    return call(
        kernel,
        "binarize_pack",
        bits,
        [in_hbm(w) for w in weights],
        specs,
        [hbm(w.shape, bf16) for w in weights] + [vmem((total, STRIP))],
        specs + [IN_VMEM],
        (1,),
        dep,
    )


def pack(weights, names, bits, dep):
    parts = 2 ** len(names)

    def kernel(bits_ref, ins, outs):
        at = 0
        for ref in ins:
            rows, columns = ref.shape
            for left in range(0, columns, STRIP):
                outs[0][at : at + rows, :] = ref[:, left : left + STRIP].astype(f32)
                at += rows

    specs = [
        pl.BlockSpec((w.shape[0] // parts, w.shape[1]), lambda i, b: (place_of(b, names), 0))
        for w in weights
    ]
    total = sum(w.size for w in weights) // parts // STRIP
    return call(
        kernel,
        "pack",
        bits,
        [in_hbm(w) for w in weights],
        specs,
        [vmem((total, STRIP))],
        [IN_VMEM],
        (1,),
        dep,
    )[0]


def pack_tile(weight, row_names, column_names, bits, dep):
    def kernel(bits_ref, ins, outs):
        at = pl.multiple_of(pl.program_id(0) * tall, 8)
        outs[0][pl.ds(at, tall), :] = ins[0][...].astype(f32)

    dims = (weight.shape[0] >> len(row_names), weight.shape[1] >> len(column_names))
    steps = max(1, dims[0] // 384)
    tall = dims[0] // steps
    return call(
        kernel,
        "pack_tile",
        bits,
        [weight],
        [
            pl.BlockSpec(
                (tall, dims[1]),
                lambda i, b: (place_of(b, row_names) * steps + i, place_of(b, column_names)),
            )
        ],
        [vmem(dims)],
        [IN_VMEM],
        (steps,),
        dep,
    )[0]


def touch(array, bits, dep):
    count = len(dep)

    def body(bits_ref, *refs):
        pass

    anywhere = pl.BlockSpec(memory_space=pl.ANY)
    result, token = pl.pallas_call(
        body,
        in_specs=[pl.BlockSpec(memory_space=pltpu.SMEM)] + [anywhere] * (1 + count),
        out_specs=[anywhere] * 2,
        out_shape=[shape(array.shape, array.dtype), pltpu.HBM(TOKEN, f32)],
        input_output_aliases={1: 0},
        compiler_params=pltpu.CompilerParams(vmem_limit_bytes=MIB),
        cost_estimate=pl.CostEstimate(flops=0, bytes_accessed=0, transcendentals=0),
        name="touch",
    )(bits, array, *map(in_hbm, dep))
    dep[:] = [token]
    return result


def join(first, second, bits, dep):
    rows, columns = first.shape

    def kernel(bits_ref, ins, outs):
        for k in range(2):
            outs[0][k * rows : (k + 1) * rows, :] = ins[k][...]

    return whole_call(kernel, "join", bits, [first, second], [vmem((2 * rows, columns))], dep)[0]


def half_masks():
    lane = lax.broadcasted_iota(jnp.int32, (1, 2 * HEAD), 1)
    low = jnp.where(lane < HEAD, 1.0, 0.0).astype(bf16)
    return (low, (1.0 - low.astype(f32)).astype(bf16))


def region_masks(row_ref, col_ref):
    across = row_ref[0]
    down = col_ref[...]
    same = down == across
    live = down >= 0
    size = down.shape[0]
    diagonal = lax.broadcasted_iota(jnp.int32, (size, size), 0) == lax.broadcasted_iota(
        jnp.int32, (size, size), 1
    )
    pairs = same & live
    return pairs, pairs | diagonal


def probabilities(scores, allowed):
    masked = jnp.where(allowed, scores, big_negative)
    top = jnp.max(masked, axis=-1, keepdims=True)
    expo = jnp.exp(masked - top)
    total = jnp.sum(expo, axis=-1, keepdims=True)
    return expo * (1.0 / total)


def attention(parts, allowed, masks, scale, write):
    width = parts[0].shape[1]
    for at in range(0, width, 2 * HEAD):
        query, keys, values = (part[:, at : at + 2 * HEAD] for part in parts)
        probs = [
            probabilities(dot_nt(query * mask, keys) * scale, allowed).astype(bf16) for mask in masks
        ]
        stacked = jnp.concatenate([values * mask for mask in masks], axis=0)
        write(at, dot_nn(jnp.concatenate(probs, axis=1), stacked).astype(bf16))


def attend_own(x, weights, biases, seg_row, seg_col, bits, dep):
    rows, dim = x.shape
    width = weights[0].shape[1]

    def kernel(bits_ref, ins, outs):
        x_ref, bias_ref, row_ref, col_ref = ins[:4]
        tokens = x_ref[...]
        pairs, allowed = region_masks(row_ref, col_ref)
        masks = half_masks()
        for net in range(2):
            parts = []
            for k in range(3):
                row = 3 * net + k
                part = dot_nn(tokens, ins[4 + row][...]) + bias_ref[row : row + 1, :]
                parts.append(part.astype(bf16))
                if row < 5:
                    outs[0][:, row * width : (row + 1) * width] = parts[k]

            def write(at, mixed, net=net):
                outs[1 + net][:, at : at + 2 * HEAD] = mixed

            attention(parts, allowed, masks, HEAD ** (-0.5), write)

    def block(columns):
        return pl.BlockSpec((REGION, columns), lambda i, b: (i, 0))

    return call(
        kernel,
        "attend_own",
        bits,
        [x, biases, seg_row, seg_col, *weights],
        [
            block(dim),
            fixed(biases.shape),
            pl.BlockSpec((1, 1, REGION), lambda i, b: (i, 0, 0)),
            block(1),
        ]
        + [fixed(w.shape) for w in weights],
        [shape((rows, 5 * width), bf16), shape((rows, width), bf16), shape((rows, width), bf16)],
        [block(5 * width), block(width), block(width)],
        (rows // REGION,),
        dep,
    )


def attend_other(
    x, pieces, names, biases, seg_row, seg_col, mixed, output, model, student, bits, dep
):
    rows, dim = x.shape
    width = mixed.shape[1]
    parts = 2 ** len(names)
    half_parts = parts // 2
    tall = dim // parts
    short = width // parts
    per_part = 3 * tall + 2 * short
    first_row = 0 if student else 3
    kept = 3 if student else 2

    def kernel(bits_ref, ins, outs):
        x_ref, bias_ref, row_ref, col_ref, mine_ref, theirs_ref, mixed_ref, out_ref, model_ref = ins
        qkv_ref, low_ref, first_ref = outs[:3]
        weight_refs = outs[5:9] if student else outs[3:7]
        part = place_of(bits_ref, names)

        @pl.when(pl.program_id(0) == 0)
        def _():
            for k in range(parts):
                ref = (mine_ref, theirs_ref)[k // half_parts]
                base = (k % half_parts) * per_part
                where = jnp.bitwise_xor(part, k)
                for m in range(3):
                    weight_refs[m][pl.ds(pl.multiple_of(where * tall, 16), tall), :] = ref[
                        base + m * tall : base + (m + 1) * tall, :
                    ].astype(bf16)
                for m in range(2):
                    at = base + 3 * tall + m * short
                    weight_refs[3][
                        pl.ds(pl.multiple_of(where * short, 16), short), m * STRIP : (m + 1) * STRIP
                    ] = ref[at : at + short, :].astype(bf16)

        tokens = x_ref[...]
        pairs, allowed = region_masks(row_ref, col_ref)
        masks = half_masks()
        parts_qkv = []
        for k in range(3):
            row = first_row + k
            part_k = dot_nn(tokens, weight_refs[k][...]) + bias_ref[row : row + 1, :]
            parts_qkv.append(part_k.astype(bf16))
            if k < kept:
                qkv_ref[:, k * width : (k + 1) * width] = parts_qkv[k]
        tiles = []
        attention(parts_qkv, allowed, masks, HEAD ** (-0.5), lambda at, tile: tiles.append(tile))
        mine = jnp.concatenate(tiles, axis=1)
        pre = (
            tokens.astype(f32)
            + (dot_nn(mixed_ref[...], out_ref[...]) + dot_nn(mine, weight_refs[3][...]))
            + model_ref[0:1, :]
        )
        unit, scale = normalize(pre)
        first = unit * (1.0 + model_ref[2:3, :]) + model_ref[3:4, :]
        low_ref[...] = first.astype(bf16)
        first_ref[...] = first
        if student:
            outs[3][...] = mine
            outs[4][...] = pre

    def block(columns):
        return pl.BlockSpec((REGION, columns), lambda i, b: (i, 0))

    weights = [shape((dim, width), bf16)] * 3 + [shape((width, dim), bf16)]
    outs = [shape((rows, kept * width), bf16), shape((rows, dim), bf16), shape((rows, dim))]
    out_specs = [block(kept * width), block(dim), block(dim)]
    if student:
        outs += [shape((rows, width), bf16), hbm((rows, dim))]
        outs += [hbm(w.shape, bf16) for w in weights]
        out_specs += [block(width), block(dim)] + [fixed(w.shape) for w in weights]
    return call(
        kernel,
        "attend_other",
        bits,
        [x, biases, seg_row, seg_col, *map(pin, pieces), mixed, output, model],
        [
            block(dim),
            fixed(biases.shape),
            pl.BlockSpec((1, 1, REGION), lambda i, b: (i, 0, 0)),
            block(1),
            IN_VMEM,
            IN_VMEM,
            block(width),
            fixed(output.shape),
            fixed(model.shape),
        ],
        outs,
        out_specs,
        (rows // REGION,),
        dep,
        limit=24,
        scratch=[] if student else [pltpu.VMEM(w.shape, bf16) for w in weights],
    )


def activate(up, outs, student):
    cdf = cdf_of(up)
    outs[0][...] = (up * cdf).astype(bf16)
    if student:
        bell = jnp.exp(-0.5 * up * up) * (2.0 * jnp.pi) ** -0.5
        outs[1][...] = (cdf + up * bell).astype(bf16)


def up_own(low, weight, biases, first_row, student, bits, dep):
    tokens, dim = low.shape
    hidden = weight.shape[1]

    def kernel(bits_ref, ins, outs):
        j = pl.program_id(0)
        up = dot_nn(ins[0][...], ins[1][...]) + ins[2][pl.ds(first_row + j, 1), :]
        activate(up, outs, student)

    count = 2 if student else 1
    return call(
        kernel,
        "up_own",
        bits,
        [low, weight, biases],
        [fixed(low.shape), pl.BlockSpec((dim, STRIP), lambda j, b: (0, j)), fixed(biases.shape)],
        [shape((tokens, hidden), bf16), hbm((tokens, hidden), bf16)][:count],
        [pl.BlockSpec((tokens, STRIP), lambda j, b: (0, j))] * count,
        (hidden // STRIP,),
        dep,
    )


def up_other(low, mine, theirs, names, biases, first_row, student, bits, dep):
    tokens, dim = low.shape
    steps = mine.shape[0] // STRIP
    half = dim // 2

    def kernel(bits_ref, ins, outs):
        low_ref, tile_m, tile_o, bias_ref = ins
        j = jnp.bitwise_xor(pl.program_id(0), place_of(bits_ref, names))
        at = pl.ds(pl.multiple_of(pl.program_id(0) * half, 8), half)
        weight_ref = outs[2] if student else outs[1]
        core = bits_ref[C]
        weight_ref[pl.ds(pl.multiple_of(core * half, 16), half), :] = tile_m[at, :].astype(bf16)
        weight_ref[pl.ds(pl.multiple_of((1 - core) * half, 16), half), :] = tile_o[at, :].astype(bf16)
        up = dot_nn(low_ref[...], weight_ref[...]) + bias_ref[pl.ds(first_row + j, 1), :]
        activate(up, outs, student)

    def column(j, b):
        return (0, jnp.bitwise_xor(j, place_of(b, names)))

    outs = [shape((tokens, steps * STRIP), bf16)]
    out_specs = [pl.BlockSpec((tokens, STRIP), column)]
    if student:
        outs += [hbm((tokens, steps * STRIP), bf16), hbm((dim, steps * STRIP), bf16)]
        out_specs += [out_specs[0], pl.BlockSpec((dim, STRIP), column)]
    return call(
        kernel,
        "up_other",
        bits,
        [low, pin(mine), pin(theirs), biases],
        [fixed(low.shape), IN_VMEM, IN_VMEM, fixed(biases.shape)],
        outs,
        out_specs,
        (steps,),
        dep,
        limit=16,
        scratch=[] if student else [pltpu.VMEM((dim, STRIP), bf16)],
    )


def down_own(acts, weights, firsts, models, bits, dep):
    tokens, hidden = acts[0].shape
    dim = weights[0].shape[1]

    def kernel(bits_ref, ins, outs):
        for net in range(2):
            act, weight, first, model = ins[4 * net : 4 * net + 4]
            outs[net][...] = first[...] + model[1:2, :] + dot_nn(act[...], weight[...])

    def block(columns):
        return pl.BlockSpec((REGION, columns), lambda i, b: (i, 0))

    arrays = []
    specs = []
    for net in range(2):
        arrays += [acts[net], weights[net], firsts[net], models[net]]
        specs += [block(hidden), fixed((hidden, dim)), block(dim), fixed(models[net].shape)]
    return call(
        kernel,
        "down_own",
        bits,
        arrays,
        specs,
        [shape((tokens, dim))] * 2,
        [block(dim)] * 2,
        (tokens // REGION,),
        dep,
        limit=24,
    )


def down_other(acts, student_tiles, teacher_tiles, names, partials, models, seg_col, bits, dep):
    tokens, hidden = acts[0].shape
    dim = partials[0].shape[1]
    half = dim // 2
    steps = hidden // STRIP

    def kernel(bits_ref, ins, outs):
        act_s, act_t, s_mine, s_other, t_mine, t_other, part_s, part_t, model_s, model_t, seg = ins
        out_ref, pre_ref, down_ref, sums_ref, weight_ref, low_ref, teacher_ref = outs
        step = pl.program_id(0)
        first_core = bits_ref[C] == 0

        @pl.when(step == 0)
        def _():
            place = place_of(bits_ref, names)
            for k in range(steps):
                rows = slice(k * STRIP, (k + 1) * STRIP)
                where = pl.ds(pl.multiple_of(jnp.bitwise_xor(place, k) * STRIP, 16), STRIP)
                tile, other = s_mine[rows, :].astype(bf16), s_other[rows, :].astype(bf16)
                weight_ref[where, :half] = jnp.where(first_core, tile, other)
                weight_ref[where, half:] = jnp.where(first_core, other, tile)
                tile, other = t_mine[rows, :].astype(bf16), t_other[rows, :].astype(bf16)
                teacher_ref[rows, :half] = jnp.where(first_core, tile, other)
                teacher_ref[rows, half:] = jnp.where(first_core, other, tile)

        unit_s, scale_s = normalize(part_s[...] + dot_nn(act_s[...], weight_ref[...]))
        unit_t, _ = normalize(part_t[...] + dot_nn(act_t[...], teacher_ref[...]))
        gain = model_s[4:5, :]
        out_s = unit_s * (1.0 + gain) + model_s[5:6, :]
        out_t = unit_t * (1.0 + model_t[4:5, :]) + model_t[5:6, :]
        out_ref[...] = out_s
        low_ref[0] = out_s.astype(bf16)
        grad = jnp.where(seg[...] >= 0, out_s - out_t, 0.0)
        d_pre = norm_back(grad, unit_s, scale_s, gain)
        pre_ref[...] = d_pre
        low = d_pre.astype(bf16)
        down_ref[...] = low
        add_sums(sums_ref, (grad * unit_s, grad, low.astype(f32)), step)

    def block(columns):
        return pl.BlockSpec((REGION, columns), lambda i, b: (i, 0))

    return call(
        kernel,
        "down_other",
        bits,
        [*acts, *map(pin, student_tiles), *map(pin, teacher_tiles), *partials, *models, seg_col],
        [block(hidden)] * 2
        + [IN_VMEM] * 4
        + [block(dim)] * 2
        + [fixed(m.shape) for m in models]
        + [block(1)],
        [
            shape((tokens, dim)),
            shape((tokens, dim)),
            shape((tokens, dim), bf16),
            shape((8, dim)),
            hbm((hidden, dim), bf16),
            hbm((2, tokens, dim), bf16),
        ],
        [
            block(dim),
            block(dim),
            block(dim),
            fixed((8, dim)),
            fixed((hidden, dim)),
            pl.BlockSpec((1, REGION, dim), lambda i, b: (b[SIDE], i, 0)),
        ],
        (tokens // REGION,),
        dep,
        limit=28,
        scratch=[pltpu.VMEM((hidden, dim), bf16)],
    )


def up_back(d_down, weights, slopes, bits, dep):
    tokens, dim = d_down.shape
    hidden = weights[0].shape[0]

    def kernel(bits_ref, ins, outs):
        rows = []
        for half in range(2):
            grad = dot_nt(ins[0][...], ins[1 + half][...])
            low = (grad * ins[3 + half][...].astype(f32)).astype(bf16)
            outs[half][...] = low
            rows.append(jnp.sum(low.astype(f32), axis=0, keepdims=True))
        outs[2][...] = jnp.concatenate(rows + [jnp.zeros((6, STRIP), f32)], axis=0)

    block = pl.BlockSpec((tokens, STRIP), lambda j, b: (0, j))
    return call(
        kernel,
        "up_back",
        bits,
        [d_down, *weights, *slopes],
        [fixed(d_down.shape)] + [pl.BlockSpec((STRIP, dim), lambda j, b: (j, 0))] * 2 + [block] * 2,
        [shape((tokens, hidden), bf16)] * 2 + [shape((8, hidden))],
        [block, block, pl.BlockSpec((8, STRIP), lambda j, b: (0, j))],
        (hidden // STRIP,),
        dep,
    )


def add_sums(ref, arrays, step):
    rows = [jnp.sum(v, axis=0, keepdims=True) for v in arrays]
    rows.append(jnp.zeros((8 - len(rows), rows[0].shape[1]), f32))
    new = jnp.concatenate(rows, axis=0)
    ref[...] = jnp.where(step == 0, new, ref[...] + new)


def first_back(d_ups, weights, d_pre2, pre, model, outputs, bits, dep):
    tokens, hidden = d_ups[0].shape
    dim = d_pre2.shape[1]
    width = outputs[0].shape[0]

    def kernel(bits_ref, ins, outs):
        d_own, d_oth, w_own, w_oth, d_pre2_ref, pre_ref, model_ref, o_own, o_oth = ins
        grad = d_pre2_ref[...] + (dot_nt(d_own[...], w_own[...]) + dot_nt(d_oth[...], w_oth[...]))
        unit, scale = normalize(pre_ref[...])
        d_pre = norm_back(grad, unit, scale, model_ref[2:3, :])
        outs[0][...] = d_pre
        low = d_pre.astype(bf16)
        outs[1][...] = low
        outs[2][...] = dot_nt(low, o_own[...]).astype(bf16)
        outs[3][...] = dot_nt(low, o_oth[...]).astype(bf16)
        add_sums(outs[4], (grad * unit, grad, low.astype(f32)), pl.program_id(0))

    def block(columns):
        return pl.BlockSpec((REGION, columns), lambda i, b: (i, 0))

    return call(
        kernel,
        "first_back",
        bits,
        [*d_ups, *weights, d_pre2, pre, model, *outputs],
        [block(hidden)] * 2
        + [fixed(w.shape) for w in weights]
        + [block(dim)] * 2
        + [fixed(model.shape)]
        + [fixed(o.shape) for o in outputs],
        [
            shape((tokens, dim)),
            shape((tokens, dim), bf16),
            shape((tokens, width), bf16),
            shape((tokens, width), bf16),
            shape((8, dim)),
        ],
        [block(dim), block(dim), block(width), block(width), fixed((8, dim))],
        (tokens // REGION,),
        dep,
        limit=28,
    )


def token_grad(d_pre, terms, bits, dep):
    tokens, dim = d_pre.shape

    def kernel(bits_ref, ins, outs):
        total = ins[0][...]
        for k in range(len(terms)):
            total = total + dot_nt(ins[1 + 2 * k][...], ins[2 + 2 * k][...])
        outs[0][...] = total
        outs[1][0] = total

    arrays = [d_pre]
    specs = [pl.BlockSpec((REGION, dim), lambda i, b: (i, 0))]
    for grad, at, weight in terms:
        arrays += [grad, weight]
        specs += [
            pl.BlockSpec((REGION, weight.shape[1]), lambda i, b, at=at: (i, at)),
            fixed(weight.shape),
        ]
    return call(
        kernel,
        "token_grad",
        bits,
        arrays,
        specs,
        [shape((tokens, dim)), pltpu.HBM((2, tokens, dim), f32)],
        [specs[0], pl.BlockSpec((1, REGION, dim), lambda i, b: (b[SIDE], i, 0))],
        (tokens // REGION,),
        dep,
    )


def attend_back(qkv, grads, seg_row, seg_col, bits, dep):
    rows, columns = qkv[0].shape
    width = columns // 5
    step = 2 * HEAD

    def kernel(bits_ref, ins, outs):
        pairs, allowed = region_masks(ins[5], ins[6])
        weight = jnp.where(pairs, score_weight, 0.0)
        masks = half_masks()
        scale = HEAD ** (-0.5)

        @pl.when(pl.program_id(0) == 0)
        def _():
            outs[4][...] = jnp.zeros_like(outs[4])

        for part in range(2):
            for at in range(0, width, step):
                places = [(0, k) for k in range(5)] if part == 0 else [(1, 0), (1, 1), (1, 2), (2, 0), (2, 1)]
                query, keys, values, query_t, keys_t = (
                    ins[r][:, k * width + at : k * width + at + step] for r, k in places
                )
                grad = ins[3 + part][:, at : at + step]
                probs = []
                slopes = []
                for mask in masks:
                    scores = dot_nt(query * mask, keys) * scale
                    prob = probabilities(scores, allowed)
                    gap = scores - dot_nt(query_t * mask, keys_t) * scale
                    d_prob = dot_nt(grad * mask, values)
                    mean = jnp.sum(prob * d_prob, axis=-1, keepdims=True)
                    slope = prob * (d_prob - mean) + weight * gap
                    probs.append(prob.astype(bf16))
                    slopes.append(slope.astype(bf16))

                def both(array):
                    return jnp.concatenate([array * mask for mask in masks], axis=0)

                d_query = dot_nn(jnp.concatenate(slopes, axis=1), both(keys)) * scale
                d_keys = dot_tn(jnp.concatenate(slopes, axis=0), both(query)) * scale
                d_values = dot_tn(jnp.concatenate(probs, axis=0), both(grad))
                for k, result in enumerate((d_query, d_keys, d_values)):
                    low = result.astype(bf16)
                    if k < 2:
                        outs[part][:, k * width + at : k * width + at + step] = low
                    else:
                        outs[2 + part][:, at : at + step] = low
                    outs[4][part : part + 1, k * width + at : k * width + at + step] += jnp.sum(
                        low.astype(f32), axis=0, keepdims=True
                    )

    def block(columns):
        return pl.BlockSpec((REGION, columns), lambda i, b: (i, 0))

    return call(
        kernel,
        "attend_back",
        bits,
        [*qkv, *grads, seg_row, seg_col],
        [
            block(columns),
            block(3 * width),
            block(2 * width),
            block(width),
            block(width),
            pl.BlockSpec((1, 1, REGION), lambda i, b: (i, 0, 0)),
            block(1),
        ],
        [shape((rows, 2 * width), bf16)] * 2
        + [shape((rows, width), bf16)] * 2
        + [shape((8, 3 * width))],
        [block(2 * width)] * 2 + [block(width)] * 2 + [fixed((8, 3 * width))],
        (rows // REGION,),
        dep,
    )


def outer(groups, bits, dep, start=0, size=None, block=384):
    size = size or groups[0][0][0].shape[1]
    tall = size // 2
    steps = tall // block
    tokens = groups[0][0][0].shape[0]
    arrays = []
    specs = []
    for lhs, rhs, at, columns in groups:
        for half in range(2):

            def left(p, h, i, b, half=half, lhs=lhs):
                core = jnp.where(p == 0, 1 - b[C], b[C])
                where = start // block + core * steps + i
                return (0, where if lhs[0] is lhs[1] else jnp.where(h == half, where, start // block))

            arrays += [lhs[half], rhs[half]]
            specs += [
                pl.BlockSpec((tokens, block), left),
                pl.BlockSpec((tokens, columns), lambda p, h, i, b, at=at: (0, at)),
            ]
    wide = sum(g[3] for g in groups)

    def kernel(bits_ref, ins, outs):
        for phase in range(2):
            for half in range(2):

                @pl.when((pl.program_id(0) == phase) & (pl.program_id(1) == half))
                def _(phase=phase, half=half):
                    at = 0
                    row = pl.multiple_of(pl.program_id(2) * block, 8)
                    for k, group in enumerate(groups):
                        lhs, rhs = ins[4 * k + 2 * half], ins[4 * k + 2 * half + 1]
                        outs[phase][half, pl.ds(row, block), at : at + group[3]] = dot_tn(
                            lhs[...], rhs[...]
                        )
                        at += group[3]

    out = vmem((2, tall, wide))
    return call(
        kernel, "outer", bits, arrays, specs, [out, out], [IN_VMEM, IN_VMEM], (2, 2, steps), dep, limit=16
    )


def split(first, second, name, bits, dep, limit=16):
    halves, rows, columns = first.shape
    out = vmem((1, rows, columns)) if name == "x" else vmem((halves, rows // 2, columns))

    def kernel(bits_ref, ins, outs):
        for k in range(2):
            if name == "x":
                where = (pl.ds(1 - k, 1), slice(None))
            else:
                bit = bits_ref[name]
                start = (1 - bit if k == 0 else bit) * (rows // 2)
                where = (slice(None), pl.ds(pl.multiple_of(start, 8), rows // 2))
            outs[k][...] = ins[0][where] + ins[1][where]

    return whole_call(kernel, "split", bits, [first, second], [out, out], dep, limit)


def add(first, second, bits, dep):
    def kernel(bits_ref, ins, outs):
        outs[0][...] = ins[0][...] + ins[1][...]

    return whole_call(kernel, "add", bits, [first, second], [vmem(first.shape)], dep)[0]


def merge(mine, theirs, name, bits, dep):
    one, rows, columns = mine.shape

    def kernel(bits_ref, ins, outs):
        bit = bits_ref[name]
        for k in range(2):
            start = (bit if k == 0 else 1 - bit) * rows
            outs[0][:, pl.ds(pl.multiple_of(start, 8), rows)] = ins[k][...]

    return whole_call(kernel, "merge", bits, [mine, theirs], [vmem((1, 2 * rows, columns))], dep)[0]


def finish(pieces, cuts, outs, bits, dep, into=None):
    def kernel(bits_ref, ins, refs):
        results, sems = refs[:-1], refs[-1]
        copies = []
        for k, (piece, source, out, target) in enumerate(cuts):
            copy = pltpu.make_async_copy(
                ins[piece].at[source], results[out].at[target(bits_ref)], sems.at[k]
            )
            copy.start()
            copies.append(copy)
        for copy in copies:
            copy.wait()

    return invoke(
        kernel,
        "finish",
        bits,
        [*map(pin, pieces)],
        [IN_VMEM] * len(pieces),
        [pltpu.HBM(o.shape, o.dtype) for o in outs],
        [pl.BlockSpec(memory_space=pl.ANY)] * len(outs),
        dep,
        8,
        None,
        [pltpu.SemaphoreType.DMA((len(cuts),))],
        into,
    )


def flip(array, bits, dep):
    def kernel(bits_ref, ins, outs):
        outs[0][...] = ins[0][0].T

    one, rows, columns = array.shape
    return whole_call(kernel, "flip", bits, [array], [vmem((columns, rows))], dep)[0]


def put_rows(array, bits, dep, into):
    two, rows, dim = into.shape
    tall = rows // 4

    def kernel(bits_ref, ins, outs):
        at = pl.ds(pl.multiple_of(pl.program_id(0) * tall, 8), tall)
        outs[-1][0] = ins[0][at, :].astype(into.dtype)

    return call(
        kernel,
        "place",
        bits,
        [pin(array)],
        [IN_VMEM],
        [pltpu.HBM(into.shape, into.dtype)],
        [pl.BlockSpec((1, tall, dim), lambda i, b: (1 - b[SIDE], i, 0))],
        (4,),
        dep,
        into=into,
    )[0]


def collect(sums, other, bits, dep):
    wide = sum(s.shape[1] for s in sums)

    def kernel(bits_ref, ins, outs):
        at = 0
        for k, ref in enumerate(ins):
            columns = ref.shape[1]
            if other and k < 2:
                both = jnp.concatenate([ref[1:2, :], ref[0:1, :], ref[2:, :]], axis=0)
            else:
                both = ref[...]
            outs[0][:, at : at + columns] = both
            at += columns

    return whole_call(kernel, "collect", bits, sums, [vmem((8, wide))], dep)[0]


R0, R1, E0, E1, QK, VO, SUMS = range(7)
(
    DO_B0,
    DO_B1,
    DO_BIN_A,
    DO_BIN_E,
    DO_BIN_R,
    DO_ATT_O,
    DO_KBT,
    DO_KBS,
    DO_UP_OT,
    DO_UP_OS,
    DO_UP_XT,
    DO_UP_XS,
    DO_DN_O,
    DO_KD,
    DO_S,
    DO_TT,
    DO_SF,
    DO_TF,
    DO_DU,
    DO_DH1,
    DO_ATT,
    DO_TOK,
    DO_O_R0,
    DO_O_R1,
    DO_O_E0,
    DO_O_E1,
    DO_O_QK,
    DO_O_VO,
) = range(28)
OUTERS = (DO_O_R0, DO_O_R1, DO_O_E0, DO_O_E1, DO_O_QK, DO_O_VO)
CHUNK_STEP, FETCH_STEP = 50, 60
PATHS = {
    R0: ("x", Y, ZL, ZH),
    R1: ("x", Y, ZL, ZH),
    E0: (Y, ZL, "x", ZH),
    E1: (ZL, "x", ZH, Y),
    QK: ("x", Y, ZL, ZH),
    VO: (ZL, Y, "x", ZH),
}
FETCH = ((Y,), (Y, ZL), (Y, ZL), (Y, ZL), (ZL, Y))
ORDER = (
    FETCH_STEP + 3, DO_B0, DO_BIN_A, DO_B1, DO_BIN_E, DO_BIN_R, FETCH_STEP + 2, FETCH_STEP + 3,
    FETCH_STEP + 5, FETCH_STEP + 6, FETCH_STEP + 1, FETCH_STEP + 2, FETCH_STEP + 3, DO_ATT_O,
    FETCH_STEP + 2, FETCH_STEP + 1, FETCH_STEP + 3, FETCH_STEP + 4, FETCH_STEP + 5,
    FETCH_STEP + 4, FETCH_STEP + 1, FETCH_STEP + 2, FETCH_STEP + 3, FETCH_STEP + 1, DO_KBT,
    FETCH_STEP + 4, FETCH_STEP + 2, FETCH_STEP + 5, DO_KBS, DO_UP_OT, DO_UP_XT, DO_UP_OS,
    DO_DN_O, FETCH_STEP + 4, FETCH_STEP + 5, FETCH_STEP + 6, FETCH_STEP + 4, DO_UP_XS,
    FETCH_STEP + 5, FETCH_STEP + 6, DO_KD, DO_DU, DO_O_R0, DO_O_E1, CHUNK_STEP + R0,
    CHUNK_STEP + E1, DO_O_E0, CHUNK_STEP + E0, DO_O_R1, CHUNK_STEP + R1, CHUNK_STEP + E1,
    CHUNK_STEP + R0, DO_DH1, DO_ATT, DO_O_VO, CHUNK_STEP + VO, DO_O_QK, CHUNK_STEP + R0,
    CHUNK_STEP + E1, CHUNK_STEP + QK, CHUNK_STEP + VO, CHUNK_STEP + R1, DO_TOK,
    CHUNK_STEP + QK, CHUNK_STEP + E0, CHUNK_STEP + R0, CHUNK_STEP + E1, CHUNK_STEP + E1,
    CHUNK_STEP + R0, CHUNK_STEP + VO, CHUNK_STEP + E0, CHUNK_STEP + R0, CHUNK_STEP + E1,
    CHUNK_STEP + R1, DO_S, CHUNK_STEP + E0, CHUNK_STEP + QK, DO_TT, CHUNK_STEP + E1,
    CHUNK_STEP + VO, CHUNK_STEP + E0, CHUNK_STEP + SUMS, CHUNK_STEP + VO, CHUNK_STEP + R0,
    CHUNK_STEP + SUMS, CHUNK_STEP + E0, CHUNK_STEP + R1, CHUNK_STEP + SUMS, CHUNK_STEP + E1,
    CHUNK_STEP + QK, CHUNK_STEP + R1, CHUNK_STEP + SUMS, CHUNK_STEP + VO, CHUNK_STEP + R0,
    CHUNK_STEP + QK, CHUNK_STEP + R1, CHUNK_STEP + E0, CHUNK_STEP + VO, CHUNK_STEP + R1,
    CHUNK_STEP + QK, CHUNK_STEP + SUMS, DO_TF, CHUNK_STEP + QK, CHUNK_STEP + E0,
    CHUNK_STEP + R1, DO_SF, CHUNK_STEP + E1, CHUNK_STEP + E0, CHUNK_STEP + R0,
    CHUNK_STEP + SUMS, CHUNK_STEP + R1, CHUNK_STEP + QK, CHUNK_STEP + VO, CHUNK_STEP + QK,
    CHUNK_STEP + VO,
)


def on_device(n_wide, tokens, segments, *params):
    (w_q, w_k, w_v, w_o, w_e, w_r, heads_s, model_s, hidden_s) = params[:9]
    (t_q, t_k, t_v, t_o, t_e, t_r, heads_t, model_t, hidden_t) = params[9:]
    n_bits = n_wide.bit_length() - 1
    side = lax.axis_index("narrow")
    place = lax.axis_index("wide")
    bits = jnp.stack([(place >> b) & 1 for b in range(4)] + [side]).astype(jnp.int32)
    dim, width = w_q.shape
    hidden = w_e.shape[1]

    def swap(array, bit):
        if bit == "x":
            return lax.ppermute(array, "narrow", [(0, 1), (1, 0)])
        return lax.ppermute(array, "wide", [(i, i ^ (1 << bit)) for i in range(n_wide)])

    x = lax.dynamic_index_in_dim(tokens, side, 0, keepdims=False)
    segment = lax.dynamic_index_in_dim(segments, side, 0, keepdims=False)
    rows = x.shape[0]
    seg_row = segment.reshape(rows // REGION, 1, REGION)
    seg_col = segment.reshape(rows, 1)
    biases = jnp.concatenate(
        [heads_s, heads_t, hidden_s.reshape(-1, width), hidden_t.reshape(-1, width)]
    )
    blocks = hidden // width
    models = (model_s, model_t)
    half = hidden // 2

    v = types.SimpleNamespace()
    fetched = {}
    last = []

    def fetch(key, made, path):
        held = swap(made(), "x")
        yield
        held = touch(held, bits, last)
        for name in path:
            got = swap(held, name)
            yield
            held = join(held, got, bits, last)
        got = swap(held, C)
        yield
        fetched[key] = (held, touch(got, bits, last))
        yield

    def fetch_direct(key, made):
        zero = swap(made(), "x")
        yield
        zero = touch(zero, bits, last)
        got = swap(zero, C)
        yield
        fetched[key] = (zero, touch(got, bits, last))
        yield

    def reduce_chunk(made, path):
        send, keep = made
        got = swap(touch(send, bits, last), C)
        yield
        for name in path[:-1]:
            send, keep = split(keep, got, name, bits, last)
            got = swap(send, name)
            yield
        block = add(keep, got, bits, last)
        got = swap(block, path[-1])
        yield
        for extra in range(4, n_bits):
            block = block + got
            got = swap(block, extra)
        block = add(block, got, bits, last)
        back = [name for name in reversed(path[:-1]) if name != "x"] + [C]
        for name in back[:-1]:
            got = swap(block, name)
            yield
            block = merge(block, got, name, bits, last)
        got = swap(block, C)
        yield
        yield (block, got)

    def small_sums():
        sums = [v.sums_qkv, v.sums_up, v.sums1, v.sums2]
        total = collect(sums, False, bits, last)
        got = swap(collect(sums, True, bits, last), "x")
        yield
        for b in range(4):
            total = add(total, got, bits, last)
            got = swap(total, b)
            yield
        total = add(total, got, bits, last)
        for b in range(4, n_bits):
            total = total + swap(total, b)
        yield total

    tall = dim // 2
    steps = {}
    fetching = {}
    outs = types.SimpleNamespace(reduce=None, expand=None)

    def names_of(k):
        return (C, *reversed(FETCH[k - 1]))

    def start_fetch(k):
        names = names_of(k)
        makers = {
            1: lambda: pack([t_q, t_k, t_v, t_o], names, bits, last),
            2: lambda: touch(v.b_pack, bits, last),
            3: lambda: pack_tile(in_hbm(t_e), (C,), names[1:], bits, last),
            4: lambda: pack_tile(v.b_e, (C,), names[1:], bits, last),
            5: lambda: pack_tile(v.b_r, names[1:], (C,), bits, last),
        }
        return fetch(k, makers[k], FETCH[k - 1])

    def do(name):
        if name == DO_B0:
            v.biases_oth = swap(touch(biases, bits, last), "x")
        elif name == DO_B1:
            v.biases_oth = touch(v.biases_oth, bits, last)
        elif name == DO_BIN_A:
            *v.b, v.b_pack = binarize_pack(
                [w_q, w_k, w_v, w_o], (0, 0, 0, 1), names_of(2), bits, last
            )
        elif name == DO_BIN_E:
            v.b_e = binarize(w_e, 0, bits, last)
        elif name == DO_BIN_R:
            v.b_r = binarize(w_r, 1, bits, last)
        elif name == DO_ATT_O:
            b = v.b
            v.qkv_own, *v.mixed_own = attend_own(
                x,
                (b[0], b[1], b[2], in_hbm(t_q), in_hbm(t_k), in_hbm(t_v)),
                biases,
                seg_row,
                seg_col,
                bits,
                last,
            )
        elif name == DO_KBT:
            v.qk_t, v.low_t, v.first_t = attend_other(
                x,
                fetched[1],
                names_of(1),
                v.biases_oth,
                seg_row,
                seg_col,
                v.mixed_own[1],
                t_o,
                model_t,
                False,
                bits,
                last,
            )
        elif name == DO_KBS:
            v.qkv_oth, v.low_s, v.first_s, v.mixed_oth, v.pre_s, *v.o = attend_other(
                x,
                fetched[2],
                names_of(2),
                v.biases_oth,
                seg_row,
                seg_col,
                v.mixed_own[0],
                v.b[3],
                model_s,
                True,
                bits,
                last,
            )
        elif name == DO_UP_OT:
            (v.act_t_own,) = up_own(v.low_t, t_e, biases, 6 + blocks, False, bits, last)
        elif name == DO_UP_OS:
            v.act_s_own, v.slope_own = up_own(
                v.low_s, v.b_e, biases, 6, True, bits, last
            )
        elif name == DO_UP_XT:
            (v.act_t_oth,) = up_other(
                v.low_t, *fetched[3], names_of(3)[1:], v.biases_oth, 6 + blocks, False, bits, last
            )
        elif name == DO_UP_XS:
            v.act_s_oth, v.slope_oth, v.o_e = up_other(
                v.low_s, *fetched[4], names_of(4)[1:], v.biases_oth, 6, True, bits, last
            )
        elif name == DO_DN_O:
            v.partials = down_own(
                (v.act_s_own, v.act_t_own),
                (v.b_r, t_r),
                (v.first_s, v.first_t),
                models,
                bits,
                last,
            )
        elif name == DO_KD:
            v.out_s, v.d_pre2, v.d_down, v.sums2, v.o_r, v.out_low = down_other(
                (v.act_s_oth, v.act_t_oth),
                fetched[5],
                fetched[6],
                names_of(5)[1:],
                v.partials,
                models,
                seg_col,
                bits,
                last,
            )
        elif name == DO_S:
            v.out_other = swap(touch(v.out_s, bits, last), "x")
        elif name == DO_TT:
            v.tok_other = swap(touch(v.d_tokens, bits, last), "x")
        elif name in (DO_SF, DO_TF):
            if name == DO_SF:
                outs.low = put_rows(v.out_other, bits, last, v.out_low)
            else:
                outs.tok = put_rows(v.tok_other, bits, last, v.out_tok)
        elif name == DO_DU:
            v.d_up_own, v.d_up_oth, v.sums_up = up_back(
                v.d_down,
                (v.b_r, v.o_r),
                (v.slope_own, v.slope_oth),
                bits,
                last,
            )
        elif name == DO_DH1:
            v.d_pre1, v.d_attn, *v.d_mixed, v.sums1 = first_back(
                (v.d_up_own, v.d_up_oth),
                (v.b_e, v.o_e),
                v.d_pre2,
                v.pre_s,
                model_s,
                (v.b[3], v.o[3]),
                bits,
                last,
            )
        elif name == DO_ATT:
            *v.dqk, v.dv_own, v.dv_oth, v.sums_qkv = attend_back(
                (v.qkv_own, v.qkv_oth, v.qk_t), v.d_mixed, seg_row, seg_col, bits, last
            )
        elif name == DO_TOK:
            terms = []
            for d_qk, d_v, weights in (
                (v.dqk[0], v.dv_own, v.b),
                (v.dqk[1], v.dv_oth, v.o),
            ):
                terms += [(d_qk, 0, weights[0]), (d_qk, 1, weights[1]), (d_v, 0, weights[2])]
            v.d_tokens, v.out_tok = token_grad(v.d_pre1, terms, bits, last)
        elif name in OUTERS:
            chunk = OUTERS.index(name)
            part = chunk % 2
            if chunk in (R0, R1):
                acts = (v.act_s_own, v.act_s_oth)
                made = outer([(acts, (v.d_down,) * 2, 0, dim)], bits, last, half * part, half)
            elif chunk in (E0, E1):
                d_ups = (v.d_up_own, v.d_up_oth)
                made = outer([((v.low_s,) * 2, d_ups, part, half)], bits, last)
            elif chunk == QK:
                made = outer([((x, x), v.dqk, 0, 2 * width)], bits, last)
            else:
                mixed = (v.mixed_own[0], v.mixed_oth)
                made = outer(
                    [
                        ((x, x), (v.dv_own, v.dv_oth), 0, width),
                        ((v.d_attn,) * 2, mixed, 0, width),
                    ],
                    bits,
                    last,
                )
            steps[chunk] = reduce_chunk(made, PATHS[chunk])
        elif name >= FETCH_STEP:
            k = name - FETCH_STEP
            if k not in fetching:
                fetching[k] = (
                    fetch_direct(6, lambda: pack_tile(t_r, (), (C,), bits, last))
                    if k == 6
                    else start_fetch(k)
                )
            next(fetching[k])
        else:
            chunk = name - CHUNK_STEP
            if chunk == SUMS and chunk not in steps:
                steps[chunk] = small_sums()
            pieces = next(steps[chunk])
            if pieces is None:
                return
            if chunk == SUMS:
                outs.sums = pieces
                return

            def rows_of(k, b):
                place = b[C] if k == 0 else 1 - b[C]
                return pl.ds(pl.multiple_of(place * tall, 8), tall)

            everything = (0, slice(None), slice(None))
            if chunk in (R0, R1):
                base = (chunk % 2) * dim

                def target(k):
                    def at(b):
                        place = b[C] if k == 0 else 1 - b[C]
                        return (pl.ds(pl.multiple_of(base + place * tall, 8), tall), slice(None))

                    return at

                cuts = [(k, everything, 0, target(k)) for k in range(2)]
                (outs.reduce,) = finish(
                    pieces, cuts, [shape((hidden, dim))], bits, last, outs.reduce
                )
            elif chunk in (E0, E1):
                left = (chunk % 2) * half
                cuts = [
                    (k, everything, 0, lambda b, k=k: (rows_of(k, b), pl.ds(left, half)))
                    for k in range(2)
                ]
                (outs.expand,) = finish(
                    pieces, cuts, [shape((dim, hidden))], bits, last, outs.expand
                )
            else:
                cuts = []
                if chunk == VO:
                    pieces = [*pieces]
                    for k in range(2):
                        pieces.append(flip(pieces[k][:, :, width:], bits, last))
                        cuts.append(
                            (2 + k, (slice(None), slice(None)), 1, lambda b, k=k: (slice(None), rows_of(k, b)))
                        )
                for j in range(1 if chunk == VO else 2):
                    source = (0, slice(None), pl.ds(j * width, width))
                    cuts += [
                        (k, source, j, lambda b, k=k: (rows_of(k, b), slice(None))) for k in range(2)
                    ]
                dims = [(dim, width), (width, dim) if chunk == VO else (dim, width)]
                pair = finish(pieces, cuts, [shape(d) for d in dims], bits, last)
                if chunk == VO:
                    outs.value, outs.output = pair
                else:
                    outs.query, outs.key = pair

    for name in ORDER:
        do(name)
    small = outs.sums
    n_qkv, n_up = 3 * width, hidden
    out_heads = small[0, :n_qkv].reshape(3, width)
    out_hidden = small[0, n_qkv : n_qkv + n_up]
    first, second = (small[:3, n_qkv + n_up + k * dim :][:, :dim] for k in range(2))
    out_model = jnp.stack([first[2], second[2], first[0], first[1], second[0], second[1]])
    return (
        outs.low,
        outs.tok,
        outs.query,
        outs.key,
        outs.value,
        outs.output,
        outs.expand,
        outs.reduce,
        out_heads,
        out_model,
        out_hidden,
    )


def solution(mesh):
    cols = P(None, "narrow")
    rows = P("narrow", None)
    net = (cols, cols, cols, rows, cols, rows, cols, P(), P("narrow"))
    data = P(None, "wide", None)
    return jax.shard_map(
        functools.partial(on_device, mesh.shape["wide"]),
        mesh=mesh,
        in_specs=(data, P(None, "wide")) + net + net,
        out_specs=(data, data) + net,
        check_vma=False,
    )
```

```python
import functools
import types

import jax
import jax.numpy as jnp
from jax import lax
from jax.experimental import pallas as pl
from jax.experimental.pallas import tpu as pltpu
from jax.sharding import PartitionSpec as P

HEAD = 64
REGION = 256

norm_eps = 1e-06
score_weight = 0.05
big_negative = -1e30
f32 = jnp.float32
bf16 = jnp.bfloat16


def dot_nn(left, right):
    return jnp.dot(left, right, preferred_element_type=f32)


def dot_tn(left, right):
    return lax.dot_general(left, right, (((0,), (0,)), ((), ())), preferred_element_type=f32)


def dot_nt(left, right):
    return lax.dot_general(left, right, (((1,), (1,)), ((), ())), preferred_element_type=f32)


MIB = 2**20
STRIP = 384
C, Y, ZL, ZH, SIDE = range(5)


def shape(dims, dtype=f32):
    return jax.ShapeDtypeStruct(dims, dtype)


def vmem(dims, dtype=f32):
    return pltpu.VMEM(dims, dtype)


def hbm(dims, dtype=f32):
    return pltpu.HBM(dims, dtype)


TOKEN = (8, 128)


def invoke(kernel, name, bits, arrays, specs, outs, out_specs, dep, limit, grid, scratch=(), into=None):
    single = not isinstance(outs, (list, tuple))
    outs = [outs] if single else list(outs)
    out_specs = [out_specs] if single else list(out_specs)
    count = len(arrays)
    after = [in_hbm(token) for token in dep] + ([] if into is None else [in_hbm(into)])
    first = count + len(after)
    end = first + len(outs)

    def body(bits_ref, *refs):
        kernel(bits_ref, refs[:count], refs[first:end] + refs[end + 1 :])

    anywhere = pl.BlockSpec(memory_space=pl.ANY)
    in_specs = list(specs) + [anywhere] * len(after)
    form = dict(
        in_specs=in_specs, out_specs=out_specs + [anywhere], scratch_shapes=scratch
    )
    if grid is None:
        form["in_specs"] = [pl.BlockSpec(memory_space=pltpu.SMEM)] + in_specs
    else:
        form = dict(
            grid_spec=pltpu.PrefetchScalarGridSpec(num_scalar_prefetch=1, grid=grid, **form)
        )
    *results, token = pl.pallas_call(
        body,
        out_shape=outs + [pltpu.HBM(TOKEN, f32)],
        input_output_aliases={} if into is None else {first: 0},
        compiler_params=pltpu.CompilerParams(vmem_limit_bytes=limit * MIB),
        cost_estimate=pl.CostEstimate(flops=0, bytes_accessed=0, transcendentals=0),
        name=name,
        **form,
    )(bits, *arrays, *after)
    dep[:] = [token]
    return results[0] if single else results


def call(kernel, name, bits, arrays, specs, outs, out_specs, grid, dep, limit=20, scratch=(), into=None):
    return invoke(
        kernel, name, bits, arrays, specs, outs, out_specs, dep, limit, grid, scratch, into
    )


def whole_call(kernel, name, bits, arrays, outs, dep, limit=16, hold=True):
    if hold:
        arrays = [pin(a) for a in arrays]
    count = len(arrays)
    return invoke(
        kernel, name, bits, arrays, [IN_VMEM] * count, outs, [IN_VMEM] * len(outs), dep, limit, None
    )


def pin(array):
    return pltpu.with_memory_space_constraint(array, pltpu.VMEM)


def in_hbm(array):
    return pltpu.with_memory_space_constraint(array, pltpu.HBM)


IN_VMEM = pl.BlockSpec(memory_space=pltpu.VMEM)


def place_of(bits_ref, names):
    index = 0
    for name in names:
        index = index * 2 + bits_ref[name]
    return index


def fixed(dims):
    return pl.BlockSpec(dims, lambda *a: (0,) * len(dims))


def normalize(values):
    centred = values - jnp.mean(values, axis=-1, keepdims=True)
    spread = jnp.mean(centred * centred, axis=-1, keepdims=True)
    scale = lax.rsqrt(spread + norm_eps)
    return centred * scale, scale


def norm_back(grad, unit, scale, gain):
    inner = grad * (1.0 + gain)
    return scale * (
        inner
        - jnp.mean(inner, axis=-1, keepdims=True)
        - unit * jnp.mean(inner * unit, axis=-1, keepdims=True)
    )


def cdf_of(up):
    return 0.5 + 0.5 * lax.erf(up * 0.5**0.5)


def sign_of(wide, axis):
    alpha = jnp.mean(jnp.abs(wide), axis=axis, keepdims=True)
    return (jnp.where(wide > 0, alpha, jnp.where(wide < 0, -alpha, 0.0))).astype(bf16)


def binarize(weight, axis, bits, dep):
    def kernel(bits_ref, ins, outs):
        outs[0][...] = sign_of(ins[0][...].astype(f32), axis)

    rows, columns = weight.shape
    if axis == 0:
        spec = pl.BlockSpec((rows, STRIP), lambda i, b: (0, i))
        steps = columns // STRIP
    else:
        spec = pl.BlockSpec((STRIP, columns), lambda i, b: (i, 0))
        steps = rows // STRIP
    return call(
        kernel,
        "binarize",
        bits,
        [weight],
        [spec],
        hbm(weight.shape, bf16),
        spec,
        (steps,),
        dep,
    )


def binarize_pack(weights, axes, names, bits, dep):
    parts = 2 ** len(names)

    def kernel(bits_ref, ins, outs):
        part = place_of(bits_ref, names)
        at = 0
        for ref, axis, out in zip(ins, axes, outs):
            result = sign_of(ref[...].astype(f32), axis)
            out[...] = result
            rows, columns = ref.shape[0] // parts, ref.shape[1]
            mine = out[pl.ds(part * rows, rows), :].astype(f32)
            for left in range(0, columns, STRIP):
                outs[-1][at : at + rows, :] = mine[:, left : left + STRIP]
                at += rows

    total = sum(w.size for w in weights) // parts // STRIP
    specs = [fixed(w.shape) for w in weights]
    return call(
        kernel,
        "binarize_pack",
        bits,
        [in_hbm(w) for w in weights],
        specs,
        [hbm(w.shape, bf16) for w in weights] + [vmem((total, STRIP))],
        specs + [IN_VMEM],
        (1,),
        dep,
    )


def pack(weights, names, bits, dep):
    parts = 2 ** len(names)

    def kernel(bits_ref, ins, outs):
        at = 0
        for ref in ins:
            rows, columns = ref.shape
            for left in range(0, columns, STRIP):
                outs[0][at : at + rows, :] = ref[:, left : left + STRIP].astype(f32)
                at += rows

    specs = [
        pl.BlockSpec((w.shape[0] // parts, w.shape[1]), lambda i, b: (place_of(b, names), 0))
        for w in weights
    ]
    total = sum(w.size for w in weights) // parts // STRIP
    return call(
        kernel,
        "pack",
        bits,
        [in_hbm(w) for w in weights],
        specs,
        [vmem((total, STRIP))],
        [IN_VMEM],
        (1,),
        dep,
    )[0]


def pack_tile(weight, row_names, column_names, bits, dep):
    def kernel(bits_ref, ins, outs):
        at = pl.multiple_of(pl.program_id(0) * tall, 8)
        outs[0][pl.ds(at, tall), :] = ins[0][...].astype(f32)

    dims = (weight.shape[0] >> len(row_names), weight.shape[1] >> len(column_names))
    steps = max(1, dims[0] // 384)
    tall = dims[0] // steps
    return call(
        kernel,
        "pack_tile",
        bits,
        [weight],
        [
            pl.BlockSpec(
                (tall, dims[1]),
                lambda i, b: (place_of(b, row_names) * steps + i, place_of(b, column_names)),
            )
        ],
        [vmem(dims)],
        [IN_VMEM],
        (steps,),
        dep,
    )[0]


def touch(array, bits, dep):
    count = len(dep)

    def body(bits_ref, *refs):
        pass

    anywhere = pl.BlockSpec(memory_space=pl.ANY)
    result, token = pl.pallas_call(
        body,
        in_specs=[pl.BlockSpec(memory_space=pltpu.SMEM)] + [anywhere] * (1 + count),
        out_specs=[anywhere] * 2,
        out_shape=[shape(array.shape, array.dtype), pltpu.HBM(TOKEN, f32)],
        input_output_aliases={1: 0},
        compiler_params=pltpu.CompilerParams(vmem_limit_bytes=MIB),
        cost_estimate=pl.CostEstimate(flops=0, bytes_accessed=0, transcendentals=0),
        name="touch",
    )(bits, array, *map(in_hbm, dep))
    dep[:] = [token]
    return result


def join(first, second, bits, dep):
    rows, columns = first.shape

    def kernel(bits_ref, ins, outs):
        for k in range(2):
            outs[0][k * rows : (k + 1) * rows, :] = ins[k][...]

    return whole_call(kernel, "join", bits, [first, second], [vmem((2 * rows, columns))], dep)[0]


def half_masks():
    lane = lax.broadcasted_iota(jnp.int32, (1, 2 * HEAD), 1)
    low = jnp.where(lane < HEAD, 1.0, 0.0).astype(bf16)
    return (low, (1.0 - low.astype(f32)).astype(bf16))


def region_masks(row_ref, col_ref):
    across = row_ref[0]
    down = col_ref[...]
    same = down == across
    live = down >= 0
    size = down.shape[0]
    diagonal = lax.broadcasted_iota(jnp.int32, (size, size), 0) == lax.broadcasted_iota(
        jnp.int32, (size, size), 1
    )
    pairs = same & live
    return pairs, pairs | diagonal


def probabilities(scores, allowed):
    masked = jnp.where(allowed, scores, big_negative)
    top = jnp.max(masked, axis=-1, keepdims=True)
    expo = jnp.exp(masked - top)
    total = jnp.sum(expo, axis=-1, keepdims=True)
    return expo * (1.0 / total)


def attention(parts, allowed, masks, scale, write):
    width = parts[0].shape[1]
    for at in range(0, width, 2 * HEAD):
        query, keys, values = (part[:, at : at + 2 * HEAD] for part in parts)
        probs = [
            probabilities(dot_nt(query * mask, keys) * scale, allowed).astype(bf16) for mask in masks
        ]
        stacked = jnp.concatenate([values * mask for mask in masks], axis=0)
        write(at, dot_nn(jnp.concatenate(probs, axis=1), stacked).astype(bf16))


def attend_own(x, weights, biases, seg_row, seg_col, bits, dep):
    rows, dim = x.shape
    width = weights[0].shape[1]

    def kernel(bits_ref, ins, outs):
        x_ref, bias_ref, row_ref, col_ref = ins[:4]
        tokens = x_ref[...]
        pairs, allowed = region_masks(row_ref, col_ref)
        masks = half_masks()
        for net in range(2):
            parts = []
            for k in range(3):
                row = 3 * net + k
                part = dot_nn(tokens, ins[4 + row][...]) + bias_ref[row : row + 1, :]
                parts.append(part.astype(bf16))
                if row < 5:
                    outs[0][:, row * width : (row + 1) * width] = parts[k]

            def write(at, mixed, net=net):
                outs[1 + net][:, at : at + 2 * HEAD] = mixed

            attention(parts, allowed, masks, HEAD ** (-0.5), write)

    def block(columns):
        return pl.BlockSpec((REGION, columns), lambda i, b: (i, 0))

    return call(
        kernel,
        "attend_own",
        bits,
        [x, biases, seg_row, seg_col, *weights],
        [
            block(dim),
            fixed(biases.shape),
            pl.BlockSpec((1, 1, REGION), lambda i, b: (i, 0, 0)),
            block(1),
        ]
        + [fixed(w.shape) for w in weights],
        [shape((rows, 5 * width), bf16), shape((rows, width), bf16), shape((rows, width), bf16)],
        [block(5 * width), block(width), block(width)],
        (rows // REGION,),
        dep,
    )


def attend_other(
    x, pieces, names, biases, seg_row, seg_col, mixed, output, model, student, bits, dep
):
    rows, dim = x.shape
    width = mixed.shape[1]
    parts = 2 ** len(names)
    half_parts = parts // 2
    tall = dim // parts
    short = width // parts
    per_part = 3 * tall + 2 * short
    first_row = 0 if student else 3
    kept = 3 if student else 2

    def kernel(bits_ref, ins, outs):
        x_ref, bias_ref, row_ref, col_ref, mine_ref, theirs_ref, mixed_ref, out_ref, model_ref = ins
        qkv_ref, low_ref, first_ref = outs[:3]
        weight_refs = outs[5:9] if student else outs[3:7]
        part = place_of(bits_ref, names)

        @pl.when(pl.program_id(0) == 0)
        def _():
            for k in range(parts):
                ref = (mine_ref, theirs_ref)[k // half_parts]
                base = (k % half_parts) * per_part
                where = jnp.bitwise_xor(part, k)
                for m in range(3):
                    weight_refs[m][pl.ds(pl.multiple_of(where * tall, 16), tall), :] = ref[
                        base + m * tall : base + (m + 1) * tall, :
                    ].astype(bf16)
                for m in range(2):
                    at = base + 3 * tall + m * short
                    weight_refs[3][
                        pl.ds(pl.multiple_of(where * short, 16), short), m * STRIP : (m + 1) * STRIP
                    ] = ref[at : at + short, :].astype(bf16)

        tokens = x_ref[...]
        pairs, allowed = region_masks(row_ref, col_ref)
        masks = half_masks()
        parts_qkv = []
        for k in range(3):
            row = first_row + k
            part_k = dot_nn(tokens, weight_refs[k][...]) + bias_ref[row : row + 1, :]
            parts_qkv.append(part_k.astype(bf16))
            if k < kept:
                qkv_ref[:, k * width : (k + 1) * width] = parts_qkv[k]
        tiles = []
        attention(parts_qkv, allowed, masks, HEAD ** (-0.5), lambda at, tile: tiles.append(tile))
        mine = jnp.concatenate(tiles, axis=1)
        pre = (
            tokens.astype(f32)
            + (dot_nn(mixed_ref[...], out_ref[...]) + dot_nn(mine, weight_refs[3][...]))
            + model_ref[0:1, :]
        )
        unit, scale = normalize(pre)
        first = unit * (1.0 + model_ref[2:3, :]) + model_ref[3:4, :]
        low_ref[...] = first.astype(bf16)
        first_ref[...] = first
        if student:
            outs[3][...] = mine
            outs[4][...] = pre

    def block(columns):
        return pl.BlockSpec((REGION, columns), lambda i, b: (i, 0))

    weights = [shape((dim, width), bf16)] * 3 + [shape((width, dim), bf16)]
    outs = [shape((rows, kept * width), bf16), shape((rows, dim), bf16), shape((rows, dim))]
    out_specs = [block(kept * width), block(dim), block(dim)]
    if student:
        outs += [shape((rows, width), bf16), hbm((rows, dim))]
        outs += [hbm(w.shape, bf16) for w in weights]
        out_specs += [block(width), block(dim)] + [fixed(w.shape) for w in weights]
    return call(
        kernel,
        "attend_other",
        bits,
        [x, biases, seg_row, seg_col, *map(pin, pieces), mixed, output, model],
        [
            block(dim),
            fixed(biases.shape),
            pl.BlockSpec((1, 1, REGION), lambda i, b: (i, 0, 0)),
            block(1),
            IN_VMEM,
            IN_VMEM,
            block(width),
            fixed(output.shape),
            fixed(model.shape),
        ],
        outs,
        out_specs,
        (rows // REGION,),
        dep,
        limit=24,
        scratch=[] if student else [pltpu.VMEM(w.shape, bf16) for w in weights],
    )


def activate(up, outs, student):
    cdf = cdf_of(up)
    outs[0][...] = (up * cdf).astype(bf16)
    if student:
        bell = jnp.exp(-0.5 * up * up) * (2.0 * jnp.pi) ** -0.5
        outs[1][...] = (cdf + up * bell).astype(bf16)


def up_own(low, weight, biases, first_row, student, bits, dep):
    tokens, dim = low.shape
    hidden = weight.shape[1]

    def kernel(bits_ref, ins, outs):
        j = pl.program_id(0)
        up = dot_nn(ins[0][...], ins[1][...]) + ins[2][pl.ds(first_row + j, 1), :]
        activate(up, outs, student)

    count = 2 if student else 1
    return call(
        kernel,
        "up_own",
        bits,
        [low, weight, biases],
        [fixed(low.shape), pl.BlockSpec((dim, STRIP), lambda j, b: (0, j)), fixed(biases.shape)],
        [shape((tokens, hidden), bf16), hbm((tokens, hidden), bf16)][:count],
        [pl.BlockSpec((tokens, STRIP), lambda j, b: (0, j))] * count,
        (hidden // STRIP,),
        dep,
    )


def up_other(low, mine, theirs, names, biases, first_row, student, bits, dep):
    tokens, dim = low.shape
    steps = mine.shape[0] // STRIP
    half = dim // 2

    def kernel(bits_ref, ins, outs):
        low_ref, tile_m, tile_o, bias_ref = ins
        j = jnp.bitwise_xor(pl.program_id(0), place_of(bits_ref, names))
        at = pl.ds(pl.multiple_of(pl.program_id(0) * half, 8), half)
        weight_ref = outs[2] if student else outs[1]
        core = bits_ref[C]
        weight_ref[pl.ds(pl.multiple_of(core * half, 16), half), :] = tile_m[at, :].astype(bf16)
        weight_ref[pl.ds(pl.multiple_of((1 - core) * half, 16), half), :] = tile_o[at, :].astype(bf16)
        up = dot_nn(low_ref[...], weight_ref[...]) + bias_ref[pl.ds(first_row + j, 1), :]
        activate(up, outs, student)

    def column(j, b):
        return (0, jnp.bitwise_xor(j, place_of(b, names)))

    outs = [shape((tokens, steps * STRIP), bf16)]
    out_specs = [pl.BlockSpec((tokens, STRIP), column)]
    if student:
        outs += [hbm((tokens, steps * STRIP), bf16), hbm((dim, steps * STRIP), bf16)]
        out_specs += [out_specs[0], pl.BlockSpec((dim, STRIP), column)]
    return call(
        kernel,
        "up_other",
        bits,
        [low, pin(mine), pin(theirs), biases],
        [fixed(low.shape), IN_VMEM, IN_VMEM, fixed(biases.shape)],
        outs,
        out_specs,
        (steps,),
        dep,
        limit=16,
        scratch=[] if student else [pltpu.VMEM((dim, STRIP), bf16)],
    )


def down_own(acts, weights, firsts, models, bits, dep):
    tokens, hidden = acts[0].shape
    dim = weights[0].shape[1]

    def kernel(bits_ref, ins, outs):
        for net in range(2):
            act, weight, first, model = ins[4 * net : 4 * net + 4]
            outs[net][...] = first[...] + model[1:2, :] + dot_nn(act[...], weight[...])

    def block(columns):
        return pl.BlockSpec((REGION, columns), lambda i, b: (i, 0))

    arrays = []
    specs = []
    for net in range(2):
        arrays += [acts[net], weights[net], firsts[net], models[net]]
        specs += [block(hidden), fixed((hidden, dim)), block(dim), fixed(models[net].shape)]
    return call(
        kernel,
        "down_own",
        bits,
        arrays,
        specs,
        [shape((tokens, dim))] * 2,
        [block(dim)] * 2,
        (tokens // REGION,),
        dep,
        limit=24,
    )


def down_other(acts, student_tiles, teacher_tiles, names, partials, models, seg_col, bits, dep):
    tokens, hidden = acts[0].shape
    dim = partials[0].shape[1]
    half = dim // 2
    steps = hidden // STRIP

    def kernel(bits_ref, ins, outs):
        act_s, act_t, s_mine, s_other, t_mine, t_other, part_s, part_t, model_s, model_t, seg = ins
        out_ref, pre_ref, down_ref, sums_ref, weight_ref, low_ref, teacher_ref = outs
        step = pl.program_id(0)
        first_core = bits_ref[C] == 0

        @pl.when(step == 0)
        def _():
            place = place_of(bits_ref, names)
            for k in range(steps):
                rows = slice(k * STRIP, (k + 1) * STRIP)
                where = pl.ds(pl.multiple_of(jnp.bitwise_xor(place, k) * STRIP, 16), STRIP)
                tile, other = s_mine[rows, :].astype(bf16), s_other[rows, :].astype(bf16)
                weight_ref[where, :half] = jnp.where(first_core, tile, other)
                weight_ref[where, half:] = jnp.where(first_core, other, tile)
                tile, other = t_mine[rows, :].astype(bf16), t_other[rows, :].astype(bf16)
                teacher_ref[rows, :half] = jnp.where(first_core, tile, other)
                teacher_ref[rows, half:] = jnp.where(first_core, other, tile)

        unit_s, scale_s = normalize(part_s[...] + dot_nn(act_s[...], weight_ref[...]))
        unit_t, _ = normalize(part_t[...] + dot_nn(act_t[...], teacher_ref[...]))
        gain = model_s[4:5, :]
        out_s = unit_s * (1.0 + gain) + model_s[5:6, :]
        out_t = unit_t * (1.0 + model_t[4:5, :]) + model_t[5:6, :]
        out_ref[...] = out_s
        low_ref[0] = out_s.astype(bf16)
        grad = jnp.where(seg[...] >= 0, out_s - out_t, 0.0)
        d_pre = norm_back(grad, unit_s, scale_s, gain)
        pre_ref[...] = d_pre
        low = d_pre.astype(bf16)
        down_ref[...] = low
        add_sums(sums_ref, (grad * unit_s, grad, low.astype(f32)), step)

    def block(columns):
        return pl.BlockSpec((REGION, columns), lambda i, b: (i, 0))

    return call(
        kernel,
        "down_other",
        bits,
        [*acts, *map(pin, student_tiles), *map(pin, teacher_tiles), *partials, *models, seg_col],
        [block(hidden)] * 2
        + [IN_VMEM] * 4
        + [block(dim)] * 2
        + [fixed(m.shape) for m in models]
        + [block(1)],
        [
            shape((tokens, dim)),
            shape((tokens, dim)),
            shape((tokens, dim), bf16),
            shape((8, dim)),
            hbm((hidden, dim), bf16),
            hbm((2, tokens, dim), bf16),
        ],
        [
            block(dim),
            block(dim),
            block(dim),
            fixed((8, dim)),
            fixed((hidden, dim)),
            pl.BlockSpec((1, REGION, dim), lambda i, b: (b[SIDE], i, 0)),
        ],
        (tokens // REGION,),
        dep,
        limit=28,
        scratch=[pltpu.VMEM((hidden, dim), bf16)],
    )


def up_back(d_down, weights, slopes, bits, dep):
    tokens, dim = d_down.shape
    hidden = weights[0].shape[0]

    def kernel(bits_ref, ins, outs):
        rows = []
        for half in range(2):
            grad = dot_nt(ins[0][...], ins[1 + half][...])
            low = (grad * ins[3 + half][...].astype(f32)).astype(bf16)
            outs[half][...] = low
            rows.append(jnp.sum(low.astype(f32), axis=0, keepdims=True))
        outs[2][...] = jnp.concatenate(rows + [jnp.zeros((6, STRIP), f32)], axis=0)

    block = pl.BlockSpec((tokens, STRIP), lambda j, b: (0, j))
    return call(
        kernel,
        "up_back",
        bits,
        [d_down, *weights, *slopes],
        [fixed(d_down.shape)] + [pl.BlockSpec((STRIP, dim), lambda j, b: (j, 0))] * 2 + [block] * 2,
        [shape((tokens, hidden), bf16)] * 2 + [shape((8, hidden))],
        [block, block, pl.BlockSpec((8, STRIP), lambda j, b: (0, j))],
        (hidden // STRIP,),
        dep,
    )


def add_sums(ref, arrays, step):
    rows = [jnp.sum(v, axis=0, keepdims=True) for v in arrays]
    rows.append(jnp.zeros((8 - len(rows), rows[0].shape[1]), f32))
    new = jnp.concatenate(rows, axis=0)
    ref[...] = jnp.where(step == 0, new, ref[...] + new)


def first_back(d_ups, weights, d_pre2, pre, model, outputs, bits, dep):
    tokens, hidden = d_ups[0].shape
    dim = d_pre2.shape[1]
    width = outputs[0].shape[0]

    def kernel(bits_ref, ins, outs):
        d_own, d_oth, w_own, w_oth, d_pre2_ref, pre_ref, model_ref, o_own, o_oth = ins
        grad = d_pre2_ref[...] + (dot_nt(d_own[...], w_own[...]) + dot_nt(d_oth[...], w_oth[...]))
        unit, scale = normalize(pre_ref[...])
        d_pre = norm_back(grad, unit, scale, model_ref[2:3, :])
        outs[0][...] = d_pre
        low = d_pre.astype(bf16)
        outs[1][...] = low
        outs[2][...] = dot_nt(low, o_own[...]).astype(bf16)
        outs[3][...] = dot_nt(low, o_oth[...]).astype(bf16)
        add_sums(outs[4], (grad * unit, grad, low.astype(f32)), pl.program_id(0))

    def block(columns):
        return pl.BlockSpec((REGION, columns), lambda i, b: (i, 0))

    return call(
        kernel,
        "first_back",
        bits,
        [*d_ups, *weights, d_pre2, pre, model, *outputs],
        [block(hidden)] * 2
        + [fixed(w.shape) for w in weights]
        + [block(dim)] * 2
        + [fixed(model.shape)]
        + [fixed(o.shape) for o in outputs],
        [
            shape((tokens, dim)),
            shape((tokens, dim), bf16),
            shape((tokens, width), bf16),
            shape((tokens, width), bf16),
            shape((8, dim)),
        ],
        [block(dim), block(dim), block(width), block(width), fixed((8, dim))],
        (tokens // REGION,),
        dep,
        limit=28,
    )


def token_grad(d_pre, terms, bits, dep):
    tokens, dim = d_pre.shape

    def kernel(bits_ref, ins, outs):
        total = ins[0][...]
        for k in range(len(terms)):
            total = total + dot_nt(ins[1 + 2 * k][...], ins[2 + 2 * k][...])
        outs[0][...] = total
        outs[1][0] = total

    arrays = [d_pre]
    specs = [pl.BlockSpec((REGION, dim), lambda i, b: (i, 0))]
    for grad, at, weight in terms:
        arrays += [grad, weight]
        specs += [
            pl.BlockSpec((REGION, weight.shape[1]), lambda i, b, at=at: (i, at)),
            fixed(weight.shape),
        ]
    return call(
        kernel,
        "token_grad",
        bits,
        arrays,
        specs,
        [shape((tokens, dim)), pltpu.HBM((2, tokens, dim), f32)],
        [specs[0], pl.BlockSpec((1, REGION, dim), lambda i, b: (b[SIDE], i, 0))],
        (tokens // REGION,),
        dep,
    )


def attend_back(qkv, grads, seg_row, seg_col, bits, dep):
    rows, columns = qkv[0].shape
    width = columns // 5
    step = 2 * HEAD

    def kernel(bits_ref, ins, outs):
        pairs, allowed = region_masks(ins[5], ins[6])
        weight = jnp.where(pairs, score_weight, 0.0)
        masks = half_masks()
        scale = HEAD ** (-0.5)

        @pl.when(pl.program_id(0) == 0)
        def _():
            outs[4][...] = jnp.zeros_like(outs[4])

        for part in range(2):
            for at in range(0, width, step):
                places = [(0, k) for k in range(5)] if part == 0 else [(1, 0), (1, 1), (1, 2), (2, 0), (2, 1)]
                query, keys, values, query_t, keys_t = (
                    ins[r][:, k * width + at : k * width + at + step] for r, k in places
                )
                grad = ins[3 + part][:, at : at + step]
                probs = []
                slopes = []
                for mask in masks:
                    scores = dot_nt(query * mask, keys) * scale
                    prob = probabilities(scores, allowed)
                    gap = scores - dot_nt(query_t * mask, keys_t) * scale
                    d_prob = dot_nt(grad * mask, values)
                    mean = jnp.sum(prob * d_prob, axis=-1, keepdims=True)
                    slope = prob * (d_prob - mean) + weight * gap
                    probs.append(prob.astype(bf16))
                    slopes.append(slope.astype(bf16))

                def both(array):
                    return jnp.concatenate([array * mask for mask in masks], axis=0)

                d_query = dot_nn(jnp.concatenate(slopes, axis=1), both(keys)) * scale
                d_keys = dot_tn(jnp.concatenate(slopes, axis=0), both(query)) * scale
                d_values = dot_tn(jnp.concatenate(probs, axis=0), both(grad))
                for k, result in enumerate((d_query, d_keys, d_values)):
                    low = result.astype(bf16)
                    if k < 2:
                        outs[part][:, k * width + at : k * width + at + step] = low
                    else:
                        outs[2 + part][:, at : at + step] = low
                    outs[4][part : part + 1, k * width + at : k * width + at + step] += jnp.sum(
                        low.astype(f32), axis=0, keepdims=True
                    )

    def block(columns):
        return pl.BlockSpec((REGION, columns), lambda i, b: (i, 0))

    return call(
        kernel,
        "attend_back",
        bits,
        [*qkv, *grads, seg_row, seg_col],
        [
            block(columns),
            block(3 * width),
            block(2 * width),
            block(width),
            block(width),
            pl.BlockSpec((1, 1, REGION), lambda i, b: (i, 0, 0)),
            block(1),
        ],
        [shape((rows, 2 * width), bf16)] * 2
        + [shape((rows, width), bf16)] * 2
        + [shape((8, 3 * width))],
        [block(2 * width)] * 2 + [block(width)] * 2 + [fixed((8, 3 * width))],
        (rows // REGION,),
        dep,
    )


def outer(groups, bits, dep, start=0, size=None, block=384):
    size = size or groups[0][0][0].shape[1]
    tall = size // 2
    steps = tall // block
    tokens = groups[0][0][0].shape[0]
    arrays = []
    specs = []
    for lhs, rhs, at, columns in groups:
        for half in range(2):

            def left(p, h, i, b, half=half, lhs=lhs):
                core = jnp.where(p == 0, 1 - b[C], b[C])
                where = start // block + core * steps + i
                return (0, where if lhs[0] is lhs[1] else jnp.where(h == half, where, start // block))

            arrays += [lhs[half], rhs[half]]
            specs += [
                pl.BlockSpec((tokens, block), left),
                pl.BlockSpec((tokens, columns), lambda p, h, i, b, at=at: (0, at)),
            ]
    wide = sum(g[3] for g in groups)

    def kernel(bits_ref, ins, outs):
        for phase in range(2):
            for half in range(2):

                @pl.when((pl.program_id(0) == phase) & (pl.program_id(1) == half))
                def _(phase=phase, half=half):
                    at = 0
                    row = pl.multiple_of(pl.program_id(2) * block, 8)
                    for k, group in enumerate(groups):
                        lhs, rhs = ins[4 * k + 2 * half], ins[4 * k + 2 * half + 1]
                        outs[phase][half, pl.ds(row, block), at : at + group[3]] = dot_tn(
                            lhs[...], rhs[...]
                        )
                        at += group[3]

    out = vmem((2, tall, wide))
    return call(
        kernel, "outer", bits, arrays, specs, [out, out], [IN_VMEM, IN_VMEM], (2, 2, steps), dep, limit=16
    )


def split(first, second, name, bits, dep, limit=16):
    halves, rows, columns = first.shape
    out = vmem((1, rows, columns)) if name == "x" else vmem((halves, rows // 2, columns))

    def kernel(bits_ref, ins, outs):
        for k in range(2):
            if name == "x":
                where = (pl.ds(1 - k, 1), slice(None))
            else:
                bit = bits_ref[name]
                start = (1 - bit if k == 0 else bit) * (rows // 2)
                where = (slice(None), pl.ds(pl.multiple_of(start, 8), rows // 2))
            outs[k][...] = ins[0][where] + ins[1][where]

    return whole_call(kernel, "split", bits, [first, second], [out, out], dep, limit)


def add(first, second, bits, dep):
    def kernel(bits_ref, ins, outs):
        outs[0][...] = ins[0][...] + ins[1][...]

    return whole_call(kernel, "add", bits, [first, second], [vmem(first.shape)], dep)[0]


def merge(mine, theirs, name, bits, dep):
    one, rows, columns = mine.shape

    def kernel(bits_ref, ins, outs):
        bit = bits_ref[name]
        for k in range(2):
            start = (bit if k == 0 else 1 - bit) * rows
            outs[0][:, pl.ds(pl.multiple_of(start, 8), rows)] = ins[k][...]

    return whole_call(kernel, "merge", bits, [mine, theirs], [vmem((1, 2 * rows, columns))], dep)[0]


def finish(pieces, cuts, outs, bits, dep, into=None):
    def kernel(bits_ref, ins, refs):
        results, sems = refs[:-1], refs[-1]
        copies = []
        for k, (piece, source, out, target) in enumerate(cuts):
            copy = pltpu.make_async_copy(
                ins[piece].at[source], results[out].at[target(bits_ref)], sems.at[k]
            )
            copy.start()
            copies.append(copy)
        for copy in copies:
            copy.wait()

    return invoke(
        kernel,
        "finish",
        bits,
        [*map(pin, pieces)],
        [IN_VMEM] * len(pieces),
        [pltpu.HBM(o.shape, o.dtype) for o in outs],
        [pl.BlockSpec(memory_space=pl.ANY)] * len(outs),
        dep,
        8,
        None,
        [pltpu.SemaphoreType.DMA((len(cuts),))],
        into,
    )


def flip(array, bits, dep):
    def kernel(bits_ref, ins, outs):
        outs[0][...] = ins[0][0].T

    one, rows, columns = array.shape
    return whole_call(kernel, "flip", bits, [array], [vmem((columns, rows))], dep)[0]


def put_rows(array, bits, dep, into):
    two, rows, dim = into.shape
    tall = rows // 4

    def kernel(bits_ref, ins, outs):
        at = pl.ds(pl.multiple_of(pl.program_id(0) * tall, 8), tall)
        outs[-1][0] = ins[0][at, :].astype(into.dtype)

    return call(
        kernel,
        "place",
        bits,
        [pin(array)],
        [IN_VMEM],
        [pltpu.HBM(into.shape, into.dtype)],
        [pl.BlockSpec((1, tall, dim), lambda i, b: (1 - b[SIDE], i, 0))],
        (4,),
        dep,
        into=into,
    )[0]


def collect(sums, other, bits, dep):
    wide = sum(s.shape[1] for s in sums)

    def kernel(bits_ref, ins, outs):
        at = 0
        for k, ref in enumerate(ins):
            columns = ref.shape[1]
            if other and k < 2:
                both = jnp.concatenate([ref[1:2, :], ref[0:1, :], ref[2:, :]], axis=0)
            else:
                both = ref[...]
            outs[0][:, at : at + columns] = both
            at += columns

    return whole_call(kernel, "collect", bits, sums, [vmem((8, wide))], dep)[0]


R0, R1, E0, E1, QK, VO, SUMS = range(7)
(
    DO_B0,
    DO_B1,
    DO_BIN_A,
    DO_BIN_E,
    DO_BIN_R,
    DO_ATT_O,
    DO_KBT,
    DO_KBS,
    DO_UP_OT,
    DO_UP_OS,
    DO_UP_XT,
    DO_UP_XS,
    DO_DN_O,
    DO_KD,
    DO_S,
    DO_TT,
    DO_SF,
    DO_TF,
    DO_DU,
    DO_DH1,
    DO_ATT,
    DO_TOK,
    DO_O_R0,
    DO_O_R1,
    DO_O_E0,
    DO_O_E1,
    DO_O_QK,
    DO_O_VO,
) = range(28)
OUTERS = (DO_O_R0, DO_O_R1, DO_O_E0, DO_O_E1, DO_O_QK, DO_O_VO)
CHUNK_STEP, FETCH_STEP = 50, 60
PATHS = {
    R0: ("x", Y, ZL, ZH),
    R1: ("x", Y, ZL, ZH),
    E0: (Y, ZL, "x", ZH),
    E1: (ZL, "x", Y, ZH),
    QK: ("x", Y, ZL, ZH),
    VO: (ZL, Y, "x", ZH),
}
FETCH = ((ZL,), (ZL, Y), (ZL, Y), (Y, ZL), (ZL, Y))
ORDER = (
    FETCH_STEP + 3, DO_BIN_A, DO_BIN_E, DO_BIN_R, FETCH_STEP + 2, FETCH_STEP + 3,
    FETCH_STEP + 6, FETCH_STEP + 4, FETCH_STEP + 1, FETCH_STEP + 2, FETCH_STEP + 3, DO_B0,
    FETCH_STEP + 5, FETCH_STEP + 2, FETCH_STEP + 1, DO_ATT_O, FETCH_STEP + 3, DO_B1,
    FETCH_STEP + 5, FETCH_STEP + 4, FETCH_STEP + 1, FETCH_STEP + 2, FETCH_STEP + 3,
    FETCH_STEP + 1, DO_KBT, DO_UP_OT, FETCH_STEP + 2, FETCH_STEP + 4, FETCH_STEP + 5, DO_UP_XT,
    DO_KBS, DO_UP_OS, DO_DN_O, FETCH_STEP + 4, FETCH_STEP + 5, FETCH_STEP + 6, FETCH_STEP + 4,
    DO_UP_XS, FETCH_STEP + 5, FETCH_STEP + 6, DO_KD, DO_O_R1, CHUNK_STEP + R1, DO_DU, DO_O_E1,
    CHUNK_STEP + R1, CHUNK_STEP + E1, DO_O_R0, DO_DH1, DO_O_E0, CHUNK_STEP + E1, DO_ATT,
    CHUNK_STEP + R1, CHUNK_STEP + SUMS, CHUNK_STEP + E0, CHUNK_STEP + R0, DO_O_QK,
    CHUNK_STEP + QK, DO_O_VO, CHUNK_STEP + SUMS, CHUNK_STEP + E1, CHUNK_STEP + R1,
    CHUNK_STEP + VO, CHUNK_STEP + QK, CHUNK_STEP + E0, CHUNK_STEP + SUMS, CHUNK_STEP + VO,
    CHUNK_STEP + R1, CHUNK_STEP + R1, CHUNK_STEP + QK, CHUNK_STEP + R0, DO_TOK,
    CHUNK_STEP + E0, CHUNK_STEP + VO, CHUNK_STEP + QK, CHUNK_STEP + R1, CHUNK_STEP + QK,
    CHUNK_STEP + E1, CHUNK_STEP + E1, CHUNK_STEP + QK, CHUNK_STEP + VO, CHUNK_STEP + E0,
    CHUNK_STEP + R0, CHUNK_STEP + VO, DO_S, DO_TT, CHUNK_STEP + R1, CHUNK_STEP + E1,
    CHUNK_STEP + E0, CHUNK_STEP + SUMS, CHUNK_STEP + VO, CHUNK_STEP + QK, CHUNK_STEP + R0,
    CHUNK_STEP + E0, CHUNK_STEP + SUMS, CHUNK_STEP + VO, CHUNK_STEP + R0, CHUNK_STEP + E1,
    CHUNK_STEP + E0, CHUNK_STEP + R0, CHUNK_STEP + QK, DO_TF, CHUNK_STEP + VO, CHUNK_STEP + R0,
    CHUNK_STEP + E0, CHUNK_STEP + VO, CHUNK_STEP + QK, DO_SF, CHUNK_STEP + E0, CHUNK_STEP + R1,
    CHUNK_STEP + SUMS, CHUNK_STEP + R0, CHUNK_STEP + E1, CHUNK_STEP + R0, CHUNK_STEP + E1,
)


def on_device(n_wide, tokens, segments, *params):
    (w_q, w_k, w_v, w_o, w_e, w_r, heads_s, model_s, hidden_s) = params[:9]
    (t_q, t_k, t_v, t_o, t_e, t_r, heads_t, model_t, hidden_t) = params[9:]
    n_bits = n_wide.bit_length() - 1
    side = lax.axis_index("narrow")
    place = lax.axis_index("wide")
    bits = jnp.stack([(place >> b) & 1 for b in range(4)] + [side]).astype(jnp.int32)
    dim, width = w_q.shape
    hidden = w_e.shape[1]

    def swap(array, bit):
        if bit == "x":
            return lax.ppermute(array, "narrow", [(0, 1), (1, 0)])
        return lax.ppermute(array, "wide", [(i, i ^ (1 << bit)) for i in range(n_wide)])

    x = lax.dynamic_index_in_dim(tokens, side, 0, keepdims=False)
    segment = lax.dynamic_index_in_dim(segments, side, 0, keepdims=False)
    rows = x.shape[0]
    seg_row = segment.reshape(rows // REGION, 1, REGION)
    seg_col = segment.reshape(rows, 1)
    biases = jnp.concatenate(
        [heads_s, heads_t, hidden_s.reshape(-1, width), hidden_t.reshape(-1, width)]
    )
    blocks = hidden // width
    models = (model_s, model_t)
    half = hidden // 2

    v = types.SimpleNamespace()
    fetched = {}
    last = []

    def fetch(key, made, path):
        held = swap(made(), "x")
        yield
        held = touch(held, bits, last)
        for name in path:
            got = swap(held, name)
            yield
            held = join(held, got, bits, last)
        got = swap(held, C)
        yield
        fetched[key] = (held, touch(got, bits, last))
        yield

    def fetch_direct(key, made):
        zero = swap(made(), "x")
        yield
        zero = touch(zero, bits, last)
        got = swap(zero, C)
        yield
        fetched[key] = (zero, touch(got, bits, last))
        yield

    def reduce_chunk(made, path):
        send, keep = made
        got = swap(touch(send, bits, last), C)
        yield
        for name in path[:-1]:
            send, keep = split(keep, got, name, bits, last)
            got = swap(send, name)
            yield
        block = add(keep, got, bits, last)
        got = swap(block, path[-1])
        yield
        for extra in range(4, n_bits):
            block = block + got
            got = swap(block, extra)
        block = add(block, got, bits, last)
        back = [name for name in reversed(path[:-1]) if name != "x"] + [C]
        for name in back[:-1]:
            got = swap(block, name)
            yield
            block = merge(block, got, name, bits, last)
        got = swap(block, C)
        yield
        yield (block, got)

    def small_sums():
        sums = [v.sums_qkv, v.sums_up, v.sums1, v.sums2]
        total = collect(sums, False, bits, last)
        got = swap(collect(sums, True, bits, last), "x")
        yield
        for b in range(4):
            total = add(total, got, bits, last)
            got = swap(total, b)
            yield
        total = add(total, got, bits, last)
        for b in range(4, n_bits):
            total = total + swap(total, b)
        yield total

    tall = dim // 2
    steps = {}
    fetching = {}
    outs = types.SimpleNamespace(reduce=None, expand=None)

    def names_of(k):
        return (C, *reversed(FETCH[k - 1]))

    def start_fetch(k):
        names = names_of(k)
        makers = {
            1: lambda: pack([t_q, t_k, t_v, t_o], names, bits, last),
            2: lambda: touch(v.b_pack, bits, last),
            3: lambda: pack_tile(in_hbm(t_e), (C,), names[1:], bits, last),
            4: lambda: pack_tile(v.b_e, (C,), names[1:], bits, last),
            5: lambda: pack_tile(v.b_r, names[1:], (C,), bits, last),
        }
        return fetch(k, makers[k], FETCH[k - 1])

    def do(name):
        if name == DO_B0:
            v.biases_oth = swap(touch(biases, bits, last), "x")
        elif name == DO_B1:
            v.biases_oth = touch(v.biases_oth, bits, last)
        elif name == DO_BIN_A:
            *v.b, v.b_pack = binarize_pack(
                [w_q, w_k, w_v, w_o], (0, 0, 0, 1), names_of(2), bits, last
            )
        elif name == DO_BIN_E:
            v.b_e = binarize(w_e, 0, bits, last)
        elif name == DO_BIN_R:
            v.b_r = binarize(w_r, 1, bits, last)
        elif name == DO_ATT_O:
            b = v.b
            v.qkv_own, *v.mixed_own = attend_own(
                x,
                (b[0], b[1], b[2], in_hbm(t_q), in_hbm(t_k), in_hbm(t_v)),
                biases,
                seg_row,
                seg_col,
                bits,
                last,
            )
        elif name == DO_KBT:
            v.qk_t, v.low_t, v.first_t = attend_other(
                x,
                fetched[1],
                names_of(1),
                v.biases_oth,
                seg_row,
                seg_col,
                v.mixed_own[1],
                t_o,
                model_t,
                False,
                bits,
                last,
            )
        elif name == DO_KBS:
            v.qkv_oth, v.low_s, v.first_s, v.mixed_oth, v.pre_s, *v.o = attend_other(
                x,
                fetched[2],
                names_of(2),
                v.biases_oth,
                seg_row,
                seg_col,
                v.mixed_own[0],
                v.b[3],
                model_s,
                True,
                bits,
                last,
            )
        elif name == DO_UP_OT:
            (v.act_t_own,) = up_own(v.low_t, t_e, biases, 6 + blocks, False, bits, last)
        elif name == DO_UP_OS:
            v.act_s_own, v.slope_own = up_own(
                v.low_s, v.b_e, biases, 6, True, bits, last
            )
        elif name == DO_UP_XT:
            (v.act_t_oth,) = up_other(
                v.low_t, *fetched[3], names_of(3)[1:], v.biases_oth, 6 + blocks, False, bits, last
            )
        elif name == DO_UP_XS:
            v.act_s_oth, v.slope_oth, v.o_e = up_other(
                v.low_s, *fetched[4], names_of(4)[1:], v.biases_oth, 6, True, bits, last
            )
        elif name == DO_DN_O:
            v.partials = down_own(
                (v.act_s_own, v.act_t_own),
                (v.b_r, t_r),
                (v.first_s, v.first_t),
                models,
                bits,
                last,
            )
        elif name == DO_KD:
            v.out_s, v.d_pre2, v.d_down, v.sums2, v.o_r, v.out_low = down_other(
                (v.act_s_oth, v.act_t_oth),
                fetched[5],
                fetched[6],
                names_of(5)[1:],
                v.partials,
                models,
                seg_col,
                bits,
                last,
            )
        elif name == DO_S:
            v.out_other = swap(touch(v.out_s, bits, last), "x")
        elif name == DO_TT:
            v.tok_other = swap(touch(v.d_tokens, bits, last), "x")
        elif name in (DO_SF, DO_TF):
            if name == DO_SF:
                outs.low = put_rows(v.out_other, bits, last, v.out_low)
            else:
                outs.tok = put_rows(v.tok_other, bits, last, v.out_tok)
        elif name == DO_DU:
            v.d_up_own, v.d_up_oth, v.sums_up = up_back(
                v.d_down,
                (v.b_r, v.o_r),
                (v.slope_own, v.slope_oth),
                bits,
                last,
            )
        elif name == DO_DH1:
            v.d_pre1, v.d_attn, *v.d_mixed, v.sums1 = first_back(
                (v.d_up_own, v.d_up_oth),
                (v.b_e, v.o_e),
                v.d_pre2,
                v.pre_s,
                model_s,
                (v.b[3], v.o[3]),
                bits,
                last,
            )
        elif name == DO_ATT:
            *v.dqk, v.dv_own, v.dv_oth, v.sums_qkv = attend_back(
                (v.qkv_own, v.qkv_oth, v.qk_t), v.d_mixed, seg_row, seg_col, bits, last
            )
        elif name == DO_TOK:
            terms = []
            for d_qk, d_v, weights in (
                (v.dqk[0], v.dv_own, v.b),
                (v.dqk[1], v.dv_oth, v.o),
            ):
                terms += [(d_qk, 0, weights[0]), (d_qk, 1, weights[1]), (d_v, 0, weights[2])]
            v.d_tokens, v.out_tok = token_grad(v.d_pre1, terms, bits, last)
        elif name in OUTERS:
            chunk = OUTERS.index(name)
            part = chunk % 2
            if chunk in (R0, R1):
                acts = (v.act_s_own, v.act_s_oth)
                made = outer([(acts, (v.d_down,) * 2, 0, dim)], bits, last, half * part, half)
            elif chunk in (E0, E1):
                d_ups = (v.d_up_own, v.d_up_oth)
                made = outer([((v.low_s,) * 2, d_ups, part, half)], bits, last)
            elif chunk == QK:
                made = outer([((x, x), v.dqk, 0, 2 * width)], bits, last)
            else:
                mixed = (v.mixed_own[0], v.mixed_oth)
                made = outer(
                    [
                        ((x, x), (v.dv_own, v.dv_oth), 0, width),
                        ((v.d_attn,) * 2, mixed, 0, width),
                    ],
                    bits,
                    last,
                )
            steps[chunk] = reduce_chunk(made, PATHS[chunk])
        elif name >= FETCH_STEP:
            k = name - FETCH_STEP
            if k not in fetching:
                fetching[k] = (
                    fetch_direct(6, lambda: pack_tile(t_r, (), (C,), bits, last))
                    if k == 6
                    else start_fetch(k)
                )
            next(fetching[k])
        else:
            chunk = name - CHUNK_STEP
            if chunk == SUMS and chunk not in steps:
                steps[chunk] = small_sums()
            pieces = next(steps[chunk])
            if pieces is None:
                return
            if chunk == SUMS:
                outs.sums = pieces
                return

            def rows_of(k, b):
                place = b[C] if k == 0 else 1 - b[C]
                return pl.ds(pl.multiple_of(place * tall, 8), tall)

            everything = (0, slice(None), slice(None))
            if chunk in (R0, R1):
                base = (chunk % 2) * dim

                def target(k):
                    def at(b):
                        place = b[C] if k == 0 else 1 - b[C]
                        return (pl.ds(pl.multiple_of(base + place * tall, 8), tall), slice(None))

                    return at

                cuts = [(k, everything, 0, target(k)) for k in range(2)]
                (outs.reduce,) = finish(
                    pieces, cuts, [shape((hidden, dim))], bits, last, outs.reduce
                )
            elif chunk in (E0, E1):
                left = (chunk % 2) * half
                cuts = [
                    (k, everything, 0, lambda b, k=k: (rows_of(k, b), pl.ds(left, half)))
                    for k in range(2)
                ]
                (outs.expand,) = finish(
                    pieces, cuts, [shape((dim, hidden))], bits, last, outs.expand
                )
            else:
                cuts = []
                if chunk == VO:
                    pieces = [*pieces]
                    for k in range(2):
                        pieces.append(flip(pieces[k][:, :, width:], bits, last))
                        cuts.append(
                            (2 + k, (slice(None), slice(None)), 1, lambda b, k=k: (slice(None), rows_of(k, b)))
                        )
                for j in range(1 if chunk == VO else 2):
                    source = (0, slice(None), pl.ds(j * width, width))
                    cuts += [
                        (k, source, j, lambda b, k=k: (rows_of(k, b), slice(None))) for k in range(2)
                    ]
                dims = [(dim, width), (width, dim) if chunk == VO else (dim, width)]
                pair = finish(pieces, cuts, [shape(d) for d in dims], bits, last)
                if chunk == VO:
                    outs.value, outs.output = pair
                else:
                    outs.query, outs.key = pair

    for name in ORDER:
        do(name)
    small = outs.sums
    n_qkv, n_up = 3 * width, hidden
    out_heads = small[0, :n_qkv].reshape(3, width)
    out_hidden = small[0, n_qkv : n_qkv + n_up]
    first, second = (small[:3, n_qkv + n_up + k * dim :][:, :dim] for k in range(2))
    out_model = jnp.stack([first[2], second[2], first[0], first[1], second[0], second[1]])
    return (
        outs.low,
        outs.tok,
        outs.query,
        outs.key,
        outs.value,
        outs.output,
        outs.expand,
        outs.reduce,
        out_heads,
        out_model,
        out_hidden,
    )


def solution(mesh):
    cols = P(None, "narrow")
    rows = P("narrow", None)
    net = (cols, cols, cols, rows, cols, rows, cols, P(), P("narrow"))
    data = P(None, "wide", None)
    return jax.shard_map(
        functools.partial(on_device, mesh.shape["wide"]),
        mesh=mesh,
        in_specs=(data, P(None, "wide")) + net + net,
        out_specs=(data, data) + net,
        check_vma=False,
    )
```

```python
import functools
import types

import jax
import jax.numpy as jnp
from jax import lax
from jax.experimental import pallas as pl
from jax.experimental.pallas import tpu as pltpu
from jax.sharding import PartitionSpec as P

HEAD = 64
REGION = 256

norm_eps = 1e-06
score_weight = 0.05
big_negative = -1e30
f32 = jnp.float32
bf16 = jnp.bfloat16


def dot_nn(left, right):
    return jnp.dot(left, right, preferred_element_type=f32)


def dot_tn(left, right):
    return lax.dot_general(left, right, (((0,), (0,)), ((), ())), preferred_element_type=f32)


def dot_nt(left, right):
    return lax.dot_general(left, right, (((1,), (1,)), ((), ())), preferred_element_type=f32)


MIB = 2**20
STRIP = 384
C, Y, ZL, ZH, SIDE = range(5)


def shape(dims, dtype=f32):
    return jax.ShapeDtypeStruct(dims, dtype)


def vmem(dims, dtype=f32):
    return pltpu.VMEM(dims, dtype)


def hbm(dims, dtype=f32):
    return pltpu.HBM(dims, dtype)


TOKEN = (8, 128)


def invoke(kernel, name, bits, arrays, specs, outs, out_specs, dep, limit, grid, scratch=(), into=None):
    single = not isinstance(outs, (list, tuple))
    outs = [outs] if single else list(outs)
    out_specs = [out_specs] if single else list(out_specs)
    count = len(arrays)
    after = [in_hbm(token) for token in dep] + ([] if into is None else [in_hbm(into)])
    first = count + len(after)
    end = first + len(outs)

    def body(bits_ref, *refs):
        kernel(bits_ref, refs[:count], refs[first:end] + refs[end + 1 :])

    anywhere = pl.BlockSpec(memory_space=pl.ANY)
    in_specs = list(specs) + [anywhere] * len(after)
    form = dict(
        in_specs=in_specs, out_specs=out_specs + [anywhere], scratch_shapes=scratch
    )
    if grid is None:
        form["in_specs"] = [pl.BlockSpec(memory_space=pltpu.SMEM)] + in_specs
    else:
        form = dict(
            grid_spec=pltpu.PrefetchScalarGridSpec(num_scalar_prefetch=1, grid=grid, **form)
        )
    *results, token = pl.pallas_call(
        body,
        out_shape=outs + [pltpu.HBM(TOKEN, f32)],
        input_output_aliases={} if into is None else {first: 0},
        compiler_params=pltpu.CompilerParams(vmem_limit_bytes=limit * MIB),
        cost_estimate=pl.CostEstimate(flops=0, bytes_accessed=0, transcendentals=0),
        name=name,
        **form,
    )(bits, *arrays, *after)
    dep[:] = [token]
    return results[0] if single else results


def call(kernel, name, bits, arrays, specs, outs, out_specs, grid, dep, limit=20, scratch=(), into=None):
    return invoke(
        kernel, name, bits, arrays, specs, outs, out_specs, dep, limit, grid, scratch, into
    )


def whole_call(kernel, name, bits, arrays, outs, dep, limit=16, hold=True):
    if hold:
        arrays = [pin(a) for a in arrays]
    count = len(arrays)
    return invoke(
        kernel, name, bits, arrays, [IN_VMEM] * count, outs, [IN_VMEM] * len(outs), dep, limit, None
    )


def pin(array):
    return pltpu.with_memory_space_constraint(array, pltpu.VMEM)


def in_hbm(array):
    return pltpu.with_memory_space_constraint(array, pltpu.HBM)


IN_VMEM = pl.BlockSpec(memory_space=pltpu.VMEM)


def place_of(bits_ref, names):
    index = 0
    for name in names:
        index = index * 2 + bits_ref[name]
    return index


def fixed(dims):
    return pl.BlockSpec(dims, lambda *a: (0,) * len(dims))


def normalize(values):
    centred = values - jnp.mean(values, axis=-1, keepdims=True)
    spread = jnp.mean(centred * centred, axis=-1, keepdims=True)
    scale = lax.rsqrt(spread + norm_eps)
    return centred * scale, scale


def norm_back(grad, unit, scale, gain):
    inner = grad * (1.0 + gain)
    return scale * (
        inner
        - jnp.mean(inner, axis=-1, keepdims=True)
        - unit * jnp.mean(inner * unit, axis=-1, keepdims=True)
    )


def cdf_of(up):
    return 0.5 + 0.5 * lax.erf(up * 0.5**0.5)


def sign_of(wide, axis):
    alpha = jnp.mean(jnp.abs(wide), axis=axis, keepdims=True)
    return (jnp.where(wide > 0, alpha, jnp.where(wide < 0, -alpha, 0.0))).astype(bf16)


def binarize(weight, axis, bits, dep):
    def kernel(bits_ref, ins, outs):
        outs[0][...] = sign_of(ins[0][...].astype(f32), axis)

    rows, columns = weight.shape
    if axis == 0:
        spec = pl.BlockSpec((rows, STRIP), lambda i, b: (0, i))
        steps = columns // STRIP
    else:
        spec = pl.BlockSpec((STRIP, columns), lambda i, b: (i, 0))
        steps = rows // STRIP
    return call(
        kernel,
        "binarize",
        bits,
        [weight],
        [spec],
        hbm(weight.shape, bf16),
        spec,
        (steps,),
        dep,
    )


def binarize_pack(weights, axes, names, bits, dep):
    parts = 2 ** len(names)

    def kernel(bits_ref, ins, outs):
        part = place_of(bits_ref, names)
        at = 0
        for ref, axis, out in zip(ins, axes, outs):
            result = sign_of(ref[...].astype(f32), axis)
            out[...] = result
            rows, columns = ref.shape[0] // parts, ref.shape[1]
            mine = out[pl.ds(part * rows, rows), :].astype(f32)
            for left in range(0, columns, STRIP):
                outs[-1][at : at + rows, :] = mine[:, left : left + STRIP]
                at += rows

    total = sum(w.size for w in weights) // parts // STRIP
    specs = [fixed(w.shape) for w in weights]
    return call(
        kernel,
        "binarize_pack",
        bits,
        [in_hbm(w) for w in weights],
        specs,
        [hbm(w.shape, bf16) for w in weights] + [vmem((total, STRIP))],
        specs + [IN_VMEM],
        (1,),
        dep,
    )


def pack(weights, names, bits, dep):
    parts = 2 ** len(names)

    def kernel(bits_ref, ins, outs):
        at = 0
        for ref in ins:
            rows, columns = ref.shape
            for left in range(0, columns, STRIP):
                outs[0][at : at + rows, :] = ref[:, left : left + STRIP].astype(f32)
                at += rows

    specs = [
        pl.BlockSpec((w.shape[0] // parts, w.shape[1]), lambda i, b: (place_of(b, names), 0))
        for w in weights
    ]
    total = sum(w.size for w in weights) // parts // STRIP
    return call(
        kernel,
        "pack",
        bits,
        [in_hbm(w) for w in weights],
        specs,
        [vmem((total, STRIP))],
        [IN_VMEM],
        (1,),
        dep,
    )[0]


def pack_tile(weight, row_names, column_names, bits, dep):
    def kernel(bits_ref, ins, outs):
        at = pl.multiple_of(pl.program_id(0) * tall, 8)
        outs[0][pl.ds(at, tall), :] = ins[0][...].astype(f32)

    dims = (weight.shape[0] >> len(row_names), weight.shape[1] >> len(column_names))
    steps = max(1, dims[0] // 384)
    tall = dims[0] // steps
    return call(
        kernel,
        "pack_tile",
        bits,
        [weight],
        [
            pl.BlockSpec(
                (tall, dims[1]),
                lambda i, b: (place_of(b, row_names) * steps + i, place_of(b, column_names)),
            )
        ],
        [vmem(dims)],
        [IN_VMEM],
        (steps,),
        dep,
    )[0]


def touch(array, bits, dep):
    count = len(dep)

    def body(bits_ref, *refs):
        pass

    anywhere = pl.BlockSpec(memory_space=pl.ANY)
    result, token = pl.pallas_call(
        body,
        in_specs=[pl.BlockSpec(memory_space=pltpu.SMEM)] + [anywhere] * (1 + count),
        out_specs=[anywhere] * 2,
        out_shape=[shape(array.shape, array.dtype), pltpu.HBM(TOKEN, f32)],
        input_output_aliases={1: 0},
        compiler_params=pltpu.CompilerParams(vmem_limit_bytes=MIB),
        cost_estimate=pl.CostEstimate(flops=0, bytes_accessed=0, transcendentals=0),
        name="touch",
    )(bits, array, *map(in_hbm, dep))
    dep[:] = [token]
    return result


def join(first, second, bits, dep):
    rows, columns = first.shape

    def kernel(bits_ref, ins, outs):
        for k in range(2):
            outs[0][k * rows : (k + 1) * rows, :] = ins[k][...]

    return whole_call(kernel, "join", bits, [first, second], [vmem((2 * rows, columns))], dep)[0]


def half_masks():
    lane = lax.broadcasted_iota(jnp.int32, (1, 2 * HEAD), 1)
    low = jnp.where(lane < HEAD, 1.0, 0.0).astype(bf16)
    return (low, (1.0 - low.astype(f32)).astype(bf16))


def region_masks(row_ref, col_ref):
    across = row_ref[0]
    down = col_ref[...]
    same = down == across
    live = down >= 0
    size = down.shape[0]
    diagonal = lax.broadcasted_iota(jnp.int32, (size, size), 0) == lax.broadcasted_iota(
        jnp.int32, (size, size), 1
    )
    pairs = same & live
    return pairs, pairs | diagonal


def probabilities(scores, allowed):
    masked = jnp.where(allowed, scores, big_negative)
    top = jnp.max(masked, axis=-1, keepdims=True)
    expo = jnp.exp(masked - top)
    total = jnp.sum(expo, axis=-1, keepdims=True)
    return expo * (1.0 / total)


def attention(parts, allowed, masks, scale, write):
    width = parts[0].shape[1]
    for at in range(0, width, 2 * HEAD):
        query, keys, values = (part[:, at : at + 2 * HEAD] for part in parts)
        probs = [
            probabilities(dot_nt(query * mask, keys) * scale, allowed).astype(bf16) for mask in masks
        ]
        stacked = jnp.concatenate([values * mask for mask in masks], axis=0)
        write(at, dot_nn(jnp.concatenate(probs, axis=1), stacked).astype(bf16))


def attend_own(x, weights, biases, seg_row, seg_col, bits, dep):
    rows, dim = x.shape
    width = weights[0].shape[1]

    def kernel(bits_ref, ins, outs):
        x_ref, bias_ref, row_ref, col_ref = ins[:4]
        tokens = x_ref[...]
        pairs, allowed = region_masks(row_ref, col_ref)
        masks = half_masks()
        for net in range(2):
            parts = []
            for k in range(3):
                row = 3 * net + k
                part = dot_nn(tokens, ins[4 + row][...]) + bias_ref[row : row + 1, :]
                parts.append(part.astype(bf16))
                if row < 5:
                    outs[0][:, row * width : (row + 1) * width] = parts[k]

            def write(at, mixed, net=net):
                outs[1 + net][:, at : at + 2 * HEAD] = mixed

            attention(parts, allowed, masks, HEAD ** (-0.5), write)

    def block(columns):
        return pl.BlockSpec((REGION, columns), lambda i, b: (i, 0))

    return call(
        kernel,
        "attend_own",
        bits,
        [x, biases, seg_row, seg_col, *weights],
        [
            block(dim),
            fixed(biases.shape),
            pl.BlockSpec((1, 1, REGION), lambda i, b: (i, 0, 0)),
            block(1),
        ]
        + [fixed(w.shape) for w in weights],
        [shape((rows, 5 * width), bf16), shape((rows, width), bf16), shape((rows, width), bf16)],
        [block(5 * width), block(width), block(width)],
        (rows // REGION,),
        dep,
    )


def attend_other(
    x, pieces, names, biases, seg_row, seg_col, mixed, output, model, student, bits, dep
):
    rows, dim = x.shape
    width = mixed.shape[1]
    parts = 2 ** len(names)
    half_parts = parts // 2
    tall = dim // parts
    short = width // parts
    per_part = 3 * tall + 2 * short
    first_row = 0 if student else 3
    kept = 3 if student else 2

    def kernel(bits_ref, ins, outs):
        x_ref, bias_ref, row_ref, col_ref, mine_ref, theirs_ref, mixed_ref, out_ref, model_ref = ins
        qkv_ref, low_ref, first_ref = outs[:3]
        weight_refs = outs[5:9] if student else outs[3:7]
        part = place_of(bits_ref, names)

        @pl.when(pl.program_id(0) == 0)
        def _():
            for k in range(parts):
                ref = (mine_ref, theirs_ref)[k // half_parts]
                base = (k % half_parts) * per_part
                where = jnp.bitwise_xor(part, k)
                for m in range(3):
                    weight_refs[m][pl.ds(pl.multiple_of(where * tall, 16), tall), :] = ref[
                        base + m * tall : base + (m + 1) * tall, :
                    ].astype(bf16)
                for m in range(2):
                    at = base + 3 * tall + m * short
                    weight_refs[3][
                        pl.ds(pl.multiple_of(where * short, 16), short), m * STRIP : (m + 1) * STRIP
                    ] = ref[at : at + short, :].astype(bf16)

        tokens = x_ref[...]
        pairs, allowed = region_masks(row_ref, col_ref)
        masks = half_masks()
        parts_qkv = []
        for k in range(3):
            row = first_row + k
            part_k = dot_nn(tokens, weight_refs[k][...]) + bias_ref[row : row + 1, :]
            parts_qkv.append(part_k.astype(bf16))
            if k < kept:
                qkv_ref[:, k * width : (k + 1) * width] = parts_qkv[k]
        tiles = []
        attention(parts_qkv, allowed, masks, HEAD ** (-0.5), lambda at, tile: tiles.append(tile))
        mine = jnp.concatenate(tiles, axis=1)
        pre = (
            tokens.astype(f32)
            + (dot_nn(mixed_ref[...], out_ref[...]) + dot_nn(mine, weight_refs[3][...]))
            + model_ref[0:1, :]
        )
        unit, scale = normalize(pre)
        first = unit * (1.0 + model_ref[2:3, :]) + model_ref[3:4, :]
        low_ref[...] = first.astype(bf16)
        first_ref[...] = first
        if student:
            outs[3][...] = mine
            outs[4][...] = pre

    def block(columns):
        return pl.BlockSpec((REGION, columns), lambda i, b: (i, 0))

    weights = [shape((dim, width), bf16)] * 3 + [shape((width, dim), bf16)]
    outs = [shape((rows, kept * width), bf16), shape((rows, dim), bf16), shape((rows, dim))]
    out_specs = [block(kept * width), block(dim), block(dim)]
    if student:
        outs += [shape((rows, width), bf16), hbm((rows, dim))]
        outs += [hbm(w.shape, bf16) for w in weights]
        out_specs += [block(width), block(dim)] + [fixed(w.shape) for w in weights]
    return call(
        kernel,
        "attend_other",
        bits,
        [x, biases, seg_row, seg_col, *map(pin, pieces), mixed, output, model],
        [
            block(dim),
            fixed(biases.shape),
            pl.BlockSpec((1, 1, REGION), lambda i, b: (i, 0, 0)),
            block(1),
            IN_VMEM,
            IN_VMEM,
            block(width),
            fixed(output.shape),
            fixed(model.shape),
        ],
        outs,
        out_specs,
        (rows // REGION,),
        dep,
        limit=24,
        scratch=[] if student else [pltpu.VMEM(w.shape, bf16) for w in weights],
    )


def activate(up, outs, student):
    cdf = cdf_of(up)
    outs[0][...] = (up * cdf).astype(bf16)
    if student:
        bell = jnp.exp(-0.5 * up * up) * (2.0 * jnp.pi) ** -0.5
        outs[1][...] = (cdf + up * bell).astype(bf16)


def up_own(low, weight, biases, first_row, student, bits, dep):
    tokens, dim = low.shape
    hidden = weight.shape[1]

    def kernel(bits_ref, ins, outs):
        j = pl.program_id(0)
        up = dot_nn(ins[0][...], ins[1][...]) + ins[2][pl.ds(first_row + j, 1), :]
        activate(up, outs, student)

    count = 2 if student else 1
    return call(
        kernel,
        "up_own",
        bits,
        [low, weight, biases],
        [fixed(low.shape), pl.BlockSpec((dim, STRIP), lambda j, b: (0, j)), fixed(biases.shape)],
        [shape((tokens, hidden), bf16), hbm((tokens, hidden), bf16)][:count],
        [pl.BlockSpec((tokens, STRIP), lambda j, b: (0, j))] * count,
        (hidden // STRIP,),
        dep,
    )


def up_other(low, mine, theirs, names, biases, first_row, student, bits, dep):
    tokens, dim = low.shape
    steps = mine.shape[0] // STRIP
    half = dim // 2

    def kernel(bits_ref, ins, outs):
        low_ref, tile_m, tile_o, bias_ref = ins
        j = jnp.bitwise_xor(pl.program_id(0), place_of(bits_ref, names))
        at = pl.ds(pl.multiple_of(pl.program_id(0) * half, 8), half)
        weight_ref = outs[2] if student else outs[1]
        core = bits_ref[C]
        weight_ref[pl.ds(pl.multiple_of(core * half, 16), half), :] = tile_m[at, :].astype(bf16)
        weight_ref[pl.ds(pl.multiple_of((1 - core) * half, 16), half), :] = tile_o[at, :].astype(bf16)
        up = dot_nn(low_ref[...], weight_ref[...]) + bias_ref[pl.ds(first_row + j, 1), :]
        activate(up, outs, student)

    def column(j, b):
        return (0, jnp.bitwise_xor(j, place_of(b, names)))

    outs = [shape((tokens, steps * STRIP), bf16)]
    out_specs = [pl.BlockSpec((tokens, STRIP), column)]
    if student:
        outs += [hbm((tokens, steps * STRIP), bf16), hbm((dim, steps * STRIP), bf16)]
        out_specs += [out_specs[0], pl.BlockSpec((dim, STRIP), column)]
    return call(
        kernel,
        "up_other",
        bits,
        [low, pin(mine), pin(theirs), biases],
        [fixed(low.shape), IN_VMEM, IN_VMEM, fixed(biases.shape)],
        outs,
        out_specs,
        (steps,),
        dep,
        limit=16,
        scratch=[] if student else [pltpu.VMEM((dim, STRIP), bf16)],
    )


def down_own(acts, weights, firsts, models, bits, dep):
    tokens, hidden = acts[0].shape
    dim = weights[0].shape[1]

    def kernel(bits_ref, ins, outs):
        for net in range(2):
            act, weight, first, model = ins[4 * net : 4 * net + 4]
            outs[net][...] = first[...] + model[1:2, :] + dot_nn(act[...], weight[...])

    def block(columns):
        return pl.BlockSpec((REGION, columns), lambda i, b: (i, 0))

    arrays = []
    specs = []
    for net in range(2):
        arrays += [acts[net], weights[net], firsts[net], models[net]]
        specs += [block(hidden), fixed((hidden, dim)), block(dim), fixed(models[net].shape)]
    return call(
        kernel,
        "down_own",
        bits,
        arrays,
        specs,
        [shape((tokens, dim))] * 2,
        [block(dim)] * 2,
        (tokens // REGION,),
        dep,
        limit=24,
    )


def down_other(acts, student_tiles, teacher_tiles, names, partials, models, seg_col, bits, dep):
    tokens, hidden = acts[0].shape
    dim = partials[0].shape[1]
    half = dim // 2
    steps = hidden // STRIP

    def kernel(bits_ref, ins, outs):
        act_s, act_t, s_mine, s_other, t_mine, t_other, part_s, part_t, model_s, model_t, seg = ins
        out_ref, pre_ref, down_ref, sums_ref, weight_ref, low_ref, teacher_ref = outs
        step = pl.program_id(0)
        first_core = bits_ref[C] == 0

        @pl.when(step == 0)
        def _():
            place = place_of(bits_ref, names)
            for k in range(steps):
                rows = slice(k * STRIP, (k + 1) * STRIP)
                where = pl.ds(pl.multiple_of(jnp.bitwise_xor(place, k) * STRIP, 16), STRIP)
                tile, other = s_mine[rows, :].astype(bf16), s_other[rows, :].astype(bf16)
                weight_ref[where, :half] = jnp.where(first_core, tile, other)
                weight_ref[where, half:] = jnp.where(first_core, other, tile)
                tile, other = t_mine[rows, :].astype(bf16), t_other[rows, :].astype(bf16)
                teacher_ref[rows, :half] = jnp.where(first_core, tile, other)
                teacher_ref[rows, half:] = jnp.where(first_core, other, tile)

        unit_s, scale_s = normalize(part_s[...] + dot_nn(act_s[...], weight_ref[...]))
        unit_t, _ = normalize(part_t[...] + dot_nn(act_t[...], teacher_ref[...]))
        gain = model_s[4:5, :]
        out_s = unit_s * (1.0 + gain) + model_s[5:6, :]
        out_t = unit_t * (1.0 + model_t[4:5, :]) + model_t[5:6, :]
        out_ref[...] = out_s
        low_ref[0] = out_s.astype(bf16)
        grad = jnp.where(seg[...] >= 0, out_s - out_t, 0.0)
        d_pre = norm_back(grad, unit_s, scale_s, gain)
        pre_ref[...] = d_pre
        low = d_pre.astype(bf16)
        down_ref[...] = low
        add_sums(sums_ref, (grad * unit_s, grad, low.astype(f32)), step)

    def block(columns):
        return pl.BlockSpec((REGION, columns), lambda i, b: (i, 0))

    return call(
        kernel,
        "down_other",
        bits,
        [*acts, *map(pin, student_tiles), *map(pin, teacher_tiles), *partials, *models, seg_col],
        [block(hidden)] * 2
        + [IN_VMEM] * 4
        + [block(dim)] * 2
        + [fixed(m.shape) for m in models]
        + [block(1)],
        [
            shape((tokens, dim)),
            shape((tokens, dim)),
            shape((tokens, dim), bf16),
            shape((8, dim)),
            hbm((hidden, dim), bf16),
            hbm((2, tokens, dim), bf16),
        ],
        [
            block(dim),
            block(dim),
            block(dim),
            fixed((8, dim)),
            fixed((hidden, dim)),
            pl.BlockSpec((1, REGION, dim), lambda i, b: (b[SIDE], i, 0)),
        ],
        (tokens // REGION,),
        dep,
        limit=28,
        scratch=[pltpu.VMEM((hidden, dim), bf16)],
    )


def up_back(d_down, weights, slopes, bits, dep):
    tokens, dim = d_down.shape
    hidden = weights[0].shape[0]

    def kernel(bits_ref, ins, outs):
        rows = []
        for half in range(2):
            grad = dot_nt(ins[0][...], ins[1 + half][...])
            low = (grad * ins[3 + half][...].astype(f32)).astype(bf16)
            outs[half][...] = low
            rows.append(jnp.sum(low.astype(f32), axis=0, keepdims=True))
        outs[2][...] = jnp.concatenate(rows + [jnp.zeros((6, STRIP), f32)], axis=0)

    block = pl.BlockSpec((tokens, STRIP), lambda j, b: (0, j))
    return call(
        kernel,
        "up_back",
        bits,
        [d_down, *weights, *slopes],
        [fixed(d_down.shape)] + [pl.BlockSpec((STRIP, dim), lambda j, b: (j, 0))] * 2 + [block] * 2,
        [shape((tokens, hidden), bf16)] * 2 + [shape((8, hidden))],
        [block, block, pl.BlockSpec((8, STRIP), lambda j, b: (0, j))],
        (hidden // STRIP,),
        dep,
    )


def add_sums(ref, arrays, step):
    rows = [jnp.sum(v, axis=0, keepdims=True) for v in arrays]
    rows.append(jnp.zeros((8 - len(rows), rows[0].shape[1]), f32))
    new = jnp.concatenate(rows, axis=0)
    ref[...] = jnp.where(step == 0, new, ref[...] + new)


def first_back(d_ups, weights, d_pre2, pre, model, outputs, bits, dep):
    tokens, hidden = d_ups[0].shape
    dim = d_pre2.shape[1]
    width = outputs[0].shape[0]

    def kernel(bits_ref, ins, outs):
        d_own, d_oth, w_own, w_oth, d_pre2_ref, pre_ref, model_ref, o_own, o_oth = ins
        grad = d_pre2_ref[...] + (dot_nt(d_own[...], w_own[...]) + dot_nt(d_oth[...], w_oth[...]))
        unit, scale = normalize(pre_ref[...])
        d_pre = norm_back(grad, unit, scale, model_ref[2:3, :])
        outs[0][...] = d_pre
        low = d_pre.astype(bf16)
        outs[1][...] = low
        outs[2][...] = dot_nt(low, o_own[...]).astype(bf16)
        outs[3][...] = dot_nt(low, o_oth[...]).astype(bf16)
        add_sums(outs[4], (grad * unit, grad, low.astype(f32)), pl.program_id(0))

    def block(columns):
        return pl.BlockSpec((REGION, columns), lambda i, b: (i, 0))

    return call(
        kernel,
        "first_back",
        bits,
        [*d_ups, *weights, d_pre2, pre, model, *outputs],
        [block(hidden)] * 2
        + [fixed(w.shape) for w in weights]
        + [block(dim)] * 2
        + [fixed(model.shape)]
        + [fixed(o.shape) for o in outputs],
        [
            shape((tokens, dim)),
            shape((tokens, dim), bf16),
            shape((tokens, width), bf16),
            shape((tokens, width), bf16),
            shape((8, dim)),
        ],
        [block(dim), block(dim), block(width), block(width), fixed((8, dim))],
        (tokens // REGION,),
        dep,
        limit=28,
    )


def token_grad(d_pre, terms, bits, dep):
    tokens, dim = d_pre.shape

    def kernel(bits_ref, ins, outs):
        total = ins[0][...]
        for k in range(len(terms)):
            total = total + dot_nt(ins[1 + 2 * k][...], ins[2 + 2 * k][...])
        outs[0][...] = total
        outs[1][0] = total

    arrays = [d_pre]
    specs = [pl.BlockSpec((REGION, dim), lambda i, b: (i, 0))]
    for grad, at, weight in terms:
        arrays += [grad, weight]
        specs += [
            pl.BlockSpec((REGION, weight.shape[1]), lambda i, b, at=at: (i, at)),
            fixed(weight.shape),
        ]
    return call(
        kernel,
        "token_grad",
        bits,
        arrays,
        specs,
        [shape((tokens, dim)), pltpu.HBM((2, tokens, dim), f32)],
        [specs[0], pl.BlockSpec((1, REGION, dim), lambda i, b: (b[SIDE], i, 0))],
        (tokens // REGION,),
        dep,
    )


def attend_back(qkv, grads, seg_row, seg_col, bits, dep):
    rows, columns = qkv[0].shape
    width = columns // 5
    step = 2 * HEAD

    def kernel(bits_ref, ins, outs):
        pairs, allowed = region_masks(ins[5], ins[6])
        weight = jnp.where(pairs, score_weight, 0.0)
        masks = half_masks()
        scale = HEAD ** (-0.5)

        @pl.when(pl.program_id(0) == 0)
        def _():
            outs[4][...] = jnp.zeros_like(outs[4])

        for part in range(2):
            for at in range(0, width, step):
                places = [(0, k) for k in range(5)] if part == 0 else [(1, 0), (1, 1), (1, 2), (2, 0), (2, 1)]
                query, keys, values, query_t, keys_t = (
                    ins[r][:, k * width + at : k * width + at + step] for r, k in places
                )
                grad = ins[3 + part][:, at : at + step]
                probs = []
                slopes = []
                for mask in masks:
                    scores = dot_nt(query * mask, keys) * scale
                    prob = probabilities(scores, allowed)
                    gap = scores - dot_nt(query_t * mask, keys_t) * scale
                    d_prob = dot_nt(grad * mask, values)
                    mean = jnp.sum(prob * d_prob, axis=-1, keepdims=True)
                    slope = prob * (d_prob - mean) + weight * gap
                    probs.append(prob.astype(bf16))
                    slopes.append(slope.astype(bf16))

                def both(array):
                    return jnp.concatenate([array * mask for mask in masks], axis=0)

                d_query = dot_nn(jnp.concatenate(slopes, axis=1), both(keys)) * scale
                d_keys = dot_tn(jnp.concatenate(slopes, axis=0), both(query)) * scale
                d_values = dot_tn(jnp.concatenate(probs, axis=0), both(grad))
                for k, result in enumerate((d_query, d_keys, d_values)):
                    low = result.astype(bf16)
                    if k < 2:
                        outs[part][:, k * width + at : k * width + at + step] = low
                    else:
                        outs[2 + part][:, at : at + step] = low
                    outs[4][part : part + 1, k * width + at : k * width + at + step] += jnp.sum(
                        low.astype(f32), axis=0, keepdims=True
                    )

    def block(columns):
        return pl.BlockSpec((REGION, columns), lambda i, b: (i, 0))

    return call(
        kernel,
        "attend_back",
        bits,
        [*qkv, *grads, seg_row, seg_col],
        [
            block(columns),
            block(3 * width),
            block(2 * width),
            block(width),
            block(width),
            pl.BlockSpec((1, 1, REGION), lambda i, b: (i, 0, 0)),
            block(1),
        ],
        [shape((rows, 2 * width), bf16)] * 2
        + [shape((rows, width), bf16)] * 2
        + [shape((8, 3 * width))],
        [block(2 * width)] * 2 + [block(width)] * 2 + [fixed((8, 3 * width))],
        (rows // REGION,),
        dep,
    )


def outer(groups, bits, dep, start=0, size=None, block=384):
    size = size or groups[0][0][0].shape[1]
    tall = size // 2
    steps = tall // block
    tokens = groups[0][0][0].shape[0]
    arrays = []
    specs = []
    for lhs, rhs, at, columns in groups:
        for half in range(2):

            def left(p, h, i, b, half=half, lhs=lhs):
                core = jnp.where(p == 0, 1 - b[C], b[C])
                where = start // block + core * steps + i
                return (0, where if lhs[0] is lhs[1] else jnp.where(h == half, where, start // block))

            arrays += [lhs[half], rhs[half]]
            specs += [
                pl.BlockSpec((tokens, block), left),
                pl.BlockSpec((tokens, columns), lambda p, h, i, b, at=at: (0, at)),
            ]
    wide = sum(g[3] for g in groups)

    def kernel(bits_ref, ins, outs):
        for phase in range(2):
            for half in range(2):

                @pl.when((pl.program_id(0) == phase) & (pl.program_id(1) == half))
                def _(phase=phase, half=half):
                    at = 0
                    row = pl.multiple_of(pl.program_id(2) * block, 8)
                    for k, group in enumerate(groups):
                        lhs, rhs = ins[4 * k + 2 * half], ins[4 * k + 2 * half + 1]
                        outs[phase][half, pl.ds(row, block), at : at + group[3]] = dot_tn(
                            lhs[...], rhs[...]
                        )
                        at += group[3]

    out = vmem((2, tall, wide))
    return call(
        kernel, "outer", bits, arrays, specs, [out, out], [IN_VMEM, IN_VMEM], (2, 2, steps), dep, limit=16
    )


def split(first, second, name, bits, dep, limit=16):
    halves, rows, columns = first.shape
    out = vmem((1, rows, columns)) if name == "x" else vmem((halves, rows // 2, columns))

    def kernel(bits_ref, ins, outs):
        for k in range(2):
            if name == "x":
                where = (pl.ds(1 - k, 1), slice(None))
            else:
                bit = bits_ref[name]
                start = (1 - bit if k == 0 else bit) * (rows // 2)
                where = (slice(None), pl.ds(pl.multiple_of(start, 8), rows // 2))
            outs[k][...] = ins[0][where] + ins[1][where]

    return whole_call(kernel, "split", bits, [first, second], [out, out], dep, limit)


def add(first, second, bits, dep):
    def kernel(bits_ref, ins, outs):
        outs[0][...] = ins[0][...] + ins[1][...]

    return whole_call(kernel, "add", bits, [first, second], [vmem(first.shape)], dep)[0]


def merge(mine, theirs, name, bits, dep):
    one, rows, columns = mine.shape

    def kernel(bits_ref, ins, outs):
        bit = bits_ref[name]
        for k in range(2):
            start = (bit if k == 0 else 1 - bit) * rows
            outs[0][:, pl.ds(pl.multiple_of(start, 8), rows)] = ins[k][...]

    return whole_call(kernel, "merge", bits, [mine, theirs], [vmem((1, 2 * rows, columns))], dep)[0]


def finish(pieces, cuts, outs, bits, dep, into=None):
    def kernel(bits_ref, ins, refs):
        results, sems = refs[:-1], refs[-1]
        copies = []
        for k, (piece, source, out, target) in enumerate(cuts):
            copy = pltpu.make_async_copy(
                ins[piece].at[source], results[out].at[target(bits_ref)], sems.at[k]
            )
            copy.start()
            copies.append(copy)
        for copy in copies:
            copy.wait()

    return invoke(
        kernel,
        "finish",
        bits,
        [*map(pin, pieces)],
        [IN_VMEM] * len(pieces),
        [pltpu.HBM(o.shape, o.dtype) for o in outs],
        [pl.BlockSpec(memory_space=pl.ANY)] * len(outs),
        dep,
        8,
        None,
        [pltpu.SemaphoreType.DMA((len(cuts),))],
        into,
    )


def flip(array, bits, dep):
    def kernel(bits_ref, ins, outs):
        outs[0][...] = ins[0][0].T

    one, rows, columns = array.shape
    return whole_call(kernel, "flip", bits, [array], [vmem((columns, rows))], dep)[0]


def put_rows(array, bits, dep, into):
    two, rows, dim = into.shape
    tall = rows // 4

    def kernel(bits_ref, ins, outs):
        at = pl.ds(pl.multiple_of(pl.program_id(0) * tall, 8), tall)
        outs[-1][0] = ins[0][at, :].astype(into.dtype)

    return call(
        kernel,
        "place",
        bits,
        [pin(array)],
        [IN_VMEM],
        [pltpu.HBM(into.shape, into.dtype)],
        [pl.BlockSpec((1, tall, dim), lambda i, b: (1 - b[SIDE], i, 0))],
        (4,),
        dep,
        into=into,
    )[0]


def collect(sums, other, bits, dep):
    wide = sum(s.shape[1] for s in sums)

    def kernel(bits_ref, ins, outs):
        at = 0
        for k, ref in enumerate(ins):
            columns = ref.shape[1]
            if other and k < 2:
                both = jnp.concatenate([ref[1:2, :], ref[0:1, :], ref[2:, :]], axis=0)
            else:
                both = ref[...]
            outs[0][:, at : at + columns] = both
            at += columns

    return whole_call(kernel, "collect", bits, sums, [vmem((8, wide))], dep)[0]


R0, R1, E0, E1, QK, VO, SUMS = range(7)
(
    DO_B0,
    DO_B1,
    DO_BIN_A,
    DO_BIN_E,
    DO_BIN_R,
    DO_ATT_O,
    DO_KBT,
    DO_KBS,
    DO_UP_OT,
    DO_UP_OS,
    DO_UP_XT,
    DO_UP_XS,
    DO_DN_O,
    DO_KD,
    DO_S,
    DO_TT,
    DO_SF,
    DO_TF,
    DO_DU,
    DO_DH1,
    DO_ATT,
    DO_TOK,
    DO_O_R0,
    DO_O_R1,
    DO_O_E0,
    DO_O_E1,
    DO_O_QK,
    DO_O_VO,
) = range(28)
OUTERS = (DO_O_R0, DO_O_R1, DO_O_E0, DO_O_E1, DO_O_QK, DO_O_VO)
CHUNK_STEP, FETCH_STEP = 50, 60
PATHS = {
    R0: (Y, ZL, "x", ZH),
    R1: ("x", Y, ZL, ZH),
    E0: ("x", Y, ZL, ZH),
    E1: (ZL, "x", Y, ZH),
    QK: (ZL, "x", Y, ZH),
    VO: (Y, "x", ZL, ZH),
}
FETCH = ((ZL,), (ZL, Y), (ZL, Y), (Y, ZL), (ZL, Y))
ORDER = (
    FETCH_STEP + 3, DO_BIN_A, FETCH_STEP + 1, FETCH_STEP + 2, DO_BIN_E, FETCH_STEP + 4,
    FETCH_STEP + 3, DO_BIN_R, FETCH_STEP + 5, FETCH_STEP + 6, FETCH_STEP + 2, FETCH_STEP + 3,
    DO_B0, FETCH_STEP + 2, FETCH_STEP + 1, FETCH_STEP + 3, DO_ATT_O, FETCH_STEP + 5,
    FETCH_STEP + 4, DO_B1, FETCH_STEP + 1, FETCH_STEP + 2, FETCH_STEP + 1, DO_KBT,
    FETCH_STEP + 3, DO_UP_XT, FETCH_STEP + 4, FETCH_STEP + 2, FETCH_STEP + 5, DO_UP_OT, DO_KBS,
    DO_UP_OS, DO_DN_O, FETCH_STEP + 4, FETCH_STEP + 5, FETCH_STEP + 6, FETCH_STEP + 4,
    DO_UP_XS, FETCH_STEP + 5, FETCH_STEP + 6, DO_KD, DO_O_R0, CHUNK_STEP + R0, DO_O_R1,
    CHUNK_STEP + R1, DO_DU, DO_O_E1, CHUNK_STEP + E1, CHUNK_STEP + R1, CHUNK_STEP + R0,
    CHUNK_STEP + E1, DO_DH1, DO_O_E0, DO_ATT, DO_O_VO, CHUNK_STEP + R0, CHUNK_STEP + R1, DO_S,
    CHUNK_STEP + E1, DO_O_QK, DO_TOK, CHUNK_STEP + SUMS, CHUNK_STEP + QK, CHUNK_STEP + E0,
    CHUNK_STEP + E1, CHUNK_STEP + R1, CHUNK_STEP + R0, CHUNK_STEP + VO, CHUNK_STEP + E0,
    CHUNK_STEP + QK, CHUNK_STEP + SUMS, CHUNK_STEP + E1, CHUNK_STEP + R1, CHUNK_STEP + VO,
    CHUNK_STEP + SUMS, CHUNK_STEP + E0, CHUNK_STEP + R1, CHUNK_STEP + QK, CHUNK_STEP + R0,
    CHUNK_STEP + VO, CHUNK_STEP + SUMS, DO_TT, CHUNK_STEP + R1, CHUNK_STEP + QK,
    CHUNK_STEP + E1, CHUNK_STEP + E0, CHUNK_STEP + SUMS, CHUNK_STEP + R0, CHUNK_STEP + VO,
    CHUNK_STEP + E0, CHUNK_STEP + VO, CHUNK_STEP + R1, CHUNK_STEP + QK, CHUNK_STEP + E0,
    CHUNK_STEP + R0, CHUNK_STEP + E1, CHUNK_STEP + VO, CHUNK_STEP + E0, DO_TF, CHUNK_STEP + R0,
    CHUNK_STEP + QK, CHUNK_STEP + E0, CHUNK_STEP + QK, CHUNK_STEP + VO, CHUNK_STEP + E1,
    CHUNK_STEP + E0, CHUNK_STEP + E1, DO_SF, CHUNK_STEP + QK, CHUNK_STEP + VO, CHUNK_STEP + R0,
    CHUNK_STEP + R1, CHUNK_STEP + VO, CHUNK_STEP + SUMS, CHUNK_STEP + QK,
)


def on_device(n_wide, tokens, segments, *params):
    (w_q, w_k, w_v, w_o, w_e, w_r, heads_s, model_s, hidden_s) = params[:9]
    (t_q, t_k, t_v, t_o, t_e, t_r, heads_t, model_t, hidden_t) = params[9:]
    n_bits = n_wide.bit_length() - 1
    side = lax.axis_index("narrow")
    place = lax.axis_index("wide")
    bits = jnp.stack([(place >> b) & 1 for b in range(4)] + [side]).astype(jnp.int32)
    dim, width = w_q.shape
    hidden = w_e.shape[1]

    def swap(array, bit):
        if bit == "x":
            return lax.ppermute(array, "narrow", [(0, 1), (1, 0)])
        return lax.ppermute(array, "wide", [(i, i ^ (1 << bit)) for i in range(n_wide)])

    x = lax.dynamic_index_in_dim(tokens, side, 0, keepdims=False)
    segment = lax.dynamic_index_in_dim(segments, side, 0, keepdims=False)
    rows = x.shape[0]
    seg_row = segment.reshape(rows // REGION, 1, REGION)
    seg_col = segment.reshape(rows, 1)
    biases = jnp.concatenate(
        [heads_s, heads_t, hidden_s.reshape(-1, width), hidden_t.reshape(-1, width)]
    )
    blocks = hidden // width
    models = (model_s, model_t)
    half = hidden // 2

    v = types.SimpleNamespace()
    fetched = {}
    last = []

    def fetch(key, made, path):
        held = swap(made(), "x")
        yield
        held = touch(held, bits, last)
        for name in path:
            got = swap(held, name)
            yield
            held = join(held, got, bits, last)
        got = swap(held, C)
        yield
        fetched[key] = (held, touch(got, bits, last))
        yield

    def fetch_direct(key, made):
        zero = swap(made(), "x")
        yield
        zero = touch(zero, bits, last)
        got = swap(zero, C)
        yield
        fetched[key] = (zero, touch(got, bits, last))
        yield

    def reduce_chunk(made, path):
        send, keep = made
        got = swap(touch(send, bits, last), C)
        yield
        for name in path[:-1]:
            send, keep = split(keep, got, name, bits, last)
            got = swap(send, name)
            yield
        block = add(keep, got, bits, last)
        got = swap(block, path[-1])
        yield
        for extra in range(4, n_bits):
            block = block + got
            got = swap(block, extra)
        block = add(block, got, bits, last)
        back = [name for name in reversed(path[:-1]) if name != "x"] + [C]
        for name in back[:-1]:
            got = swap(block, name)
            yield
            block = merge(block, got, name, bits, last)
        got = swap(block, C)
        yield
        yield (block, got)

    def small_sums():
        sums = [v.sums_qkv, v.sums_up, v.sums1, v.sums2]
        total = collect(sums, False, bits, last)
        got = swap(collect(sums, True, bits, last), "x")
        yield
        for b in range(4):
            total = add(total, got, bits, last)
            got = swap(total, b)
            yield
        total = add(total, got, bits, last)
        for b in range(4, n_bits):
            total = total + swap(total, b)
        yield total

    tall = dim // 2
    steps = {}
    fetching = {}
    outs = types.SimpleNamespace(reduce=None, expand=None)

    def names_of(k):
        return (C, *reversed(FETCH[k - 1]))

    def start_fetch(k):
        names = names_of(k)
        makers = {
            1: lambda: pack([t_q, t_k, t_v, t_o], names, bits, last),
            2: lambda: touch(v.b_pack, bits, last),
            3: lambda: pack_tile(in_hbm(t_e), (C,), names[1:], bits, last),
            4: lambda: pack_tile(v.b_e, (C,), names[1:], bits, last),
            5: lambda: pack_tile(v.b_r, names[1:], (C,), bits, last),
        }
        return fetch(k, makers[k], FETCH[k - 1])

    def do(name):
        if name == DO_B0:
            v.biases_oth = swap(touch(biases, bits, last), "x")
        elif name == DO_B1:
            v.biases_oth = touch(v.biases_oth, bits, last)
        elif name == DO_BIN_A:
            *v.b, v.b_pack = binarize_pack(
                [w_q, w_k, w_v, w_o], (0, 0, 0, 1), names_of(2), bits, last
            )
        elif name == DO_BIN_E:
            v.b_e = binarize(w_e, 0, bits, last)
        elif name == DO_BIN_R:
            v.b_r = binarize(w_r, 1, bits, last)
        elif name == DO_ATT_O:
            b = v.b
            v.qkv_own, *v.mixed_own = attend_own(
                x,
                (b[0], b[1], b[2], in_hbm(t_q), in_hbm(t_k), in_hbm(t_v)),
                biases,
                seg_row,
                seg_col,
                bits,
                last,
            )
        elif name == DO_KBT:
            v.qk_t, v.low_t, v.first_t = attend_other(
                x,
                fetched[1],
                names_of(1),
                v.biases_oth,
                seg_row,
                seg_col,
                v.mixed_own[1],
                t_o,
                model_t,
                False,
                bits,
                last,
            )
        elif name == DO_KBS:
            v.qkv_oth, v.low_s, v.first_s, v.mixed_oth, v.pre_s, *v.o = attend_other(
                x,
                fetched[2],
                names_of(2),
                v.biases_oth,
                seg_row,
                seg_col,
                v.mixed_own[0],
                v.b[3],
                model_s,
                True,
                bits,
                last,
            )
        elif name == DO_UP_OT:
            (v.act_t_own,) = up_own(v.low_t, t_e, biases, 6 + blocks, False, bits, last)
        elif name == DO_UP_OS:
            v.act_s_own, v.slope_own = up_own(
                v.low_s, v.b_e, biases, 6, True, bits, last
            )
        elif name == DO_UP_XT:
            (v.act_t_oth,) = up_other(
                v.low_t, *fetched[3], names_of(3)[1:], v.biases_oth, 6 + blocks, False, bits, last
            )
        elif name == DO_UP_XS:
            v.act_s_oth, v.slope_oth, v.o_e = up_other(
                v.low_s, *fetched[4], names_of(4)[1:], v.biases_oth, 6, True, bits, last
            )
        elif name == DO_DN_O:
            v.partials = down_own(
                (v.act_s_own, v.act_t_own),
                (v.b_r, t_r),
                (v.first_s, v.first_t),
                models,
                bits,
                last,
            )
        elif name == DO_KD:
            v.out_s, v.d_pre2, v.d_down, v.sums2, v.o_r, v.out_low = down_other(
                (v.act_s_oth, v.act_t_oth),
                fetched[5],
                fetched[6],
                names_of(5)[1:],
                v.partials,
                models,
                seg_col,
                bits,
                last,
            )
        elif name == DO_S:
            v.out_other = swap(touch(v.out_s, bits, last), "x")
        elif name == DO_TT:
            v.tok_other = swap(touch(v.d_tokens, bits, last), "x")
        elif name in (DO_SF, DO_TF):
            if name == DO_SF:
                outs.low = put_rows(v.out_other, bits, last, v.out_low)
            else:
                outs.tok = put_rows(v.tok_other, bits, last, v.out_tok)
        elif name == DO_DU:
            v.d_up_own, v.d_up_oth, v.sums_up = up_back(
                v.d_down,
                (v.b_r, v.o_r),
                (v.slope_own, v.slope_oth),
                bits,
                last,
            )
        elif name == DO_DH1:
            v.d_pre1, v.d_attn, *v.d_mixed, v.sums1 = first_back(
                (v.d_up_own, v.d_up_oth),
                (v.b_e, v.o_e),
                v.d_pre2,
                v.pre_s,
                model_s,
                (v.b[3], v.o[3]),
                bits,
                last,
            )
        elif name == DO_ATT:
            *v.dqk, v.dv_own, v.dv_oth, v.sums_qkv = attend_back(
                (v.qkv_own, v.qkv_oth, v.qk_t), v.d_mixed, seg_row, seg_col, bits, last
            )
        elif name == DO_TOK:
            terms = []
            for d_qk, d_v, weights in (
                (v.dqk[0], v.dv_own, v.b),
                (v.dqk[1], v.dv_oth, v.o),
            ):
                terms += [(d_qk, 0, weights[0]), (d_qk, 1, weights[1]), (d_v, 0, weights[2])]
            v.d_tokens, v.out_tok = token_grad(v.d_pre1, terms, bits, last)
        elif name in OUTERS:
            chunk = OUTERS.index(name)
            part = chunk % 2
            if chunk in (R0, R1):
                acts = (v.act_s_own, v.act_s_oth)
                made = outer([(acts, (v.d_down,) * 2, 0, dim)], bits, last, half * part, half)
            elif chunk in (E0, E1):
                d_ups = (v.d_up_own, v.d_up_oth)
                made = outer([((v.low_s,) * 2, d_ups, part, half)], bits, last)
            elif chunk == QK:
                made = outer([((x, x), v.dqk, 0, 2 * width)], bits, last)
            else:
                mixed = (v.mixed_own[0], v.mixed_oth)
                made = outer(
                    [
                        ((x, x), (v.dv_own, v.dv_oth), 0, width),
                        ((v.d_attn,) * 2, mixed, 0, width),
                    ],
                    bits,
                    last,
                )
            steps[chunk] = reduce_chunk(made, PATHS[chunk])
        elif name >= FETCH_STEP:
            k = name - FETCH_STEP
            if k not in fetching:
                fetching[k] = (
                    fetch_direct(6, lambda: pack_tile(t_r, (), (C,), bits, last))
                    if k == 6
                    else start_fetch(k)
                )
            next(fetching[k])
        else:
            chunk = name - CHUNK_STEP
            if chunk == SUMS and chunk not in steps:
                steps[chunk] = small_sums()
            pieces = next(steps[chunk])
            if pieces is None:
                return
            if chunk == SUMS:
                outs.sums = pieces
                return

            def rows_of(k, b):
                place = b[C] if k == 0 else 1 - b[C]
                return pl.ds(pl.multiple_of(place * tall, 8), tall)

            everything = (0, slice(None), slice(None))
            if chunk in (R0, R1):
                base = (chunk % 2) * dim

                def target(k):
                    def at(b):
                        place = b[C] if k == 0 else 1 - b[C]
                        return (pl.ds(pl.multiple_of(base + place * tall, 8), tall), slice(None))

                    return at

                cuts = [(k, everything, 0, target(k)) for k in range(2)]
                (outs.reduce,) = finish(
                    pieces, cuts, [shape((hidden, dim))], bits, last, outs.reduce
                )
            elif chunk in (E0, E1):
                left = (chunk % 2) * half
                cuts = [
                    (k, everything, 0, lambda b, k=k: (rows_of(k, b), pl.ds(left, half)))
                    for k in range(2)
                ]
                (outs.expand,) = finish(
                    pieces, cuts, [shape((dim, hidden))], bits, last, outs.expand
                )
            else:
                cuts = []
                if chunk == VO:
                    pieces = [*pieces]
                    for k in range(2):
                        pieces.append(flip(pieces[k][:, :, width:], bits, last))
                        cuts.append(
                            (2 + k, (slice(None), slice(None)), 1, lambda b, k=k: (slice(None), rows_of(k, b)))
                        )
                for j in range(1 if chunk == VO else 2):
                    source = (0, slice(None), pl.ds(j * width, width))
                    cuts += [
                        (k, source, j, lambda b, k=k: (rows_of(k, b), slice(None))) for k in range(2)
                    ]
                dims = [(dim, width), (width, dim) if chunk == VO else (dim, width)]
                pair = finish(pieces, cuts, [shape(d) for d in dims], bits, last)
                if chunk == VO:
                    outs.value, outs.output = pair
                else:
                    outs.query, outs.key = pair

    for name in ORDER:
        do(name)
    small = outs.sums
    n_qkv, n_up = 3 * width, hidden
    out_heads = small[0, :n_qkv].reshape(3, width)
    out_hidden = small[0, n_qkv : n_qkv + n_up]
    first, second = (small[:3, n_qkv + n_up + k * dim :][:, :dim] for k in range(2))
    out_model = jnp.stack([first[2], second[2], first[0], first[1], second[0], second[1]])
    return (
        outs.low,
        outs.tok,
        outs.query,
        outs.key,
        outs.value,
        outs.output,
        outs.expand,
        outs.reduce,
        out_heads,
        out_model,
        out_hidden,
    )


def solution(mesh):
    cols = P(None, "narrow")
    rows = P("narrow", None)
    net = (cols, cols, cols, rows, cols, rows, cols, P(), P("narrow"))
    data = P(None, "wide", None)
    return jax.shard_map(
        functools.partial(on_device, mesh.shape["wide"]),
        mesh=mesh,
        in_specs=(data, P(None, "wide")) + net + net,
        out_specs=(data, data) + net,
        check_vma=False,
    )
```

```python
import functools
import types

import jax
import jax.numpy as jnp
from jax import lax
from jax.experimental import pallas as pl
from jax.experimental.pallas import tpu as pltpu
from jax.sharding import PartitionSpec as P

HEAD = 64
REGION = 256

norm_eps = 1e-06
score_weight = 0.05
big_negative = -1e30
f32 = jnp.float32
bf16 = jnp.bfloat16


def dot_nn(left, right):
    return jnp.dot(left, right, preferred_element_type=f32)


def dot_tn(left, right):
    return lax.dot_general(left, right, (((0,), (0,)), ((), ())), preferred_element_type=f32)


def dot_nt(left, right):
    return lax.dot_general(left, right, (((1,), (1,)), ((), ())), preferred_element_type=f32)


MIB = 2**20
STRIP = 384
C, Y, ZL, ZH, SIDE = range(5)


def shape(dims, dtype=f32):
    return jax.ShapeDtypeStruct(dims, dtype)


def vmem(dims, dtype=f32):
    return pltpu.VMEM(dims, dtype)


def hbm(dims, dtype=f32):
    return pltpu.HBM(dims, dtype)


TOKEN = (8, 128)


def invoke(kernel, name, bits, arrays, specs, outs, out_specs, dep, limit, grid, scratch=(), into=None):
    single = not isinstance(outs, (list, tuple))
    outs = [outs] if single else list(outs)
    out_specs = [out_specs] if single else list(out_specs)
    count = len(arrays)
    after = [in_hbm(token) for token in dep] + ([] if into is None else [in_hbm(into)])
    first = count + len(after)
    end = first + len(outs)

    def body(bits_ref, *refs):
        kernel(bits_ref, refs[:count], refs[first:end] + refs[end + 1 :])

    anywhere = pl.BlockSpec(memory_space=pl.ANY)
    in_specs = list(specs) + [anywhere] * len(after)
    form = dict(
        in_specs=in_specs, out_specs=out_specs + [anywhere], scratch_shapes=scratch
    )
    if grid is None:
        form["in_specs"] = [pl.BlockSpec(memory_space=pltpu.SMEM)] + in_specs
    else:
        form = dict(
            grid_spec=pltpu.PrefetchScalarGridSpec(num_scalar_prefetch=1, grid=grid, **form)
        )
    *results, token = pl.pallas_call(
        body,
        out_shape=outs + [pltpu.HBM(TOKEN, f32)],
        input_output_aliases={} if into is None else {first: 0},
        compiler_params=pltpu.CompilerParams(vmem_limit_bytes=limit * MIB),
        cost_estimate=pl.CostEstimate(flops=0, bytes_accessed=0, transcendentals=0),
        name=name,
        **form,
    )(bits, *arrays, *after)
    dep[:] = [token]
    return results[0] if single else results


def call(kernel, name, bits, arrays, specs, outs, out_specs, grid, dep, limit=20, scratch=(), into=None):
    return invoke(
        kernel, name, bits, arrays, specs, outs, out_specs, dep, limit, grid, scratch, into
    )


def whole_call(kernel, name, bits, arrays, outs, dep, limit=16, hold=True):
    if hold:
        arrays = [pin(a) for a in arrays]
    count = len(arrays)
    return invoke(
        kernel, name, bits, arrays, [IN_VMEM] * count, outs, [IN_VMEM] * len(outs), dep, limit, None
    )


def pin(array):
    return pltpu.with_memory_space_constraint(array, pltpu.VMEM)


def in_hbm(array):
    return pltpu.with_memory_space_constraint(array, pltpu.HBM)


IN_VMEM = pl.BlockSpec(memory_space=pltpu.VMEM)


def place_of(bits_ref, names):
    index = 0
    for name in names:
        index = index * 2 + bits_ref[name]
    return index


def fixed(dims):
    return pl.BlockSpec(dims, lambda *a: (0,) * len(dims))


def normalize(values):
    centred = values - jnp.mean(values, axis=-1, keepdims=True)
    spread = jnp.mean(centred * centred, axis=-1, keepdims=True)
    scale = lax.rsqrt(spread + norm_eps)
    return centred * scale, scale


def norm_back(grad, unit, scale, gain):
    inner = grad * (1.0 + gain)
    return scale * (
        inner
        - jnp.mean(inner, axis=-1, keepdims=True)
        - unit * jnp.mean(inner * unit, axis=-1, keepdims=True)
    )


def cdf_of(up):
    return 0.5 + 0.5 * lax.erf(up * 0.5**0.5)


def sign_of(wide, axis):
    alpha = jnp.mean(jnp.abs(wide), axis=axis, keepdims=True)
    return (jnp.where(wide > 0, alpha, jnp.where(wide < 0, -alpha, 0.0))).astype(bf16)


def binarize(weight, axis, bits, dep):
    def kernel(bits_ref, ins, outs):
        outs[0][...] = sign_of(ins[0][...].astype(f32), axis)

    rows, columns = weight.shape
    if axis == 0:
        spec = pl.BlockSpec((rows, STRIP), lambda i, b: (0, i))
        steps = columns // STRIP
    else:
        spec = pl.BlockSpec((STRIP, columns), lambda i, b: (i, 0))
        steps = rows // STRIP
    return call(
        kernel,
        "binarize",
        bits,
        [weight],
        [spec],
        hbm(weight.shape, bf16),
        spec,
        (steps,),
        dep,
    )


def binarize_pack(weights, axes, names, bits, dep):
    parts = 2 ** len(names)

    def kernel(bits_ref, ins, outs):
        part = place_of(bits_ref, names)
        at = 0
        for ref, axis, out in zip(ins, axes, outs):
            result = sign_of(ref[...].astype(f32), axis)
            out[...] = result
            rows, columns = ref.shape[0] // parts, ref.shape[1]
            mine = out[pl.ds(part * rows, rows), :].astype(f32)
            for left in range(0, columns, STRIP):
                outs[-1][at : at + rows, :] = mine[:, left : left + STRIP]
                at += rows

    total = sum(w.size for w in weights) // parts // STRIP
    specs = [fixed(w.shape) for w in weights]
    return call(
        kernel,
        "binarize_pack",
        bits,
        [in_hbm(w) for w in weights],
        specs,
        [hbm(w.shape, bf16) for w in weights] + [vmem((total, STRIP))],
        specs + [IN_VMEM],
        (1,),
        dep,
    )


def pack(weights, names, bits, dep):
    parts = 2 ** len(names)

    def kernel(bits_ref, ins, outs):
        at = 0
        for ref in ins:
            rows, columns = ref.shape
            for left in range(0, columns, STRIP):
                outs[0][at : at + rows, :] = ref[:, left : left + STRIP].astype(f32)
                at += rows

    specs = [
        pl.BlockSpec((w.shape[0] // parts, w.shape[1]), lambda i, b: (place_of(b, names), 0))
        for w in weights
    ]
    total = sum(w.size for w in weights) // parts // STRIP
    return call(
        kernel,
        "pack",
        bits,
        [in_hbm(w) for w in weights],
        specs,
        [vmem((total, STRIP))],
        [IN_VMEM],
        (1,),
        dep,
    )[0]


def pack_tile(weight, row_names, column_names, bits, dep):
    def kernel(bits_ref, ins, outs):
        at = pl.multiple_of(pl.program_id(0) * tall, 8)
        outs[0][pl.ds(at, tall), :] = ins[0][...].astype(f32)

    dims = (weight.shape[0] >> len(row_names), weight.shape[1] >> len(column_names))
    steps = max(1, dims[0] // 384)
    tall = dims[0] // steps
    return call(
        kernel,
        "pack_tile",
        bits,
        [weight],
        [
            pl.BlockSpec(
                (tall, dims[1]),
                lambda i, b: (place_of(b, row_names) * steps + i, place_of(b, column_names)),
            )
        ],
        [vmem(dims)],
        [IN_VMEM],
        (steps,),
        dep,
    )[0]


def touch(array, bits, dep):
    count = len(dep)

    def body(bits_ref, *refs):
        pass

    anywhere = pl.BlockSpec(memory_space=pl.ANY)
    result, token = pl.pallas_call(
        body,
        in_specs=[pl.BlockSpec(memory_space=pltpu.SMEM)] + [anywhere] * (1 + count),
        out_specs=[anywhere] * 2,
        out_shape=[shape(array.shape, array.dtype), pltpu.HBM(TOKEN, f32)],
        input_output_aliases={1: 0},
        compiler_params=pltpu.CompilerParams(vmem_limit_bytes=MIB),
        cost_estimate=pl.CostEstimate(flops=0, bytes_accessed=0, transcendentals=0),
        name="touch",
    )(bits, array, *map(in_hbm, dep))
    dep[:] = [token]
    return result


def join(first, second, bits, dep):
    rows, columns = first.shape

    def kernel(bits_ref, ins, outs):
        for k in range(2):
            outs[0][k * rows : (k + 1) * rows, :] = ins[k][...]

    return whole_call(kernel, "join", bits, [first, second], [vmem((2 * rows, columns))], dep)[0]


def half_masks():
    lane = lax.broadcasted_iota(jnp.int32, (1, 2 * HEAD), 1)
    low = jnp.where(lane < HEAD, 1.0, 0.0).astype(bf16)
    return (low, (1.0 - low.astype(f32)).astype(bf16))


def region_masks(row_ref, col_ref):
    across = row_ref[0]
    down = col_ref[...]
    same = down == across
    live = down >= 0
    size = down.shape[0]
    diagonal = lax.broadcasted_iota(jnp.int32, (size, size), 0) == lax.broadcasted_iota(
        jnp.int32, (size, size), 1
    )
    pairs = same & live
    return pairs, pairs | diagonal


def probabilities(scores, allowed):
    masked = jnp.where(allowed, scores, big_negative)
    top = jnp.max(masked, axis=-1, keepdims=True)
    expo = jnp.exp(masked - top)
    total = jnp.sum(expo, axis=-1, keepdims=True)
    return expo * (1.0 / total)


def attention(parts, allowed, masks, scale, write):
    width = parts[0].shape[1]
    for at in range(0, width, 2 * HEAD):
        query, keys, values = (part[:, at : at + 2 * HEAD] for part in parts)
        probs = [
            probabilities(dot_nt(query * mask, keys) * scale, allowed).astype(bf16) for mask in masks
        ]
        stacked = jnp.concatenate([values * mask for mask in masks], axis=0)
        write(at, dot_nn(jnp.concatenate(probs, axis=1), stacked).astype(bf16))


def attend_own(x, weights, biases, seg_row, seg_col, bits, dep):
    rows, dim = x.shape
    width = weights[0].shape[1]

    def kernel(bits_ref, ins, outs):
        x_ref, bias_ref, row_ref, col_ref = ins[:4]
        tokens = x_ref[...]
        pairs, allowed = region_masks(row_ref, col_ref)
        masks = half_masks()
        for net in range(2):
            parts = []
            for k in range(3):
                row = 3 * net + k
                part = dot_nn(tokens, ins[4 + row][...]) + bias_ref[row : row + 1, :]
                parts.append(part.astype(bf16))
                if row < 5:
                    outs[0][:, row * width : (row + 1) * width] = parts[k]

            def write(at, mixed, net=net):
                outs[1 + net][:, at : at + 2 * HEAD] = mixed

            attention(parts, allowed, masks, HEAD ** (-0.5), write)

    def block(columns):
        return pl.BlockSpec((REGION, columns), lambda i, b: (i, 0))

    return call(
        kernel,
        "attend_own",
        bits,
        [x, biases, seg_row, seg_col, *weights],
        [
            block(dim),
            fixed(biases.shape),
            pl.BlockSpec((1, 1, REGION), lambda i, b: (i, 0, 0)),
            block(1),
        ]
        + [fixed(w.shape) for w in weights],
        [shape((rows, 5 * width), bf16), shape((rows, width), bf16), shape((rows, width), bf16)],
        [block(5 * width), block(width), block(width)],
        (rows // REGION,),
        dep,
    )


def attend_other(
    x, pieces, names, biases, seg_row, seg_col, mixed, output, model, student, bits, dep
):
    rows, dim = x.shape
    width = mixed.shape[1]
    parts = 2 ** len(names)
    half_parts = parts // 2
    tall = dim // parts
    short = width // parts
    per_part = 3 * tall + 2 * short
    first_row = 0 if student else 3
    kept = 3 if student else 2

    def kernel(bits_ref, ins, outs):
        x_ref, bias_ref, row_ref, col_ref, mine_ref, theirs_ref, mixed_ref, out_ref, model_ref = ins
        qkv_ref, low_ref, first_ref = outs[:3]
        weight_refs = outs[5:9] if student else outs[3:7]
        part = place_of(bits_ref, names)

        @pl.when(pl.program_id(0) == 0)
        def _():
            for k in range(parts):
                ref = (mine_ref, theirs_ref)[k // half_parts]
                base = (k % half_parts) * per_part
                where = jnp.bitwise_xor(part, k)
                for m in range(3):
                    weight_refs[m][pl.ds(pl.multiple_of(where * tall, 16), tall), :] = ref[
                        base + m * tall : base + (m + 1) * tall, :
                    ].astype(bf16)
                for m in range(2):
                    at = base + 3 * tall + m * short
                    weight_refs[3][
                        pl.ds(pl.multiple_of(where * short, 16), short), m * STRIP : (m + 1) * STRIP
                    ] = ref[at : at + short, :].astype(bf16)

        tokens = x_ref[...]
        pairs, allowed = region_masks(row_ref, col_ref)
        masks = half_masks()
        parts_qkv = []
        for k in range(3):
            row = first_row + k
            part_k = dot_nn(tokens, weight_refs[k][...]) + bias_ref[row : row + 1, :]
            parts_qkv.append(part_k.astype(bf16))
            if k < kept:
                qkv_ref[:, k * width : (k + 1) * width] = parts_qkv[k]
        tiles = []
        attention(parts_qkv, allowed, masks, HEAD ** (-0.5), lambda at, tile: tiles.append(tile))
        mine = jnp.concatenate(tiles, axis=1)
        pre = (
            tokens.astype(f32)
            + (dot_nn(mixed_ref[...], out_ref[...]) + dot_nn(mine, weight_refs[3][...]))
            + model_ref[0:1, :]
        )
        unit, scale = normalize(pre)
        first = unit * (1.0 + model_ref[2:3, :]) + model_ref[3:4, :]
        low_ref[...] = first.astype(bf16)
        first_ref[...] = first
        if student:
            outs[3][...] = mine
            outs[4][...] = pre

    def block(columns):
        return pl.BlockSpec((REGION, columns), lambda i, b: (i, 0))

    weights = [shape((dim, width), bf16)] * 3 + [shape((width, dim), bf16)]
    outs = [shape((rows, kept * width), bf16), shape((rows, dim), bf16), shape((rows, dim))]
    out_specs = [block(kept * width), block(dim), block(dim)]
    if student:
        outs += [shape((rows, width), bf16), hbm((rows, dim))]
        outs += [hbm(w.shape, bf16) for w in weights]
        out_specs += [block(width), block(dim)] + [fixed(w.shape) for w in weights]
    return call(
        kernel,
        "attend_other",
        bits,
        [x, biases, seg_row, seg_col, *map(pin, pieces), mixed, output, model],
        [
            block(dim),
            fixed(biases.shape),
            pl.BlockSpec((1, 1, REGION), lambda i, b: (i, 0, 0)),
            block(1),
            IN_VMEM,
            IN_VMEM,
            block(width),
            fixed(output.shape),
            fixed(model.shape),
        ],
        outs,
        out_specs,
        (rows // REGION,),
        dep,
        limit=24,
        scratch=[] if student else [pltpu.VMEM(w.shape, bf16) for w in weights],
    )


def activate(up, outs, student):
    cdf = cdf_of(up)
    outs[0][...] = (up * cdf).astype(bf16)
    if student:
        bell = jnp.exp(-0.5 * up * up) * (2.0 * jnp.pi) ** -0.5
        outs[1][...] = (cdf + up * bell).astype(bf16)


def up_own(low, weight, biases, first_row, student, bits, dep):
    tokens, dim = low.shape
    hidden = weight.shape[1]

    def kernel(bits_ref, ins, outs):
        j = pl.program_id(0)
        up = dot_nn(ins[0][...], ins[1][...]) + ins[2][pl.ds(first_row + j, 1), :]
        activate(up, outs, student)

    count = 2 if student else 1
    return call(
        kernel,
        "up_own",
        bits,
        [low, weight, biases],
        [fixed(low.shape), pl.BlockSpec((dim, STRIP), lambda j, b: (0, j)), fixed(biases.shape)],
        [shape((tokens, hidden), bf16), hbm((tokens, hidden), bf16)][:count],
        [pl.BlockSpec((tokens, STRIP), lambda j, b: (0, j))] * count,
        (hidden // STRIP,),
        dep,
    )


def up_other(low, mine, theirs, names, biases, first_row, student, bits, dep):
    tokens, dim = low.shape
    steps = mine.shape[0] // STRIP
    half = dim // 2

    def kernel(bits_ref, ins, outs):
        low_ref, tile_m, tile_o, bias_ref = ins
        j = jnp.bitwise_xor(pl.program_id(0), place_of(bits_ref, names))
        at = pl.ds(pl.multiple_of(pl.program_id(0) * half, 8), half)
        weight_ref = outs[2] if student else outs[1]
        core = bits_ref[C]
        weight_ref[pl.ds(pl.multiple_of(core * half, 16), half), :] = tile_m[at, :].astype(bf16)
        weight_ref[pl.ds(pl.multiple_of((1 - core) * half, 16), half), :] = tile_o[at, :].astype(bf16)
        up = dot_nn(low_ref[...], weight_ref[...]) + bias_ref[pl.ds(first_row + j, 1), :]
        activate(up, outs, student)

    def column(j, b):
        return (0, jnp.bitwise_xor(j, place_of(b, names)))

    outs = [shape((tokens, steps * STRIP), bf16)]
    out_specs = [pl.BlockSpec((tokens, STRIP), column)]
    if student:
        outs += [hbm((tokens, steps * STRIP), bf16), hbm((dim, steps * STRIP), bf16)]
        out_specs += [out_specs[0], pl.BlockSpec((dim, STRIP), column)]
    return call(
        kernel,
        "up_other",
        bits,
        [low, pin(mine), pin(theirs), biases],
        [fixed(low.shape), IN_VMEM, IN_VMEM, fixed(biases.shape)],
        outs,
        out_specs,
        (steps,),
        dep,
        limit=16,
        scratch=[] if student else [pltpu.VMEM((dim, STRIP), bf16)],
    )


def down_own(acts, weights, firsts, models, bits, dep):
    tokens, hidden = acts[0].shape
    dim = weights[0].shape[1]

    def kernel(bits_ref, ins, outs):
        for net in range(2):
            act, weight, first, model = ins[4 * net : 4 * net + 4]
            outs[net][...] = first[...] + model[1:2, :] + dot_nn(act[...], weight[...])

    def block(columns):
        return pl.BlockSpec((REGION, columns), lambda i, b: (i, 0))

    arrays = []
    specs = []
    for net in range(2):
        arrays += [acts[net], weights[net], firsts[net], models[net]]
        specs += [block(hidden), fixed((hidden, dim)), block(dim), fixed(models[net].shape)]
    return call(
        kernel,
        "down_own",
        bits,
        arrays,
        specs,
        [shape((tokens, dim))] * 2,
        [block(dim)] * 2,
        (tokens // REGION,),
        dep,
        limit=24,
    )


def down_other(acts, student_tiles, teacher_tiles, names, partials, models, seg_col, bits, dep):
    tokens, hidden = acts[0].shape
    dim = partials[0].shape[1]
    half = dim // 2
    steps = hidden // STRIP

    def kernel(bits_ref, ins, outs):
        act_s, act_t, s_mine, s_other, t_mine, t_other, part_s, part_t, model_s, model_t, seg = ins
        out_ref, pre_ref, down_ref, sums_ref, weight_ref, low_ref, teacher_ref = outs
        step = pl.program_id(0)
        first_core = bits_ref[C] == 0

        @pl.when(step == 0)
        def _():
            place = place_of(bits_ref, names)
            for k in range(steps):
                rows = slice(k * STRIP, (k + 1) * STRIP)
                where = pl.ds(pl.multiple_of(jnp.bitwise_xor(place, k) * STRIP, 16), STRIP)
                tile, other = s_mine[rows, :].astype(bf16), s_other[rows, :].astype(bf16)
                weight_ref[where, :half] = jnp.where(first_core, tile, other)
                weight_ref[where, half:] = jnp.where(first_core, other, tile)
                tile, other = t_mine[rows, :].astype(bf16), t_other[rows, :].astype(bf16)
                teacher_ref[rows, :half] = jnp.where(first_core, tile, other)
                teacher_ref[rows, half:] = jnp.where(first_core, other, tile)

        unit_s, scale_s = normalize(part_s[...] + dot_nn(act_s[...], weight_ref[...]))
        unit_t, _ = normalize(part_t[...] + dot_nn(act_t[...], teacher_ref[...]))
        gain = model_s[4:5, :]
        out_s = unit_s * (1.0 + gain) + model_s[5:6, :]
        out_t = unit_t * (1.0 + model_t[4:5, :]) + model_t[5:6, :]
        out_ref[...] = out_s
        low_ref[0] = out_s.astype(bf16)
        grad = jnp.where(seg[...] >= 0, out_s - out_t, 0.0)
        d_pre = norm_back(grad, unit_s, scale_s, gain)
        pre_ref[...] = d_pre
        low = d_pre.astype(bf16)
        down_ref[...] = low
        add_sums(sums_ref, (grad * unit_s, grad, low.astype(f32)), step)

    def block(columns):
        return pl.BlockSpec((REGION, columns), lambda i, b: (i, 0))

    return call(
        kernel,
        "down_other",
        bits,
        [*acts, *map(pin, student_tiles), *map(pin, teacher_tiles), *partials, *models, seg_col],
        [block(hidden)] * 2
        + [IN_VMEM] * 4
        + [block(dim)] * 2
        + [fixed(m.shape) for m in models]
        + [block(1)],
        [
            shape((tokens, dim)),
            shape((tokens, dim)),
            shape((tokens, dim), bf16),
            shape((8, dim)),
            hbm((hidden, dim), bf16),
            hbm((2, tokens, dim), bf16),
        ],
        [
            block(dim),
            block(dim),
            block(dim),
            fixed((8, dim)),
            fixed((hidden, dim)),
            pl.BlockSpec((1, REGION, dim), lambda i, b: (b[SIDE], i, 0)),
        ],
        (tokens // REGION,),
        dep,
        limit=28,
        scratch=[pltpu.VMEM((hidden, dim), bf16)],
    )


def up_back(d_down, weights, slopes, bits, dep):
    tokens, dim = d_down.shape
    hidden = weights[0].shape[0]

    def kernel(bits_ref, ins, outs):
        rows = []
        for half in range(2):
            grad = dot_nt(ins[0][...], ins[1 + half][...])
            low = (grad * ins[3 + half][...].astype(f32)).astype(bf16)
            outs[half][...] = low
            rows.append(jnp.sum(low.astype(f32), axis=0, keepdims=True))
        outs[2][...] = jnp.concatenate(rows + [jnp.zeros((6, STRIP), f32)], axis=0)

    block = pl.BlockSpec((tokens, STRIP), lambda j, b: (0, j))
    return call(
        kernel,
        "up_back",
        bits,
        [d_down, *weights, *slopes],
        [fixed(d_down.shape)] + [pl.BlockSpec((STRIP, dim), lambda j, b: (j, 0))] * 2 + [block] * 2,
        [shape((tokens, hidden), bf16)] * 2 + [shape((8, hidden))],
        [block, block, pl.BlockSpec((8, STRIP), lambda j, b: (0, j))],
        (hidden // STRIP,),
        dep,
    )


def add_sums(ref, arrays, step):
    rows = [jnp.sum(v, axis=0, keepdims=True) for v in arrays]
    rows.append(jnp.zeros((8 - len(rows), rows[0].shape[1]), f32))
    new = jnp.concatenate(rows, axis=0)
    ref[...] = jnp.where(step == 0, new, ref[...] + new)


def first_back(d_ups, weights, d_pre2, pre, model, outputs, bits, dep):
    tokens, hidden = d_ups[0].shape
    dim = d_pre2.shape[1]
    width = outputs[0].shape[0]

    def kernel(bits_ref, ins, outs):
        d_own, d_oth, w_own, w_oth, d_pre2_ref, pre_ref, model_ref, o_own, o_oth = ins
        grad = d_pre2_ref[...] + (dot_nt(d_own[...], w_own[...]) + dot_nt(d_oth[...], w_oth[...]))
        unit, scale = normalize(pre_ref[...])
        d_pre = norm_back(grad, unit, scale, model_ref[2:3, :])
        outs[0][...] = d_pre
        low = d_pre.astype(bf16)
        outs[1][...] = low
        outs[2][...] = dot_nt(low, o_own[...]).astype(bf16)
        outs[3][...] = dot_nt(low, o_oth[...]).astype(bf16)
        add_sums(outs[4], (grad * unit, grad, low.astype(f32)), pl.program_id(0))

    def block(columns):
        return pl.BlockSpec((REGION, columns), lambda i, b: (i, 0))

    return call(
        kernel,
        "first_back",
        bits,
        [*d_ups, *weights, d_pre2, pre, model, *outputs],
        [block(hidden)] * 2
        + [fixed(w.shape) for w in weights]
        + [block(dim)] * 2
        + [fixed(model.shape)]
        + [fixed(o.shape) for o in outputs],
        [
            shape((tokens, dim)),
            shape((tokens, dim), bf16),
            shape((tokens, width), bf16),
            shape((tokens, width), bf16),
            shape((8, dim)),
        ],
        [block(dim), block(dim), block(width), block(width), fixed((8, dim))],
        (tokens // REGION,),
        dep,
        limit=28,
    )


def token_grad(d_pre, terms, bits, dep):
    tokens, dim = d_pre.shape

    def kernel(bits_ref, ins, outs):
        total = ins[0][...]
        for k in range(len(terms)):
            total = total + dot_nt(ins[1 + 2 * k][...], ins[2 + 2 * k][...])
        outs[0][...] = total
        outs[1][0] = total

    arrays = [d_pre]
    specs = [pl.BlockSpec((REGION, dim), lambda i, b: (i, 0))]
    for grad, at, weight in terms:
        arrays += [grad, weight]
        specs += [
            pl.BlockSpec((REGION, weight.shape[1]), lambda i, b, at=at: (i, at)),
            fixed(weight.shape),
        ]
    return call(
        kernel,
        "token_grad",
        bits,
        arrays,
        specs,
        [shape((tokens, dim)), pltpu.HBM((2, tokens, dim), f32)],
        [specs[0], pl.BlockSpec((1, REGION, dim), lambda i, b: (b[SIDE], i, 0))],
        (tokens // REGION,),
        dep,
    )


def attend_back(qkv, grads, seg_row, seg_col, bits, dep):
    rows, columns = qkv[0].shape
    width = columns // 5
    step = 2 * HEAD

    def kernel(bits_ref, ins, outs):
        pairs, allowed = region_masks(ins[5], ins[6])
        weight = jnp.where(pairs, score_weight, 0.0)
        masks = half_masks()
        scale = HEAD ** (-0.5)

        @pl.when(pl.program_id(0) == 0)
        def _():
            outs[4][...] = jnp.zeros_like(outs[4])

        for part in range(2):
            for at in range(0, width, step):
                places = [(0, k) for k in range(5)] if part == 0 else [(1, 0), (1, 1), (1, 2), (2, 0), (2, 1)]
                query, keys, values, query_t, keys_t = (
                    ins[r][:, k * width + at : k * width + at + step] for r, k in places
                )
                grad = ins[3 + part][:, at : at + step]
                probs = []
                slopes = []
                for mask in masks:
                    scores = dot_nt(query * mask, keys) * scale
                    prob = probabilities(scores, allowed)
                    gap = scores - dot_nt(query_t * mask, keys_t) * scale
                    d_prob = dot_nt(grad * mask, values)
                    mean = jnp.sum(prob * d_prob, axis=-1, keepdims=True)
                    slope = prob * (d_prob - mean) + weight * gap
                    probs.append(prob.astype(bf16))
                    slopes.append(slope.astype(bf16))

                def both(array):
                    return jnp.concatenate([array * mask for mask in masks], axis=0)

                d_query = dot_nn(jnp.concatenate(slopes, axis=1), both(keys)) * scale
                d_keys = dot_tn(jnp.concatenate(slopes, axis=0), both(query)) * scale
                d_values = dot_tn(jnp.concatenate(probs, axis=0), both(grad))
                for k, result in enumerate((d_query, d_keys, d_values)):
                    low = result.astype(bf16)
                    if k < 2:
                        outs[part][:, k * width + at : k * width + at + step] = low
                    else:
                        outs[2 + part][:, at : at + step] = low
                    outs[4][part : part + 1, k * width + at : k * width + at + step] += jnp.sum(
                        low.astype(f32), axis=0, keepdims=True
                    )

    def block(columns):
        return pl.BlockSpec((REGION, columns), lambda i, b: (i, 0))

    return call(
        kernel,
        "attend_back",
        bits,
        [*qkv, *grads, seg_row, seg_col],
        [
            block(columns),
            block(3 * width),
            block(2 * width),
            block(width),
            block(width),
            pl.BlockSpec((1, 1, REGION), lambda i, b: (i, 0, 0)),
            block(1),
        ],
        [shape((rows, 2 * width), bf16)] * 2
        + [shape((rows, width), bf16)] * 2
        + [shape((8, 3 * width))],
        [block(2 * width)] * 2 + [block(width)] * 2 + [fixed((8, 3 * width))],
        (rows // REGION,),
        dep,
    )


def outer(groups, bits, dep, start=0, size=None, block=384):
    size = size or groups[0][0][0].shape[1]
    tall = size // 2
    steps = tall // block
    tokens = groups[0][0][0].shape[0]
    arrays = []
    specs = []
    for lhs, rhs, at, columns in groups:
        for half in range(2):

            def left(p, h, i, b, half=half, lhs=lhs):
                core = jnp.where(p == 0, 1 - b[C], b[C])
                where = start // block + core * steps + i
                return (0, where if lhs[0] is lhs[1] else jnp.where(h == half, where, start // block))

            arrays += [lhs[half], rhs[half]]
            specs += [
                pl.BlockSpec((tokens, block), left),
                pl.BlockSpec((tokens, columns), lambda p, h, i, b, at=at: (0, at)),
            ]
    wide = sum(g[3] for g in groups)

    def kernel(bits_ref, ins, outs):
        for phase in range(2):
            for half in range(2):

                @pl.when((pl.program_id(0) == phase) & (pl.program_id(1) == half))
                def _(phase=phase, half=half):
                    at = 0
                    row = pl.multiple_of(pl.program_id(2) * block, 8)
                    for k, group in enumerate(groups):
                        lhs, rhs = ins[4 * k + 2 * half], ins[4 * k + 2 * half + 1]
                        outs[phase][half, pl.ds(row, block), at : at + group[3]] = dot_tn(
                            lhs[...], rhs[...]
                        )
                        at += group[3]

    out = vmem((2, tall, wide))
    return call(
        kernel, "outer", bits, arrays, specs, [out, out], [IN_VMEM, IN_VMEM], (2, 2, steps), dep, limit=16
    )


def split(first, second, name, bits, dep, limit=16):
    halves, rows, columns = first.shape
    out = vmem((1, rows, columns)) if name == "x" else vmem((halves, rows // 2, columns))

    def kernel(bits_ref, ins, outs):
        for k in range(2):
            if name == "x":
                where = (pl.ds(1 - k, 1), slice(None))
            else:
                bit = bits_ref[name]
                start = (1 - bit if k == 0 else bit) * (rows // 2)
                where = (slice(None), pl.ds(pl.multiple_of(start, 8), rows // 2))
            outs[k][...] = ins[0][where] + ins[1][where]

    return whole_call(kernel, "split", bits, [first, second], [out, out], dep, limit)


def add(first, second, bits, dep):
    def kernel(bits_ref, ins, outs):
        outs[0][...] = ins[0][...] + ins[1][...]

    return whole_call(kernel, "add", bits, [first, second], [vmem(first.shape)], dep)[0]


def merge(mine, theirs, name, bits, dep):
    one, rows, columns = mine.shape

    def kernel(bits_ref, ins, outs):
        bit = bits_ref[name]
        for k in range(2):
            start = (bit if k == 0 else 1 - bit) * rows
            outs[0][:, pl.ds(pl.multiple_of(start, 8), rows)] = ins[k][...]

    return whole_call(kernel, "merge", bits, [mine, theirs], [vmem((1, 2 * rows, columns))], dep)[0]


def finish(pieces, cuts, outs, bits, dep, into=None):
    def kernel(bits_ref, ins, refs):
        results, sems = refs[:-1], refs[-1]
        copies = []
        for k, (piece, source, out, target) in enumerate(cuts):
            copy = pltpu.make_async_copy(
                ins[piece].at[source], results[out].at[target(bits_ref)], sems.at[k]
            )
            copy.start()
            copies.append(copy)
        for copy in copies:
            copy.wait()

    return invoke(
        kernel,
        "finish",
        bits,
        [*map(pin, pieces)],
        [IN_VMEM] * len(pieces),
        [pltpu.HBM(o.shape, o.dtype) for o in outs],
        [pl.BlockSpec(memory_space=pl.ANY)] * len(outs),
        dep,
        8,
        None,
        [pltpu.SemaphoreType.DMA((len(cuts),))],
        into,
    )


def flip(array, bits, dep):
    def kernel(bits_ref, ins, outs):
        outs[0][...] = ins[0][0].T

    one, rows, columns = array.shape
    return whole_call(kernel, "flip", bits, [array], [vmem((columns, rows))], dep)[0]


def put_rows(array, bits, dep, into):
    two, rows, dim = into.shape
    tall = rows // 4

    def kernel(bits_ref, ins, outs):
        at = pl.ds(pl.multiple_of(pl.program_id(0) * tall, 8), tall)
        outs[-1][0] = ins[0][at, :].astype(into.dtype)

    return call(
        kernel,
        "place",
        bits,
        [pin(array)],
        [IN_VMEM],
        [pltpu.HBM(into.shape, into.dtype)],
        [pl.BlockSpec((1, tall, dim), lambda i, b: (1 - b[SIDE], i, 0))],
        (4,),
        dep,
        into=into,
    )[0]


def collect(sums, other, bits, dep):
    wide = sum(s.shape[1] for s in sums)

    def kernel(bits_ref, ins, outs):
        at = 0
        for k, ref in enumerate(ins):
            columns = ref.shape[1]
            if other and k < 2:
                both = jnp.concatenate([ref[1:2, :], ref[0:1, :], ref[2:, :]], axis=0)
            else:
                both = ref[...]
            outs[0][:, at : at + columns] = both
            at += columns

    return whole_call(kernel, "collect", bits, sums, [vmem((8, wide))], dep)[0]


R0, R1, E0, E1, QK, VO, SUMS = range(7)
(
    DO_B0,
    DO_B1,
    DO_BIN_A,
    DO_BIN_E,
    DO_BIN_R,
    DO_ATT_O,
    DO_KBT,
    DO_KBS,
    DO_UP_OT,
    DO_UP_OS,
    DO_UP_XT,
    DO_UP_XS,
    DO_DN_O,
    DO_KD,
    DO_S,
    DO_TT,
    DO_SF,
    DO_TF,
    DO_DU,
    DO_DH1,
    DO_ATT,
    DO_TOK,
    DO_O_R0,
    DO_O_R1,
    DO_O_E0,
    DO_O_E1,
    DO_O_QK,
    DO_O_VO,
) = range(28)
OUTERS = (DO_O_R0, DO_O_R1, DO_O_E0, DO_O_E1, DO_O_QK, DO_O_VO)
CHUNK_STEP, FETCH_STEP = 50, 60
PATHS = {
    R0: (Y, ZL, "x", ZH),
    R1: (ZL, Y, "x", ZH),
    E0: ("x", ZL, Y, ZH),
    E1: ("x", Y, ZL, ZH),
    QK: ("x", Y, ZL, ZH),
    VO: (Y, "x", ZL, ZH),
}
FETCH = ((ZL,), (ZL, Y), (ZL, Y), (ZL, Y), (Y, ZL))
ORDER = (
    FETCH_STEP + 3, FETCH_STEP + 6, FETCH_STEP + 1, DO_BIN_A, FETCH_STEP + 2, FETCH_STEP + 3,
    DO_ATT_O, FETCH_STEP + 2, DO_B0, FETCH_STEP + 3, DO_BIN_E, FETCH_STEP + 2, FETCH_STEP + 4,
    FETCH_STEP + 1, DO_B1, FETCH_STEP + 3, DO_BIN_R, FETCH_STEP + 5, FETCH_STEP + 1,
    FETCH_STEP + 4, FETCH_STEP + 5, FETCH_STEP + 2, FETCH_STEP + 1, DO_KBT, DO_UP_OT,
    FETCH_STEP + 3, FETCH_STEP + 4, FETCH_STEP + 2, FETCH_STEP + 5, DO_UP_XT, DO_KBS, DO_UP_OS,
    DO_DN_O, FETCH_STEP + 4, FETCH_STEP + 5, FETCH_STEP + 6, FETCH_STEP + 4, DO_UP_XS,
    FETCH_STEP + 5, FETCH_STEP + 6, DO_KD, DO_O_R1, DO_DU, CHUNK_STEP + R1, DO_O_E0,
    CHUNK_STEP + E0, DO_O_R0, DO_O_E1, CHUNK_STEP + E1, CHUNK_STEP + E0, CHUNK_STEP + R0,
    CHUNK_STEP + R1, CHUNK_STEP + R0, DO_DH1, CHUNK_STEP + E1, DO_ATT, CHUNK_STEP + E0,
    CHUNK_STEP + R1, CHUNK_STEP + R0, DO_O_VO, CHUNK_STEP + VO, DO_O_QK, CHUNK_STEP + E0,
    CHUNK_STEP + R1, CHUNK_STEP + E0, CHUNK_STEP + E1, CHUNK_STEP + SUMS, CHUNK_STEP + R0,
    CHUNK_STEP + R1, CHUNK_STEP + QK, DO_TOK, CHUNK_STEP + VO, CHUNK_STEP + R0,
    CHUNK_STEP + SUMS, CHUNK_STEP + E1, CHUNK_STEP + R1, CHUNK_STEP + QK, CHUNK_STEP + SUMS,
    CHUNK_STEP + E1, CHUNK_STEP + R0, DO_S, CHUNK_STEP + VO, CHUNK_STEP + SUMS,
    CHUNK_STEP + QK, CHUNK_STEP + E1, CHUNK_STEP + R0, DO_TT, CHUNK_STEP + SUMS,
    CHUNK_STEP + VO, CHUNK_STEP + R0, CHUNK_STEP + E0, CHUNK_STEP + VO, CHUNK_STEP + E1,
    CHUNK_STEP + QK, CHUNK_STEP + E0, CHUNK_STEP + VO, CHUNK_STEP + QK, CHUNK_STEP + R1,
    CHUNK_STEP + VO, DO_SF, CHUNK_STEP + E1, CHUNK_STEP + QK, CHUNK_STEP + R1, CHUNK_STEP + QK,
    CHUNK_STEP + VO, CHUNK_STEP + E1, CHUNK_STEP + VO, CHUNK_STEP + E0, DO_TF, CHUNK_STEP + QK,
    CHUNK_STEP + R0, CHUNK_STEP + R1, CHUNK_STEP + QK, CHUNK_STEP + E0, CHUNK_STEP + SUMS,
)


def on_device(n_wide, tokens, segments, *params):
    (w_q, w_k, w_v, w_o, w_e, w_r, heads_s, model_s, hidden_s) = params[:9]
    (t_q, t_k, t_v, t_o, t_e, t_r, heads_t, model_t, hidden_t) = params[9:]
    n_bits = n_wide.bit_length() - 1
    side = lax.axis_index("narrow")
    place = lax.axis_index("wide")
    bits = jnp.stack([(place >> b) & 1 for b in range(4)] + [side]).astype(jnp.int32)
    dim, width = w_q.shape
    hidden = w_e.shape[1]

    def swap(array, bit):
        if bit == "x":
            return lax.ppermute(array, "narrow", [(0, 1), (1, 0)])
        return lax.ppermute(array, "wide", [(i, i ^ (1 << bit)) for i in range(n_wide)])

    x = lax.dynamic_index_in_dim(tokens, side, 0, keepdims=False)
    segment = lax.dynamic_index_in_dim(segments, side, 0, keepdims=False)
    rows = x.shape[0]
    seg_row = segment.reshape(rows // REGION, 1, REGION)
    seg_col = segment.reshape(rows, 1)
    biases = jnp.concatenate(
        [heads_s, heads_t, hidden_s.reshape(-1, width), hidden_t.reshape(-1, width)]
    )
    blocks = hidden // width
    models = (model_s, model_t)
    half = hidden // 2

    v = types.SimpleNamespace()
    fetched = {}
    last = []

    def fetch(key, made, path):
        held = swap(made(), "x")
        yield
        held = touch(held, bits, last)
        for name in path:
            got = swap(held, name)
            yield
            held = join(held, got, bits, last)
        got = swap(held, C)
        yield
        fetched[key] = (held, touch(got, bits, last))
        yield

    def fetch_direct(key, made):
        zero = swap(made(), "x")
        yield
        zero = touch(zero, bits, last)
        got = swap(zero, C)
        yield
        fetched[key] = (zero, touch(got, bits, last))
        yield

    def reduce_chunk(made, path):
        send, keep = made
        got = swap(touch(send, bits, last), C)
        yield
        for name in path[:-1]:
            send, keep = split(keep, got, name, bits, last)
            got = swap(send, name)
            yield
        block = add(keep, got, bits, last)
        got = swap(block, path[-1])
        yield
        for extra in range(4, n_bits):
            block = block + got
            got = swap(block, extra)
        block = add(block, got, bits, last)
        back = [name for name in reversed(path[:-1]) if name != "x"] + [C]
        for name in back[:-1]:
            got = swap(block, name)
            yield
            block = merge(block, got, name, bits, last)
        got = swap(block, C)
        yield
        yield (block, got)

    def small_sums():
        sums = [v.sums_qkv, v.sums_up, v.sums1, v.sums2]
        total = collect(sums, False, bits, last)
        got = swap(collect(sums, True, bits, last), "x")
        yield
        for b in range(4):
            total = add(total, got, bits, last)
            got = swap(total, b)
            yield
        total = add(total, got, bits, last)
        for b in range(4, n_bits):
            total = total + swap(total, b)
        yield total

    tall = dim // 2
    steps = {}
    fetching = {}
    outs = types.SimpleNamespace(reduce=None, expand=None)

    def names_of(k):
        return (C, *reversed(FETCH[k - 1]))

    def start_fetch(k):
        names = names_of(k)
        makers = {
            1: lambda: pack([t_q, t_k, t_v, t_o], names, bits, last),
            2: lambda: touch(v.b_pack, bits, last),
            3: lambda: pack_tile(in_hbm(t_e), (C,), names[1:], bits, last),
            4: lambda: pack_tile(v.b_e, (C,), names[1:], bits, last),
            5: lambda: pack_tile(v.b_r, names[1:], (C,), bits, last),
        }
        return fetch(k, makers[k], FETCH[k - 1])

    def do(name):
        if name == DO_B0:
            v.biases_oth = swap(touch(biases, bits, last), "x")
        elif name == DO_B1:
            v.biases_oth = touch(v.biases_oth, bits, last)
        elif name == DO_BIN_A:
            *v.b, v.b_pack = binarize_pack(
                [w_q, w_k, w_v, w_o], (0, 0, 0, 1), names_of(2), bits, last
            )
        elif name == DO_BIN_E:
            v.b_e = binarize(w_e, 0, bits, last)
        elif name == DO_BIN_R:
            v.b_r = binarize(w_r, 1, bits, last)
        elif name == DO_ATT_O:
            b = v.b
            v.qkv_own, *v.mixed_own = attend_own(
                x,
                (b[0], b[1], b[2], in_hbm(t_q), in_hbm(t_k), in_hbm(t_v)),
                biases,
                seg_row,
                seg_col,
                bits,
                last,
            )
        elif name == DO_KBT:
            v.qk_t, v.low_t, v.first_t = attend_other(
                x,
                fetched[1],
                names_of(1),
                v.biases_oth,
                seg_row,
                seg_col,
                v.mixed_own[1],
                t_o,
                model_t,
                False,
                bits,
                last,
            )
        elif name == DO_KBS:
            v.qkv_oth, v.low_s, v.first_s, v.mixed_oth, v.pre_s, *v.o = attend_other(
                x,
                fetched[2],
                names_of(2),
                v.biases_oth,
                seg_row,
                seg_col,
                v.mixed_own[0],
                v.b[3],
                model_s,
                True,
                bits,
                last,
            )
        elif name == DO_UP_OT:
            (v.act_t_own,) = up_own(v.low_t, t_e, biases, 6 + blocks, False, bits, last)
        elif name == DO_UP_OS:
            v.act_s_own, v.slope_own = up_own(
                v.low_s, v.b_e, biases, 6, True, bits, last
            )
        elif name == DO_UP_XT:
            (v.act_t_oth,) = up_other(
                v.low_t, *fetched[3], names_of(3)[1:], v.biases_oth, 6 + blocks, False, bits, last
            )
        elif name == DO_UP_XS:
            v.act_s_oth, v.slope_oth, v.o_e = up_other(
                v.low_s, *fetched[4], names_of(4)[1:], v.biases_oth, 6, True, bits, last
            )
        elif name == DO_DN_O:
            v.partials = down_own(
                (v.act_s_own, v.act_t_own),
                (v.b_r, t_r),
                (v.first_s, v.first_t),
                models,
                bits,
                last,
            )
        elif name == DO_KD:
            v.out_s, v.d_pre2, v.d_down, v.sums2, v.o_r, v.out_low = down_other(
                (v.act_s_oth, v.act_t_oth),
                fetched[5],
                fetched[6],
                names_of(5)[1:],
                v.partials,
                models,
                seg_col,
                bits,
                last,
            )
        elif name == DO_S:
            v.out_other = swap(touch(v.out_s, bits, last), "x")
        elif name == DO_TT:
            v.tok_other = swap(touch(v.d_tokens, bits, last), "x")
        elif name in (DO_SF, DO_TF):
            if name == DO_SF:
                outs.low = put_rows(v.out_other, bits, last, v.out_low)
            else:
                outs.tok = put_rows(v.tok_other, bits, last, v.out_tok)
        elif name == DO_DU:
            v.d_up_own, v.d_up_oth, v.sums_up = up_back(
                v.d_down,
                (v.b_r, v.o_r),
                (v.slope_own, v.slope_oth),
                bits,
                last,
            )
        elif name == DO_DH1:
            v.d_pre1, v.d_attn, *v.d_mixed, v.sums1 = first_back(
                (v.d_up_own, v.d_up_oth),
                (v.b_e, v.o_e),
                v.d_pre2,
                v.pre_s,
                model_s,
                (v.b[3], v.o[3]),
                bits,
                last,
            )
        elif name == DO_ATT:
            *v.dqk, v.dv_own, v.dv_oth, v.sums_qkv = attend_back(
                (v.qkv_own, v.qkv_oth, v.qk_t), v.d_mixed, seg_row, seg_col, bits, last
            )
        elif name == DO_TOK:
            terms = []
            for d_qk, d_v, weights in (
                (v.dqk[0], v.dv_own, v.b),
                (v.dqk[1], v.dv_oth, v.o),
            ):
                terms += [(d_qk, 0, weights[0]), (d_qk, 1, weights[1]), (d_v, 0, weights[2])]
            v.d_tokens, v.out_tok = token_grad(v.d_pre1, terms, bits, last)
        elif name in OUTERS:
            chunk = OUTERS.index(name)
            part = chunk % 2
            if chunk in (R0, R1):
                acts = (v.act_s_own, v.act_s_oth)
                made = outer([(acts, (v.d_down,) * 2, 0, dim)], bits, last, half * part, half)
            elif chunk in (E0, E1):
                d_ups = (v.d_up_own, v.d_up_oth)
                made = outer([((v.low_s,) * 2, d_ups, part, half)], bits, last)
            elif chunk == QK:
                made = outer([((x, x), v.dqk, 0, 2 * width)], bits, last)
            else:
                mixed = (v.mixed_own[0], v.mixed_oth)
                made = outer(
                    [
                        ((x, x), (v.dv_own, v.dv_oth), 0, width),
                        ((v.d_attn,) * 2, mixed, 0, width),
                    ],
                    bits,
                    last,
                )
            steps[chunk] = reduce_chunk(made, PATHS[chunk])
        elif name >= FETCH_STEP:
            k = name - FETCH_STEP
            if k not in fetching:
                fetching[k] = (
                    fetch_direct(6, lambda: pack_tile(t_r, (), (C,), bits, last))
                    if k == 6
                    else start_fetch(k)
                )
            next(fetching[k])
        else:
            chunk = name - CHUNK_STEP
            if chunk == SUMS and chunk not in steps:
                steps[chunk] = small_sums()
            pieces = next(steps[chunk])
            if pieces is None:
                return
            if chunk == SUMS:
                outs.sums = pieces
                return

            def rows_of(k, b):
                place = b[C] if k == 0 else 1 - b[C]
                return pl.ds(pl.multiple_of(place * tall, 8), tall)

            everything = (0, slice(None), slice(None))
            if chunk in (R0, R1):
                base = (chunk % 2) * dim

                def target(k):
                    def at(b):
                        place = b[C] if k == 0 else 1 - b[C]
                        return (pl.ds(pl.multiple_of(base + place * tall, 8), tall), slice(None))

                    return at

                cuts = [(k, everything, 0, target(k)) for k in range(2)]
                (outs.reduce,) = finish(
                    pieces, cuts, [shape((hidden, dim))], bits, last, outs.reduce
                )
            elif chunk in (E0, E1):
                left = (chunk % 2) * half
                cuts = [
                    (k, everything, 0, lambda b, k=k: (rows_of(k, b), pl.ds(left, half)))
                    for k in range(2)
                ]
                (outs.expand,) = finish(
                    pieces, cuts, [shape((dim, hidden))], bits, last, outs.expand
                )
            else:
                cuts = []
                if chunk == VO:
                    pieces = [*pieces]
                    for k in range(2):
                        pieces.append(flip(pieces[k][:, :, width:], bits, last))
                        cuts.append(
                            (2 + k, (slice(None), slice(None)), 1, lambda b, k=k: (slice(None), rows_of(k, b)))
                        )
                for j in range(1 if chunk == VO else 2):
                    source = (0, slice(None), pl.ds(j * width, width))
                    cuts += [
                        (k, source, j, lambda b, k=k: (rows_of(k, b), slice(None))) for k in range(2)
                    ]
                dims = [(dim, width), (width, dim) if chunk == VO else (dim, width)]
                pair = finish(pieces, cuts, [shape(d) for d in dims], bits, last)
                if chunk == VO:
                    outs.value, outs.output = pair
                else:
                    outs.query, outs.key = pair

    for name in ORDER:
        do(name)
    small = outs.sums
    n_qkv, n_up = 3 * width, hidden
    out_heads = small[0, :n_qkv].reshape(3, width)
    out_hidden = small[0, n_qkv : n_qkv + n_up]
    first, second = (small[:3, n_qkv + n_up + k * dim :][:, :dim] for k in range(2))
    out_model = jnp.stack([first[2], second[2], first[0], first[1], second[0], second[1]])
    return (
        outs.low,
        outs.tok,
        outs.query,
        outs.key,
        outs.value,
        outs.output,
        outs.expand,
        outs.reduce,
        out_heads,
        out_model,
        out_hidden,
    )


def solution(mesh):
    cols = P(None, "narrow")
    rows = P("narrow", None)
    net = (cols, cols, cols, rows, cols, rows, cols, P(), P("narrow"))
    data = P(None, "wide", None)
    return jax.shard_map(
        functools.partial(on_device, mesh.shape["wide"]),
        mesh=mesh,
        in_specs=(data, P(None, "wide")) + net + net,
        out_specs=(data, data) + net,
        check_vma=False,
    )
```
